256 devices in a mesh: row: 8 (over z), col: 32 (over y, x, core).
Axes of the slice: x: 4, y: 4, z: 8, core: 2. Of those that a mesh axis runs over, the one named last changes fastest.
Arguments:
- image_embed: bfloat16 [8192, 768], P(('row', 'col')), may hold values from -64 to 64
- text_embed: bfloat16 [8192, 768], P(('col', 'row')), may hold values from -16 to 16
- partner: int32 [8192], P(('row', 'col')), may hold values from 0 to 8191, as said below
Outputs:
- loss: float32 [], replicated
- image_grad: float32 [8192, 768], P(('row', 'col'))
- text_grad: float32 [8192, 768], P(('col', 'row'))
The draws below stay inside these ranges and needn't reach their ends.
Inputs may be any that keep to these rules, and one draw needn't show every extreme that they name: partner is a permutation: every text matches exactly one image.
All inputs are finite; a program needn't handle non-finite values.
Results may differ from the reference program's by a relative error of at most 0.0075.
Values may be sent and summed in bfloat16 or wider, within the bound.
No kernel may reach another device: no remote copies, remote signals or barrier semaphores. Data moves between devices by JAX's collectives and lax.ppermute only.
A program may use at most 64 MiB of HBM per device.

```python
import math
import jax
import jax.numpy as jnp
from jax import lax

FEATURE_DIMENSION = 768
SAMPLE_COUNT = 8192


def paired_embeddings(key):
    splits = jax.random.split(key, 7)
    order = jax.random.permutation(splits[0], SAMPLE_COUNT).astype(jnp.int32)
    cluster_count = max(SAMPLE_COUNT // 32, 2)
    member = jax.random.randint(splits[1], (SAMPLE_COUNT,), 0, cluster_count)
    centers = jax.random.normal(splits[2], (cluster_count, FEATURE_DIMENSION), jnp.float32)
    tightness = jax.random.uniform(splits[3], (SAMPLE_COUNT, 1), jnp.float32, 0.4, 0.7)
    own_part = jax.random.normal(splits[4], (SAMPLE_COUNT, FEATURE_DIMENSION), jnp.float32)
    base = jnp.sqrt(tightness) * centers[member] + jnp.sqrt(1.0 - tightness) * own_part
    mixing = jax.random.uniform(splits[5], (SAMPLE_COUNT, 1), jnp.float32, 0.55, 0.9)
    noise = jax.random.normal(splits[6], (SAMPLE_COUNT, FEATURE_DIMENSION), jnp.float32)
    paired = mixing * base + jnp.sqrt(1.0 - mixing * mixing) * noise
    texts = jnp.zeros((SAMPLE_COUNT, FEATURE_DIMENSION), jnp.float32).at[order].set(paired)
    return (order, base, texts)


def draw_image_embed(key, part):
    spread = 4.0
    order, images, texts = paired_embeddings(key)
    own_key = jax.random.fold_in(key, 11)
    scales = jnp.exp(jax.random.uniform(own_key, (SAMPLE_COUNT, 1), jnp.float32, 0.0, jnp.log(spread)))
    return jnp.clip(images * scales, -64.0, 64.0).astype(jnp.bfloat16)


def draw_text_embed(key, part):
    spread = 2.0
    order, images, texts = paired_embeddings(key)
    own_key = jax.random.fold_in(key, 13)
    scales = jnp.exp(jax.random.uniform(own_key, (SAMPLE_COUNT, 1), jnp.float32, 0.0, jnp.log(spread)))
    return jnp.clip(texts * scales, -16.0, 16.0).astype(jnp.bfloat16)


def draw_partner(key, part):
    order, images, texts = paired_embeddings(key)
    return order


def setup_inputs(seed: int = 0) -> dict:
    arg_keys = jax.random.split(jax.random.key(seed), 4)
    return {
        "image_embed": draw_image_embed(jax.random.fold_in(arg_keys[3], 71), 0),
        "text_embed": draw_text_embed(jax.random.fold_in(arg_keys[3], 71), 0),
        "partner": draw_partner(jax.random.fold_in(arg_keys[3], 71), 0),
    }


sharpness_factor = 1.0 / 0.07

def normalize(embed):
    flat = embed.astype(jnp.float32)
    factor = lax.rsqrt(lax.optimization_barrier(jnp.sum(flat * flat, axis=1, keepdims=True)) + 1e-06)
    return (flat * factor, factor)

def reference(image_embed, text_embed, partner):
    img_unit, img_factor = normalize(image_embed)
    txt_unit, txt_factor = normalize(text_embed)
    img_send = img_unit.astype(jnp.bfloat16)
    caption_departing = txt_unit.astype(jnp.bfloat16)
    block_rows = math.gcd(SAMPLE_COUNT, 512)
    block_count = SAMPLE_COUNT // block_rows
    img_blocks = img_send.reshape(block_count, block_rows, FEATURE_DIMENSION)
    partner_blocks = partner.reshape(block_count, block_rows)
    columns = jnp.arange(SAMPLE_COUNT, dtype=jnp.int32)

    def first_pass(col_sums, inputs):
        normed_derivative_segment, p_block = inputs
        similarity_table = sharpness_factor * jnp.dot(normed_derivative_segment, caption_departing.T, preferred_element_type=jnp.float32)
        expos = jnp.exp(similarity_table)
        match = p_block[:, None] == columns[None, :]
        positive = lax.optimization_barrier(jnp.sum(jnp.where(match, similarity_table, jnp.float32(0.0)), axis=1))
        return (col_sums + lax.optimization_barrier(jnp.sum(expos, axis=0)), (lax.optimization_barrier(jnp.sum(expos, axis=1)), positive))
    col_total, (row_total, positive) = lax.scan(first_pass, jnp.zeros((SAMPLE_COUNT,), jnp.float32), (img_blocks, partner_blocks))
    row_lse = jnp.log(row_total)
    col_lse = jnp.log(col_total)
    loss = (jnp.sum(row_lse) + jnp.sum(col_lse) - 2.0 * jnp.sum(positive)) / (2.0 * SAMPLE_COUNT)

    def second_pass(caption_running_total, inputs):
        normed_derivative_segment, p_block, lse_block = inputs
        similarity_table = sharpness_factor * jnp.dot(normed_derivative_segment, caption_departing.T, preferred_element_type=jnp.float32)
        match = jnp.where(p_block[:, None] == columns[None, :], jnp.float32(2.0), jnp.float32(0.0))
        dscores = (jnp.exp(similarity_table - lse_block[:, None]) + jnp.exp(similarity_table - col_lse[None, :]) - match) / (2.0 * SAMPLE_COUNT)
        grad_block = dscores.astype(jnp.bfloat16)
        img_part = jnp.dot(grad_block, caption_departing, preferred_element_type=jnp.float32)
        caption_running_total = caption_running_total + jnp.dot(grad_block.T, normed_derivative_segment, preferred_element_type=jnp.float32)
        return (caption_running_total, img_part)
    caption_running_total, picture_portions = lax.scan(second_pass, jnp.zeros((SAMPLE_COUNT, FEATURE_DIMENSION), jnp.float32), (img_blocks, partner_blocks, row_lse.reshape(block_count, block_rows)))
    picture_normed_derivative = sharpness_factor * picture_portions.reshape(SAMPLE_COUNT, FEATURE_DIMENSION)
    caption_normed_derivative = sharpness_factor * caption_running_total
    image_grad = img_factor * (picture_normed_derivative - img_unit * lax.optimization_barrier(jnp.sum(img_unit * picture_normed_derivative, axis=1, keepdims=True)))
    text_grad = txt_factor * (caption_normed_derivative - txt_unit * lax.optimization_barrier(jnp.sum(txt_unit * caption_normed_derivative, axis=1, keepdims=True)))
    return (loss, image_grad, text_grad)
```

```python
import functools

import jax
import jax.numpy as jnp
from jax import lax
from jax.experimental import pallas as pl
from jax.experimental.pallas import tpu as pltpu
from jax.sharding import Mesh, PartitionSpec as P

sharpness = 1.0 / 0.07
f32 = jnp.float32
bf16 = jnp.bfloat16
NT = (((1,), (1,)), ((), ()))
TN = (((0,), (0,)), ((), ()))
VMEM = pltpu.CompilerParams(vmem_limit_bytes=48 * 1024 * 1024)


def normalize(embed):
    flat = embed.astype(f32)
    factor = lax.rsqrt(jnp.sum(flat * flat, axis=1, keepdims=True) + 1e-06)
    return flat * factor, factor


def prep_kernel(img_ref, txt_ref, img_out, txt_out):
    for src, dst in ((img_ref, img_out), (txt_ref, txt_out)):
        unit = normalize(src[...])[0].astype(bf16)
        for b in range(dst.shape[0]):
            dst[b] = unit


def scores_kernel(u_ref, own_ref, oth_ref, partner_ref, e_ref, rpay_ref, cpay_ref):
    half = own_ref.shape[0]
    chunks = u_ref.shape[0] // 128
    rows = []
    cols = [None, None]
    for r in range(chunks):
        at = pl.ds(r * 128, 128)
        u = u_ref[at, :]
        lanes = None
        for h, t_ref in enumerate((own_ref, oth_ref)):
            s = lax.dot_general(u, t_ref[...], NT, preferred_element_type=f32)
            e = jnp.exp(s * f32(sharpness))
            e_ref[at, h * half : (h + 1) * half] = e
            c = jnp.sum(e, axis=0, keepdims=True)
            cols[h] = c if cols[h] is None else cols[h] + c
            for k in range(half // 128):
                piece = e[:, k * 128 : (k + 1) * 128]
                lanes = piece if lanes is None else lanes + piece
        rows.append(jnp.sum(lanes.T, axis=0, keepdims=True))
    p = partner_ref[...].astype(f32)
    p = jnp.concatenate([p] * (128 // p.shape[1]), axis=1)
    zero = jnp.zeros((1, 128), f32)
    rpay = jnp.concatenate(rows + [p] + [zero] * (7 - chunks), axis=0)
    cs = [c[:, k * 128 : (k + 1) * 128] for c in cols for k in range(half // 128)]
    cpay = jnp.concatenate(cs + [zero] * (8 - len(cs)), axis=0)
    for b in range(rpay_ref.shape[0]):
        rpay_ref[b] = rpay
    for b in range(cpay_ref.shape[0]):
        cpay_ref[b] = cpay


def sum_kernel(x_ref, o_ref):
    o_ref[...] = jnp.sum(x_ref[...], axis=0)


def split3(v):
    hi = v.astype(bf16).astype(f32)
    mid = (v - hi).astype(bf16).astype(f32)
    return hi, mid, v - hi - mid


def share_tile(v):
    hi, mid, lo = split3(v)
    row = lax.broadcasted_iota(jnp.int32, (16, 128), 0)
    tile = jnp.where(row == 0, hi, jnp.where(row == 1, mid, jnp.where(row == 2, lo, f32(0.0))))
    return tile.astype(bf16)


def grads_kernel(
    base_ref, u_ref, own_ref, oth_ref, e_ref, rx_ref, c_ref, cx_ref, img_out, own_out, oth_out, d_ref
):
    half = own_ref.shape[0]
    hc = half // 128
    chunks = u_ref.shape[0] // 128
    rx = rx_ref[...]
    row_total = jnp.sum(rx, axis=0)[:chunks]
    c, cx = c_ref[...], cx_ref[...]
    col_total = jnp.concatenate([c[:hc] + cx[hc : 2 * hc], c[hc : 2 * hc] + cx[:hc]], axis=0)
    logs = jnp.sum(jnp.log(row_total), axis=0, keepdims=True) / f32(rx.shape[0])
    logs += jnp.sum(jnp.log(col_total), axis=0, keepdims=True) / f32(rx.shape[0])
    logs = jnp.sum(logs, axis=1, keepdims=True)
    row_inv = f32(1.0) / row_total
    col_inv = f32(1.0) / col_total
    lane = lax.broadcasted_iota(jnp.int32, (128, 128), 1)
    lane1 = lane[:1] // 32
    positive = jnp.zeros((1, 1), f32)
    for r in range(chunks):
        at = pl.ds(r * 128, 128)
        p = jnp.zeros((1, 128), f32)
        for q in range(4):
            p = jnp.where(lane1 == q, rx[4 * r + q, chunks : chunks + 1], p)
        p = jnp.broadcast_to(p, (128, 128)).T.astype(jnp.int32)
        ri = jnp.broadcast_to(row_inv[r : r + 1], (128, 128)).T
        found = jnp.zeros((128, 128), f32)
        for k in range(2 * hc):
            e = e_ref[at, k * 128 : (k + 1) * 128]
            first = base_ref[k // hc] + (k % hc) * 128
            match = p - first == lane
            found += jnp.where(match, e, f32(0.0))
            d = e * (ri + col_inv[k : k + 1]) - jnp.where(match, f32(2.0), f32(0.0))
            d_ref[at, k * 128 : (k + 1) * 128] = d.astype(bf16)
        found = jnp.sum(found, axis=1, keepdims=True)
        found = jnp.where(found > 0.0, jnp.log(jnp.where(found > 0.0, found, f32(1.0))), f32(0.0))
        positive += jnp.sum(found, axis=0, keepdims=True)
    share = share_tile(jnp.broadcast_to(logs - 2.0 * positive, (1, 128)))
    blocks = img_out.shape[0]
    rows = u_ref.shape[0] // blocks
    width = u_ref.shape[1] // 128
    for b in range(blocks):
        img_out[b, rows * width :, :] = share
    for r in range(chunks):
        at = pl.ds(r * 128, 128)
        g = jnp.dot(d_ref[at, :half], own_ref[...], preferred_element_type=f32)
        g += jnp.dot(d_ref[at, half:], oth_ref[...], preferred_element_type=f32)
        g = g.astype(bf16)
        for q in range(128 // rows):
            for k in range(width):
                img_out[r * (128 // rows) + q, k * rows : (k + 1) * rows, :] = g[
                    q * rows : (q + 1) * rows, k * 128 : (k + 1) * 128
                ]
    oth_out[...] = lax.dot_general(
        d_ref[:, half:], u_ref[...], TN, preferred_element_type=f32
    ).astype(bf16)
    own_out[...] = lax.dot_general(d_ref[:, :half], u_ref[...], TN, preferred_element_type=f32)


def merge_kernel(own_ref, recv_ref, share_ref, out_ref):
    blocks = out_ref.shape[0]
    rows = own_ref.shape[0] // blocks
    width = own_ref.shape[1] // 128
    share = jnp.sum(jnp.sum(share_ref[...].astype(f32), axis=0), axis=0, keepdims=True)
    tile = share_tile(share)
    for b in range(blocks):
        at = pl.ds(b * rows, rows)
        g = (own_ref[at, :] + recv_ref[at, :].astype(f32)).astype(bf16)
        for k in range(width):
            out_ref[b, k * rows : (k + 1) * rows, :] = g[:, k * 128 : (k + 1) * 128]
        out_ref[b, rows * width :, :] = tile


def finish_kernel(scale, img_ref, txt_ref, imgs_ref, txts_ref, img_out, txt_out, share_out):
    for src, parts, dst in ((img_ref, imgs_ref, img_out), (txt_ref, txts_ref, txt_out)):
        rows, size = src.shape
        width = size // 128
        unit, factor = normalize(src[...])
        total = parts[0, : rows * width, :].astype(f32)
        for b in range(1, parts.shape[0]):
            total += parts[b, : rows * width, :].astype(f32)
        total = total * f32(scale)
        total = jnp.concatenate([total[k * rows : (k + 1) * rows] for k in range(width)], axis=1)
        along = jnp.sum(unit * total, axis=1, keepdims=True)
        dst[...] = factor * (total - unit * along)
        if parts is txts_ref:
            share = parts[:, rows * width :, :].astype(f32)
            share = jnp.sum(jnp.sum(share, axis=0), axis=0, keepdims=True)
            share_out[...] = jnp.broadcast_to(share, share_out.shape)


def call(kernel, outs, **kw):
    return pl.pallas_call(
        kernel,
        out_shape=[jax.ShapeDtypeStruct(s, d) for s, d in outs],
        compiler_params=VMEM,
        **kw,
    )


def exchange(x, axes):
    return lax.all_to_all(x, axes, 0, 0)


def swap(x):
    return lax.ppermute(x, "c", [(0, 1), (1, 0)])


def local(image_embed, text_embed, partner):
    rows, size = image_embed.shape
    plane, line = ("y", "x"), "z"
    n_plane = lax.axis_size("y") * lax.axis_size("x")
    n_line = lax.axis_size("z")
    batch = rows * n_plane * n_line * 2
    chip = lax.axis_index("y") * lax.axis_size("x") + lax.axis_index("x")
    core = lax.axis_index("c")
    tile_rows, half = rows * n_plane, rows * n_line
    packed = rows * (size // 128) + 16
    base = (chip * 2 + jnp.stack([core, 1 - core])) * half

    img_pay, txt_pay = call(
        prep_kernel, [((n_plane, rows, size), bf16), ((n_line, rows, size), bf16)]
    )(image_embed, text_embed)
    own = exchange(txt_pay, line).reshape(half, size)
    oth = swap(own)
    u = exchange(img_pay, plane).reshape(tile_rows, size)
    e, rpay, cpay = call(
        scores_kernel,
        [
            ((tile_rows, 2 * half), f32),
            ((n_plane, 8, 128), f32),
            ((n_line, 8, 128), f32),
        ],
    )(u, own, oth, partner.reshape(1, rows))
    c = call(sum_kernel, [((8, 128), f32)])(exchange(cpay, line))[0]
    cx = swap(c)
    rx = exchange(rpay, plane)
    img_part, own_part, oth_part = call(
        grads_kernel,
        [((n_plane, packed, 128), bf16), ((half, size), f32), ((half, size), bf16)],
        in_specs=[pl.BlockSpec(memory_space=pltpu.SMEM)]
        + [pl.BlockSpec(memory_space=pltpu.VMEM)] * 7,
        scratch_shapes=[pltpu.VMEM((tile_rows, 2 * half), bf16)],
    )(base, u, own, oth, e, rx, c, cx)
    recv = swap(oth_part)
    imgs = exchange(img_part, plane)
    txt_part = call(
        merge_kernel,
        [((n_line, packed, 128), bf16)],
        grid=(1,),
        in_specs=[
            pl.BlockSpec((half, size), lambda i: (0, 0)),
            pl.BlockSpec((half, size), lambda i: (0, 0)),
            pl.BlockSpec((n_plane, 16, 128), lambda i: (0, packed // 16 - 1, 0)),
        ],
        out_specs=[pl.BlockSpec((n_line, packed, 128), lambda i: (0, 0, 0))],
    )(own_part, recv, imgs)[0]
    txts = exchange(txt_part, line)
    image_grad, text_grad, share = call(
        functools.partial(finish_kernel, sharpness / (2.0 * batch)),
        [((rows, size), f32), ((rows, size), f32), ((8, 128), f32)],
    )(image_embed, text_embed, imgs, txts)
    loss = (share[0, 0] + swap(share)[0, 0]) / (2.0 * batch)
    return loss, image_grad, text_grad


def solution(mesh):
    shape = (mesh.shape["row"], 4, mesh.shape["col"] // 8, 2)
    fine = Mesh(mesh.devices.reshape(shape), ("z", "y", "x", "c"))
    by_image, by_text = P(("z", "y", "x", "c")), P(("y", "x", "c", "z"))
    return jax.shard_map(
        local,
        mesh=fine,
        in_specs=(by_image, by_text, by_image),
        out_specs=(P(), by_image, by_text),
        check_vma=False,
    )
```

```python
import functools

import jax
import jax.numpy as jnp
from jax import lax
from jax.experimental import pallas as pl
from jax.experimental.pallas import tpu as pltpu
from jax.sharding import Mesh, PartitionSpec as P

sharpness = 1.0 / 0.07
f32 = jnp.float32
bf16 = jnp.bfloat16
NT = (((1,), (1,)), ((), ()))
TN = (((0,), (0,)), ((), ()))
PLANE, LINE = ("y", "x"), "z"
EXTRA = 16


def normalize(embed):
    flat = embed.astype(f32)
    factor = lax.rsqrt(jnp.sum(flat * flat, axis=1, keepdims=True) + 1e-06)
    return flat * factor, factor


def pack(dst, b, value):
    rows = value.shape[0]
    for k in range(value.shape[1] // 128):
        dst[b, k * rows : (k + 1) * rows, :] = value[:, k * 128 : (k + 1) * 128]


def unpack(ref, first, count, rows, width):
    return jnp.concatenate(
        [
            ref[first : first + count, k * rows : (k + 1) * rows, :].reshape(count * rows, 128)
            for k in range(width // 128)
        ],
        axis=1,
    )


def rows_tile(values):
    row = lax.broadcasted_iota(jnp.int32, (EXTRA, 128), 0)
    tile = jnp.zeros((EXTRA, 128), f32)
    for i, v in enumerate(values):
        tile = jnp.where(row == i, v, tile)
    return tile.astype(bf16)


def prep_kernel(*refs):
    first, second, *partner, out = refs
    unit = jnp.concatenate([normalize(first[...])[0], normalize(second[...])[0]], axis=0)
    unit = unit.astype(bf16)
    size = unit.size // 128
    tile = jnp.zeros((EXTRA, 128), bf16)
    if partner:
        p = jnp.concatenate([partner[0][...], partner[1][...]] * 2, axis=1)
        hi = p // 128
        tile = rows_tile([hi.astype(f32), (p - hi * 128).astype(f32)])
    for b in range(out.shape[0]):
        pack(out, b, unit)
        out[b, size:, :] = tile


def scores_kernel(rows, place_ref, x_ref, y_ref, e_ref, row_ref, col_ref):
    blocks, packed, _ = x_ref.shape
    width = (packed - EXTRA) // rows * 128
    chunks = blocks * rows // 128
    per = 128 // rows
    image_core = place_ref[0] == 0
    lane = lax.broadcasted_iota(jnp.int32, (1, 128), 1)
    tail = jnp.where(
        image_core,
        x_ref[:, packed - EXTRA :, :].astype(f32),
        y_ref[:, packed - EXTRA :, :].astype(f32),
    )
    partner = tail[:, 0, :] * 128.0 + tail[:, 1, :]
    half = rows // 2
    xs, ys = [], []
    for t in range(chunks):
        p = partner[per * t : per * t + 1]
        for q in range(1, per):
            p = jnp.where(lane >= q * rows, partner[per * t + q : per * t + q + 1], p)
        ids = (lane % rows) // half * (blocks * half) + (per * t + lane // rows) * half
        ids = (place_ref[1] * (blocks * rows) + ids + lane % half).astype(f32)
        xs.append(jnp.where(image_core, p, ids))
        ys.append(jnp.where(image_core, ids, p))
    y = unpack(y_ref, 0, blocks, rows, width)
    row_sums, col_sums = [], [None] * chunks
    positive = jnp.zeros((128, 128), f32)
    for r in range(chunks):
        x = unpack(x_ref, r * per, per, rows, width)
        s = lax.dot_general(x, y, NT, preferred_element_type=f32) * f32(sharpness)
        ids = jnp.broadcast_to(xs[r], (128, 128)).T
        lanes = jnp.zeros((128, 128), f32)
        for t in range(chunks):
            piece = s[:, t * 128 : (t + 1) * 128]
            match = ids == ys[t]
            positive += jnp.where(match, piece, f32(0.0))
            e = jnp.exp(piece)
            lanes += e
            c = jnp.sum(e, axis=0, keepdims=True)
            col_sums[t] = c if col_sums[t] is None else col_sums[t] + c
            e_ref[r * 128 : (r + 1) * 128, t * 128 : (t + 1) * 128] = jnp.where(match, -e, e)
        row_sums.append(jnp.sum(lanes.T, axis=0, keepdims=True))
    positive = jnp.sum(jnp.sum(positive, axis=0, keepdims=True), axis=1, keepdims=True)
    rest = [jnp.broadcast_to(positive, (1, 128)), jnp.zeros((7 - chunks, 128), f32)]
    row_ref[...] = jnp.concatenate(row_sums + rest, axis=0)
    col_ref[...] = jnp.concatenate(col_sums + rest, axis=0)


def image_sums_kernel(row_ref, recv_ref, out_ref):
    half = row_ref.shape[0] // 2
    pay = jnp.concatenate([row_ref[:half], recv_ref[:half]], axis=0)
    for b in range(out_ref.shape[0]):
        out_ref[b] = pay


def text_sums_kernel(row_ref, recv_ref, out_ref):
    pay = row_ref[...] + recv_ref[...]
    for b in range(out_ref.shape[0]):
        out_ref[b] = pay


def grads_kernel(rows, place_ref, x_ref, y_ref, e_ref, mine_ref, other_ref, gx_ref, gy_ref, d_ref):
    blocks, packed, _ = x_ref.shape
    width = (packed - EXTRA) // rows * 128
    chunks = blocks * rows // 128
    per = 128 // rows
    image_core = place_ref[0] == 0
    other = other_ref[...]
    row_inv = f32(1.0) / mine_ref[:chunks]
    col_inv = f32(1.0) / jnp.where(image_core, other[:chunks], other[chunks : 2 * chunks])
    line = lax.broadcasted_iota(jnp.int32, other.shape, 0)
    total = line < jnp.where(image_core, chunks, 2 * chunks)
    logs = jnp.sum(jnp.where(total, jnp.log(jnp.where(total, other, f32(1.0))), f32(0.0)))
    share = logs - jnp.where(image_core, 2.0 * other[chunks, 0], f32(0.0))
    hi = share.astype(bf16).astype(f32)
    mid = (share - hi).astype(bf16).astype(f32)
    tile = rows_tile([hi, mid, share - hi - mid])
    x = unpack(x_ref, 0, blocks, rows, width)
    y = unpack(y_ref, 0, blocks, rows, width)
    for r in range(chunks):
        at = slice(r * 128, (r + 1) * 128)
        ri = jnp.broadcast_to(row_inv[r : r + 1], (128, 128)).T
        for t in range(chunks):
            e = e_ref[at, t * 128 : (t + 1) * 128]
            d = jnp.abs(e) * (ri + col_inv[t : t + 1]) - jnp.where(e < 0.0, f32(2.0), f32(0.0))
            d_ref[at, t * 128 : (t + 1) * 128] = d.astype(bf16)
    for r in range(chunks):
        at = slice(r * 128, (r + 1) * 128)
        g = lax.dot_general(d_ref[:, at], x, TN, preferred_element_type=f32).astype(bf16)
        for q in range(per):
            pack(gy_ref, r * per + q, g[q * rows : (q + 1) * rows])
    for r in range(chunks):
        at = slice(r * 128, (r + 1) * 128)
        g = jnp.dot(d_ref[at, :], y, preferred_element_type=f32).astype(bf16)
        for q in range(per):
            pack(gx_ref, r * per + q, g[q * rows : (q + 1) * rows])
            gx_ref[r * per + q, packed - EXTRA :, :] = tile


def image_merge_kernel(gx_ref, recv_ref, out_ref):
    blocks, packed, _ = gx_ref.shape
    out_ref[:blocks] = gx_ref[...]
    out_ref[blocks:, : packed - EXTRA, :] = recv_ref[...]
    out_ref[blocks:, packed - EXTRA :, :] = gx_ref[:, packed - EXTRA :, :]


def text_merge_kernel(gx_ref, recv_ref, out_ref):
    packed = gx_ref.shape[1]
    both = gx_ref[:, : packed - EXTRA, :].astype(f32) + recv_ref[...].astype(f32)
    out_ref[:, : packed - EXTRA, :] = both.astype(bf16)
    out_ref[:, packed - EXTRA :, :] = gx_ref[:, packed - EXTRA :, :]


def finish_kernel(scale, keep_first, first, second, parts, keep_ref, send_ref, share_ref):
    half, size = first.shape
    rows = 2 * half
    body = rows * (size // 128)
    total = parts[0, :body, :].astype(f32)
    for b in range(1, parts.shape[0]):
        total += parts[b, :body, :].astype(f32)
    total = total * f32(scale)
    total = jnp.concatenate(
        [total[k * rows : (k + 1) * rows] for k in range(size // 128)], axis=1
    )
    grads = []
    for i, src in enumerate((first, second)):
        unit, factor = normalize(src[...])
        g = total[i * half : (i + 1) * half]
        grads.append(factor * (g - unit * jnp.sum(unit * g, axis=1, keepdims=True)))
    keep, send = grads if keep_first else grads[::-1]
    keep_ref[...] = keep
    send_ref[:half] = send
    share = parts[:, body:, :].astype(f32)
    share = jnp.sum(jnp.sum(share, axis=0), axis=0, keepdims=True)
    share_ref[...] = jnp.broadcast_to(share, share_ref.shape)
    send_ref[half:] = jnp.broadcast_to(share[:, :1], (send_ref.shape[0] - half, size))


def output_kernel(batch, place_ref, keep_ref, share_ref, recv_ref, img_ref, txt_ref, loss_ref):
    image_core = place_ref[0] == 0
    half = keep_ref.shape[0]
    keep, recv = keep_ref[...], recv_ref[:half]
    img_ref[...] = jnp.where(image_core, keep, recv)
    txt_ref[...] = jnp.where(image_core, recv, keep)
    loss_ref[...] = (share_ref[:1, :1] + recv_ref[half : half + 1, :1]) / (2.0 * batch)


def call(kernel, outs, scalars=False, **kw):
    if scalars:
        kw["in_specs"] = [pl.BlockSpec(memory_space=pltpu.SMEM)]
        kw["in_specs"] += [pl.BlockSpec(memory_space=pltpu.VMEM)] * (scalars - 1)
    return pl.pallas_call(
        kernel,
        out_shape=[jax.ShapeDtypeStruct(s, d) for s, d in outs],
        compiler_params=pltpu.CompilerParams(vmem_limit_bytes=48 * 1024 * 1024),
        **kw,
    )


def exchange(x, axes):
    return lax.all_to_all(x, axes, 0, 0)


def swap(x):
    return lax.ppermute(x, "c", [(0, 1), (1, 0)])


def local(image_embed, text_embed, partner):
    half, size = image_embed.shape
    rows = 2 * half
    n_plane = lax.axis_size("y") * lax.axis_size("x")
    n_line = lax.axis_size("z")
    batch = rows * n_plane * n_line
    chip = lax.axis_index("y") * lax.axis_size("x") + lax.axis_index("x")
    core = lax.axis_index("c")
    image_core = core == 0
    place = jnp.stack([core, chip]).astype(jnp.int32)
    body = rows * (size // 128)
    packed = body + EXTRA
    blocks = n_plane // 2
    tile = blocks * rows
    partner = partner.reshape(1, half)

    img_other = lax.ppermute(image_embed, "c", [(1, 0)])
    txt_other = lax.ppermute(text_embed, "c", [(0, 1)])
    partner_other = lax.ppermute(partner, "c", [(1, 0)])

    def gather_images():
        pay = call(prep_kernel, [((n_plane, packed, 128), bf16)])(
            image_embed, img_other, partner, partner_other
        )[0]
        every = exchange(pay, PLANE)
        return every[:blocks], every[blocks:]

    def gather_texts():
        pay = call(prep_kernel, [((n_line, packed, 128), bf16)])(txt_other, text_embed)[0]
        every = exchange(pay, LINE)
        return every, every

    x, send = lax.cond(image_core, gather_images, gather_texts)
    y = swap(send)
    e, row_sums, col_sums = call(
        functools.partial(scores_kernel, rows),
        [((tile, tile), f32), ((8, 128), f32), ((8, 128), f32)],
        scalars=3,
    )(place, x, y)
    col_sums = swap(col_sums)

    def image_sums():
        pay = call(image_sums_kernel, [((n_plane, 8, 128), f32)])(row_sums, col_sums)[0]
        return jnp.sum(exchange(pay, PLANE), axis=0)

    def text_sums():
        pay = call(text_sums_kernel, [((n_line, 8, 128), f32)])(row_sums, col_sums)[0]
        return jnp.sum(exchange(pay, LINE), axis=0)

    mine = lax.cond(image_core, image_sums, text_sums)
    other = swap(mine)
    gx, gy = call(
        functools.partial(grads_kernel, rows),
        [((blocks, packed, 128), bf16), ((blocks, body, 128), bf16)],
        scalars=6,
        scratch_shapes=[pltpu.VMEM((tile, tile), bf16)],
    )(place, x, y, e, mine, other)
    gy = swap(gy)

    scale = sharpness / (2.0 * batch)
    outs = [((half, size), f32), ((half + 8, size), f32), ((8, 128), f32)]

    def image_grads():
        pay = call(image_merge_kernel, [((n_plane, packed, 128), bf16)])(gx, gy)[0]
        return call(functools.partial(finish_kernel, scale, True), outs)(
            image_embed, img_other, exchange(pay, PLANE)
        )

    def text_grads():
        pay = call(text_merge_kernel, [((n_line, packed, 128), bf16)])(gx, gy)[0]
        return call(functools.partial(finish_kernel, scale, False), outs)(
            txt_other, text_embed, exchange(pay, LINE)
        )

    keep, send, share = lax.cond(image_core, image_grads, text_grads)
    image_grad, text_grad, loss = call(
        functools.partial(output_kernel, batch),
        [((half, size), f32), ((half, size), f32), ((1, 1), f32)],
        scalars=4,
    )(place, keep, share, swap(send))
    return loss.reshape(()), image_grad, text_grad


def solution(mesh):
    shape = (mesh.shape["row"], 4, mesh.shape["col"] // 8, 2)
    fine = Mesh(mesh.devices.reshape(shape), ("z", "y", "x", "c"))
    by_image, by_text = P(("z", "y", "x", "c")), P(("y", "x", "c", "z"))
    return jax.shard_map(
        local,
        mesh=fine,
        in_specs=(by_image, by_text, by_image),
        out_specs=(P(), by_image, by_text),
        check_vma=False,
    )
```

```python
import functools

import jax
import jax.numpy as jnp
from jax import lax
from jax.experimental import pallas as pl
from jax.experimental.pallas import tpu as pltpu
from jax.sharding import Mesh, PartitionSpec as P

sharpness = 1.0 / 0.07
f32 = jnp.float32
bf16 = jnp.bfloat16
NT = (((1,), (1,)), ((), ()))
PLANE, LINE = ("y", "x"), "z"
EXTRA = 16


def normalize(embed):
    flat = embed.astype(f32)
    factor = lax.rsqrt(jnp.sum(flat * flat, axis=1, keepdims=True) + 1e-06)
    return flat * factor, factor


def pack(dst, b, value):
    rows = value.shape[0]
    for k in range(value.shape[1] // 128):
        dst[b, k * rows : (k + 1) * rows, :] = value[:, k * 128 : (k + 1) * 128]


def unpack(ref, first, count, rows, width):
    return jnp.concatenate(
        [
            ref[first : first + count, k * rows : (k + 1) * rows, :].reshape(count * rows, 128)
            for k in range(width // 128)
        ],
        axis=1,
    )


def rows_tile(values):
    row = lax.broadcasted_iota(jnp.int32, (EXTRA, 128), 0)
    tile = jnp.zeros((EXTRA, 128), f32)
    for i, v in enumerate(values):
        tile = jnp.where(row == i, v, tile)
    return tile.astype(bf16)


def start_kernel(place_ref, img_hbm, txt_hbm, partner_hbm, keep_ref, send_ref, img, txt, partner, sems):
    copies = [
        pltpu.make_async_copy(src, dst, sems.at[i])
        for i, (src, dst) in enumerate(((img_hbm, img), (txt_hbm, txt), (partner_hbm, partner)))
    ]
    for c in copies:
        c.start()
    for c in copies:
        c.wait()
    image_core = place_ref[0] == 0
    half, size = img.shape
    a, b = img[...].astype(f32), txt[...].astype(f32)
    keep_ref[:half] = jnp.where(image_core, a, b).astype(bf16)
    send_ref[:half] = jnp.where(image_core, b, a).astype(bf16)
    p = jnp.concatenate([partner[...]] * (size // half), axis=1)
    hi = p // 128
    row = lax.broadcasted_iota(jnp.int32, (EXTRA, size), 0)
    tile = jnp.where(row == 0, hi, jnp.where(row == 1, p - hi * 128, 0)).astype(f32).astype(bf16)
    keep_ref[half:] = tile
    send_ref[half:] = tile


def prep_kernel(images, first, second, out):
    half = first.shape[0] - EXTRA
    unit = [normalize(src[:half, :])[0] for src in (first, second)]
    unit = jnp.concatenate(unit, axis=0).astype(bf16)
    size = unit.size // 128
    tile = jnp.zeros((EXTRA, 128), bf16)
    if images:
        lane = lax.broadcasted_iota(jnp.int32, (EXTRA, 128), 1)
        a, b = (src[half:, :128].astype(f32) for src in (first, second))
        tile = jnp.where(lane // half % 2 == 0, a, b).astype(bf16)
    for b in range(out.shape[0]):
        pack(out, b, unit)
        out[b, size:, :] = tile


def scores_kernel(images, rows, place_ref, x_ref, y_ref, e_ref, pay_ref):
    packed = x_ref.shape[1]
    width = (packed - EXTRA) // rows * 128
    per, half = 128 // rows, rows // 2
    texts = x_ref.shape[0] // 2
    nx, ny = x_ref.shape[0] // per, y_ref.shape[0] // per
    if images:
        ny = texts // per
    else:
        nx = texts // per
    lane = lax.broadcasted_iota(jnp.int32, (1, 128), 1)
    tail = (x_ref if images else y_ref)[:, packed - EXTRA :, :].astype(f32)
    partner = tail[:, 0, :] * 128.0 + tail[:, 1, :]

    def partners(t):
        p = partner[per * t : per * t + 1]
        for q in range(1, per):
            p = jnp.where(lane >= q * rows, partner[per * t + q : per * t + q + 1], p)
        return p

    def ids(t):
        i = (lane % rows) // half * (texts * half) + (per * t + lane // rows) * half
        return (place_ref[1] * (texts * rows) + i + lane % half).astype(f32)

    xs, ys = (partners, ids) if images else (ids, partners)
    y = unpack(y_ref, 0, ny * per, rows, width)
    targets = [ys(t) for t in range(ny)]
    sums = []
    positive = jnp.zeros((128, 128), f32)
    for r in range(nx):
        x = unpack(x_ref, r * per, per, rows, width)
        s = lax.dot_general(x, y, NT, preferred_element_type=f32) * f32(sharpness)
        own = jnp.broadcast_to(xs(r), (128, 128)).T
        lanes = jnp.zeros((128, 128), f32)
        for t in range(ny):
            piece = s[:, t * 128 : (t + 1) * 128]
            match = own == targets[t]
            if not images:
                positive += jnp.where(match, piece, f32(0.0))
            e = jnp.exp(piece)
            lanes += e
            e_ref[r * ny + t] = jnp.where(match, -e, e)
        sums.append(jnp.sum(lanes.T, axis=0, keepdims=True))
    if not images:
        positive = jnp.sum(jnp.sum(positive, axis=0, keepdims=True), axis=1, keepdims=True)
        sums += [jnp.broadcast_to(positive, (1, 128)), jnp.zeros((7 - nx, 128), f32)]
    pay = jnp.concatenate(sums, axis=0)
    for b in range(pay_ref.shape[0]):
        pay_ref[b] = pay


def grads_kernel(images, rows, y_ref, e_ref, mine_ref, other_ref, out_ref):
    blocks, packed, _ = out_ref.shape
    width = (packed - EXTRA) // rows * 128
    per = 128 // rows
    nx = blocks // per
    ny = e_ref.shape[0] // nx
    row_inv = f32(1.0) / mine_ref[:nx]
    col_total = other_ref[:ny]
    col_inv = f32(1.0) / col_total
    share = jnp.sum(jnp.log(col_total), axis=0, keepdims=True)
    share = jnp.broadcast_to(jnp.sum(share, axis=1, keepdims=True), (1, 128))
    if images:
        share -= 2.0 * other_ref[ny : ny + 1]
    hi = share.astype(bf16).astype(f32)
    mid = (share - hi).astype(bf16).astype(f32)
    tile = rows_tile([hi, mid, share - hi - mid])
    y = unpack(y_ref, 0, ny * per, rows, width)
    for r in range(nx):
        ri = jnp.broadcast_to(row_inv[r : r + 1], (128, 128)).T
        d = []
        for t in range(ny):
            e = e_ref[r * ny + t]
            v = jnp.abs(e) * (ri + col_inv[t : t + 1]) - jnp.where(e < 0.0, f32(2.0), f32(0.0))
            d.append(v.astype(bf16))
        g = jnp.dot(jnp.concatenate(d, axis=1), y, preferred_element_type=f32).astype(bf16)
        for q in range(per):
            pack(out_ref, r * per + q, g[q * rows : (q + 1) * rows])
            out_ref[r * per + q, packed - EXTRA :, :] = tile


def finish_kernel(scale, keep_first, first, second, parts, keep_ref, send_ref, share_ref):
    half, size = keep_ref.shape
    rows = 2 * half
    body = rows * (size // 128)
    total = parts[0, :body, :].astype(f32)
    for b in range(1, parts.shape[0]):
        total += parts[b, :body, :].astype(f32)
    total = total * f32(scale)
    total = jnp.concatenate(
        [total[k * rows : (k + 1) * rows] for k in range(size // 128)], axis=1
    )
    grads = []
    for i, src in enumerate((first, second)):
        unit, factor = normalize(src[:half, :])
        g = total[i * half : (i + 1) * half]
        grads.append(factor * (g - unit * jnp.sum(unit * g, axis=1, keepdims=True)))
    keep, send = grads if keep_first else grads[::-1]
    keep_ref[...] = keep
    send_ref[:half] = send
    share = parts[:, body:, :].astype(f32)
    share = jnp.sum(jnp.sum(share, axis=0), axis=0, keepdims=True)
    share_ref[...] = jnp.broadcast_to(share, share_ref.shape)
    send_ref[half:] = jnp.broadcast_to(share[:, :1], (send_ref.shape[0] - half, size))


def output_kernel(batch, place_ref, keep_ref, share_ref, recv_ref, img_ref, txt_ref, loss_ref):
    image_core = place_ref[0] == 0
    half = keep_ref.shape[0]
    keep, recv = keep_ref[...], recv_ref[:half]
    img_ref[...] = jnp.where(image_core, keep, recv)
    txt_ref[...] = jnp.where(image_core, recv, keep)
    loss_ref[...] = (share_ref[:1, :1] + recv_ref[half : half + 1, :1]) / (2.0 * batch)


def call(kernel, outs, scalars=False, **kw):
    if scalars:
        kw["in_specs"] = [pl.BlockSpec(memory_space=pltpu.SMEM)]
        kw["in_specs"] += [pl.BlockSpec(memory_space=pltpu.VMEM)] * (scalars - 1)
    return pl.pallas_call(
        kernel,
        out_shape=[jax.ShapeDtypeStruct(s, d) for s, d in outs],
        compiler_params=pltpu.CompilerParams(vmem_limit_bytes=48 * 1024 * 1024),
        **kw,
    )


def exchange(x, axes):
    return lax.all_to_all(x, axes, 0, 0)


def swap(x):
    return lax.ppermute(x, "c", [(0, 1), (1, 0)])


def local(image_embed, text_embed, partner):
    half, size = image_embed.shape
    rows = 2 * half
    n_plane = lax.axis_size("y") * lax.axis_size("x")
    n_line = lax.axis_size("z")
    batch = rows * n_plane * n_line
    chip = lax.axis_index("y") * lax.axis_size("x") + lax.axis_index("x")
    core = lax.axis_index("c")
    image_core = core == 0
    place = jnp.stack([core, chip]).astype(jnp.int32)
    packed = rows * (size // 128) + EXTRA
    tiles = n_plane * n_line * rows * rows // (128 * 128)

    own, send = call(
        start_kernel,
        [((half + EXTRA, size), bf16)] * 2,
        in_specs=[pl.BlockSpec(memory_space=pltpu.SMEM)] + [pl.BlockSpec(memory_space=pl.ANY)] * 3,
        scratch_shapes=[
            pltpu.VMEM((half, size), bf16),
            pltpu.VMEM((half, size), bf16),
            pltpu.VMEM((1, half), jnp.int32),
            pltpu.SemaphoreType.DMA((3,)),
        ],
    )(place, image_embed, text_embed, partner.reshape(1, half))
    off = swap(send)

    def gather_images():
        kernel = functools.partial(prep_kernel, True)
        return exchange(call(kernel, [((n_plane, packed, 128), bf16)])(own, off)[0], PLANE)

    def gather_texts():
        kernel = functools.partial(prep_kernel, False)
        every = exchange(call(kernel, [((n_line, packed, 128), bf16)])(off, own)[0], LINE)
        return jnp.pad(every, ((0, n_plane - n_line), (0, 0), (0, 0)))

    x = lax.cond(image_core, gather_images, gather_texts)
    y = swap(x)

    def sums(images, count, axes):
        e, pay = call(
            functools.partial(scores_kernel, images, rows),
            [((tiles, 128, 128), f32), ((count, 8, 128), f32)],
            scalars=3,
        )(place, x, y)
        return e, jnp.sum(exchange(pay, axes), axis=0)

    e, mine = lax.cond(
        image_core,
        functools.partial(sums, True, n_plane, PLANE),
        functools.partial(sums, False, n_line, LINE),
    )
    other = swap(mine)

    def grads(images, count, axes):
        pay = call(
            functools.partial(grads_kernel, images, rows), [((count, packed, 128), bf16)]
        )(y, e, mine, other)[0]
        return call(
            functools.partial(finish_kernel, sharpness / (2.0 * batch), images),
            [((half, size), f32), ((half + 8, size), f32), ((8, 128), f32)],
        )(*((own, off) if images else (off, own)), exchange(pay, axes))

    keep, send, share = lax.cond(
        image_core,
        functools.partial(grads, True, n_plane, PLANE),
        functools.partial(grads, False, n_line, LINE),
    )
    image_grad, text_grad, loss = call(
        functools.partial(output_kernel, batch),
        [((half, size), f32), ((half, size), f32), ((1, 1), f32)],
        scalars=4,
    )(place, keep, share, swap(send))
    return loss.reshape(()), image_grad, text_grad


def solution(mesh):
    shape = (mesh.shape["row"], 4, mesh.shape["col"] // 8, 2)
    fine = Mesh(mesh.devices.reshape(shape), ("z", "y", "x", "c"))
    by_image, by_text = P(("z", "y", "x", "c")), P(("y", "x", "c", "z"))
    return jax.shard_map(
        local,
        mesh=fine,
        in_specs=(by_image, by_text, by_image),
        out_specs=(P(), by_image, by_text),
        check_vma=False,
    )
```

```python
import functools
import math

import jax
import jax.numpy as jnp
from jax import lax
from jax.experimental import pallas as pl
from jax.experimental.pallas import tpu as pltpu
from jax.sharding import Mesh, PartitionSpec as P

sharpness = 1.0 / 0.07
f32 = jnp.float32
bf16 = jnp.bfloat16
NT = (((1,), (1,)), ((), ()))
PLANE, LINE = ("y", "x"), "z"
EXTRA = 16


def normalize(embed):
    flat = embed.astype(f32)
    factor = lax.rsqrt(jnp.sum(flat * flat, axis=1, keepdims=True) + 1e-06)
    return flat * factor, factor


def pack(dst, b, value):
    rows = value.shape[0]
    for k in range(value.shape[1] // 128):
        dst[b, k * rows : (k + 1) * rows, :] = value[:, k * 128 : (k + 1) * 128]


def unpack(ref, first, count, rows, width):
    return jnp.concatenate(
        [
            ref[first : first + count, k * rows : (k + 1) * rows, :].reshape(count * rows, 128)
            for k in range(width // 128)
        ],
        axis=1,
    )


def rows_tile(values):
    row = lax.broadcasted_iota(jnp.int32, (EXTRA, 128), 0)
    tile = jnp.zeros((EXTRA, 128), f32)
    for i, v in enumerate(values):
        tile = jnp.where(row == i, v, tile)
    return tile.astype(bf16)


def start_kernel(img_hbm, txt_hbm, partner_hbm, keep_ref, send_ref, img, txt, partner, sems):
    copies = [
        pltpu.make_async_copy(src, dst, sems.at[i])
        for i, (src, dst) in enumerate(((img_hbm, img), (txt_hbm, txt), (partner_hbm, partner)))
    ]
    for c in copies:
        c.start()
    for c in copies:
        c.wait()
    image_core = lax.axis_index("c") == 0
    half, size = img.shape
    a, b = img[...].astype(f32), txt[...].astype(f32)
    keep_ref[:half] = jnp.where(image_core, a, b).astype(bf16)
    send_ref[:half] = jnp.where(image_core, b, a).astype(bf16)
    p = jnp.concatenate([partner[...]] * (128 // half), axis=1)
    hi = p // 128
    tile = rows_tile([hi.astype(f32), (p - hi * 128).astype(f32)])
    for dst in (keep_ref, send_ref):
        dst[half:] = jnp.zeros((EXTRA, size), bf16)
        dst[half:, :128] = tile


def prep_kernel(images, first, second, out):
    half = first.shape[0] - EXTRA
    unit = [normalize(src[:half, :])[0] for src in (first, second)]
    unit = jnp.concatenate(unit, axis=0).astype(bf16)
    size = unit.size // 128
    tile = jnp.zeros((EXTRA, 128), bf16)
    if images:
        lane = lax.broadcasted_iota(jnp.int32, (EXTRA, 128), 1)
        a, b = (src[half:, :128].astype(f32) for src in (first, second))
        tile = jnp.where(lane // half % 2 == 0, a, b).astype(bf16)
    for b in range(out.shape[0]):
        pack(out, b, unit)
        out[b, size:, :] = tile


def scores_kernel(images, rows, x_ref, y_ref, e_ref, pay_ref, s_ref, xs_ref, ys_ref):
    packed = x_ref.shape[1]
    width = (packed - EXTRA) // rows * 128
    per, half = 128 // rows, rows // 2
    texts = x_ref.shape[0] // 2
    nx, ny = x_ref.shape[0] // per, y_ref.shape[0] // per
    if images:
        ny = texts // per
    else:
        nx = texts // per
    lane = lax.broadcasted_iota(jnp.int32, (1, 128), 1)
    chip = lax.axis_index("y") * lax.axis_size("x") + lax.axis_index("x")
    tail = (x_ref if images else y_ref)[:, packed - EXTRA :, :].astype(f32)
    partner = tail[:, 0, :] * 128.0 + tail[:, 1, :]

    def partners(t):
        p = partner[per * t : per * t + 1]
        for q in range(1, per):
            p = jnp.where(lane >= q * rows, partner[per * t + q : per * t + q + 1], p)
        return p

    def ids(t):
        i = (lane % rows) // half * (texts * half) + (per * t + lane // rows) * half
        return (chip * (texts * rows) + i + lane % half).astype(f32)

    xs, ys = (partners, ids) if images else (ids, partners)
    for r in range(nx):
        xs_ref[r : r + 1] = xs(r)
    for t in range(ny):
        ys_ref[t : t + 1] = ys(t)
    x = unpack(x_ref, 0, nx * per, rows, width)
    y = unpack(y_ref, 0, ny * per, rows, width)
    scores = lax.dot_general(x, y, NT, preferred_element_type=f32)
    for r in range(nx):
        for t in range(ny):
            s_ref[r * ny + t] = scores[r * 128 : (r + 1) * 128, t * 128 : (t + 1) * 128]
    group = nx // 2

    def part(i, positive):
        for q in range(group):
            r = i * group + q
            own = jnp.broadcast_to(xs_ref[pl.ds(r, 1)], (128, 128)).T
            lanes = jnp.zeros((128, 128), f32)
            for t in range(ny):
                piece = s_ref[r * ny + t]
                match = own == ys_ref[t : t + 1]
                if not images:
                    positive += jnp.where(match, piece, f32(0.0))
                e = jnp.exp2(piece * f32(sharpness * math.log2(math.e)))
                lanes += e
                tile = q * ny + t
                at = pl.ds(tile % 2 * 128, 128)
                e_ref[i * (group * ny // 2) + tile // 2, at] = jnp.where(match, -e, e).astype(bf16)
            pay_ref[0, pl.ds(r, 1)] = jnp.sum(lanes.T, axis=0, keepdims=True)
        return positive

    positive = lax.fori_loop(0, 2, part, jnp.zeros((128, 128), f32)) * f32(sharpness)
    if not images:
        positive = jnp.sum(jnp.sum(positive, axis=0, keepdims=True), axis=1, keepdims=True)
        pay_ref[0, nx:] = jnp.broadcast_to(positive, (8 - nx, 128))
    for b in range(1, pay_ref.shape[0]):
        pay_ref[b] = pay_ref[0]


def grads_kernel(images, rows, y_ref, e_ref, mine_ref, other_ref, out_ref):
    blocks, packed, _ = out_ref.shape
    width = (packed - EXTRA) // rows * 128
    per = 128 // rows
    nx = blocks // per
    ny = e_ref.shape[0] * 2 // nx
    col_total = other_ref[:ny]
    col_inv = f32(1.0) / col_total
    share = jnp.sum(jnp.log(col_total), axis=0, keepdims=True)
    share = jnp.broadcast_to(jnp.sum(share, axis=1, keepdims=True), (1, 128))
    if images:
        share -= 2.0 * other_ref[ny : ny + 1]
    hi = share.astype(bf16).astype(f32)
    mid = (share - hi).astype(bf16).astype(f32)
    share = rows_tile([hi, mid, share - hi - mid])
    row_inv = f32(1.0) / mine_ref[:nx]
    y = unpack(y_ref, 0, ny * per, rows, width)
    ds = []
    for r in range(nx):
        ri = jnp.broadcast_to(row_inv[r : r + 1], (128, 128)).T
        d = []
        for t in range(ny):
            tile = r * ny + t
            e = e_ref[tile // 2, tile % 2 * 128 : tile % 2 * 128 + 128].astype(f32)
            v = jnp.abs(e) * (ri + col_inv[t : t + 1]) - jnp.where(e < 0.0, f32(2.0), f32(0.0))
            d.append(v.astype(bf16))
        ds.append(jnp.concatenate(d, axis=1))
    g = jnp.dot(jnp.concatenate(ds, axis=0), y, preferred_element_type=f32).astype(bf16)
    for b in range(blocks):
        pack(out_ref, b, g[b * rows : (b + 1) * rows])
        out_ref[b, packed - EXTRA :, :] = share


def finish_kernel(scale, keep_first, first, second, parts, keep_ref, send_ref, share_ref):
    half, size = keep_ref.shape
    rows = 2 * half
    body = rows * (size // 128)
    total = parts[0, :body, :].astype(f32)
    for b in range(1, parts.shape[0]):
        total += parts[b, :body, :].astype(f32)
    total = total * f32(scale)
    total = jnp.concatenate(
        [total[k * rows : (k + 1) * rows] for k in range(size // 128)], axis=1
    )
    grads = []
    for i, src in enumerate((first, second)):
        unit, factor = normalize(src[:half, :])
        g = total[i * half : (i + 1) * half]
        grads.append(factor * (g - unit * jnp.sum(unit * g, axis=1, keepdims=True)))
    keep, send = grads if keep_first else grads[::-1]
    keep_ref[...] = keep
    send_ref[:half] = send
    share = parts[:, body:, :].astype(f32)
    share = jnp.sum(jnp.sum(share, axis=0), axis=0, keepdims=True)
    share_ref[...] = jnp.broadcast_to(share, share_ref.shape)
    send_ref[half:] = jnp.broadcast_to(share[:, :1], (send_ref.shape[0] - half, size))


def output_kernel(batch, keep_ref, share_ref, recv_ref, img_ref, txt_ref, loss_ref):
    image_core = lax.axis_index("c") == 0
    half = keep_ref.shape[0]
    keep, recv = keep_ref[...], recv_ref[:half]
    img_ref[...] = jnp.where(image_core, keep, recv)
    txt_ref[...] = jnp.where(image_core, recv, keep)
    loss_ref[...] = (share_ref[:1, :1] + recv_ref[half : half + 1, :1]) / (2.0 * batch)


def call(kernel, outs, **kw):
    return pl.pallas_call(
        kernel,
        out_shape=[jax.ShapeDtypeStruct(*o) for o in outs],
        compiler_params=pltpu.CompilerParams(vmem_limit_bytes=48 * 1024 * 1024),
        **kw,
    )


def exchange(x, axes):
    return lax.all_to_all(x, axes, 0, 0)


def swap(x):
    return lax.ppermute(x, "c", [(0, 1), (1, 0)])


def local(image_embed, text_embed, partner):
    half, size = image_embed.shape
    rows = 2 * half
    n_plane = lax.axis_size("y") * lax.axis_size("x")
    n_line = lax.axis_size("z")
    batch = rows * n_plane * n_line
    image_core = lax.axis_index("c") == 0
    packed = rows * (size // 128) + EXTRA
    tiles = n_plane * n_line * rows * rows // (128 * 128)

    args = [
        pltpu.with_memory_space_constraint(a, pltpu.HBM)
        for a in (image_embed, text_embed, partner.reshape(1, half))
    ]
    own, send = call(
        start_kernel,
        [((half + EXTRA, size), bf16)] * 2,
        in_specs=[pl.BlockSpec(memory_space=pl.ANY)] * 3,
        scratch_shapes=[
            pltpu.VMEM((half, size), bf16),
            pltpu.VMEM((half, size), bf16),
            pltpu.VMEM((1, half), jnp.int32),
            pltpu.SemaphoreType.DMA((3,)),
        ],
    )(*args)
    off = swap(send)

    def gather_images():
        kernel = functools.partial(prep_kernel, True)
        return exchange(call(kernel, [((n_plane, packed, 128), bf16)])(own, off)[0], PLANE)

    def gather_texts():
        kernel = functools.partial(prep_kernel, False)
        every = exchange(call(kernel, [((n_line, packed, 128), bf16)])(off, own)[0], LINE)
        return jnp.pad(every, ((0, n_plane - n_line), (0, 0), (0, 0)))

    x = lax.cond(image_core, gather_images, gather_texts)
    y = swap(x)

    def sums(images, count, axes):
        e, pay = call(
            functools.partial(scores_kernel, images, rows),
            [((n_plane, packed, 128), bf16), ((count, 8, 128), f32)],
            input_output_aliases={0: 0},
            scratch_shapes=[pltpu.VMEM((tiles, 128, 128), f32)] + [pltpu.VMEM((8, 128), f32)] * 2,
        )(x, y)
        return e, jnp.sum(exchange(pay, axes), axis=0)

    e, mine = lax.cond(
        image_core,
        functools.partial(sums, True, n_plane, PLANE),
        functools.partial(sums, False, n_line, LINE),
    )
    other = swap(mine)

    def grads(images, count, axes):
        pay = call(
            functools.partial(grads_kernel, images, rows),
            [((count, packed, 128), bf16)],
        )(y, e, mine, other)[0]
        return call(
            functools.partial(finish_kernel, sharpness / (2.0 * batch), images),
            [((half, size), f32), ((half + 8, size), f32), ((8, 128), f32)],
        )(*((own, off) if images else (off, own)), exchange(pay, axes))

    keep, send, share = lax.cond(
        image_core,
        functools.partial(grads, True, n_plane, PLANE),
        functools.partial(grads, False, n_line, LINE),
    )
    image_grad, text_grad, loss = call(
        functools.partial(output_kernel, batch),
        [((half, size), f32), ((half, size), f32), ((1, 1), f32)],
    )(keep, share, swap(send))
    return loss.reshape(()), image_grad, text_grad


def solution(mesh):
    shape = (mesh.shape["row"], 4, mesh.shape["col"] // 8, 2)
    fine = Mesh(mesh.devices.reshape(shape), ("z", "y", "x", "c"))
    by_image, by_text = P(("z", "y", "x", "c")), P(("y", "x", "c", "z"))
    return jax.shard_map(
        local,
        mesh=fine,
        in_specs=(by_image, by_text, by_image),
        out_specs=(P(), by_image, by_text),
        check_vma=False,
    )
```

```python
import functools
import math

import jax
import jax.numpy as jnp
from jax import lax
from jax.experimental import pallas as pl
from jax.experimental.pallas import tpu as pltpu
from jax.sharding import Mesh, PartitionSpec as P

sharpness = 1.0 / 0.07
f32 = jnp.float32
bf16 = jnp.bfloat16
NT = (((1,), (1,)), ((), ()))
PLANE, LINE = ("y", "x"), "z"
EXTRA = 16


def normalize(embed):
    flat = embed.astype(f32)
    factor = lax.rsqrt(jnp.sum(flat * flat, axis=1, keepdims=True) + 1e-06)
    return flat * factor, factor


def pack(dst, b, value):
    rows = value.shape[0]
    for k in range(value.shape[1] // 128):
        dst[b, k * rows : (k + 1) * rows, :] = value[:, k * 128 : (k + 1) * 128]


def unpack(ref, first, count, rows, width):
    return jnp.concatenate(
        [
            ref[first : first + count, k * rows : (k + 1) * rows, :].reshape(count * rows, 128)
            for k in range(width // 128)
        ],
        axis=1,
    )


def rows_tile(values):
    row = lax.broadcasted_iota(jnp.int32, (EXTRA, 128), 0)
    tile = jnp.zeros((EXTRA, 128), f32)
    for i, v in enumerate(values):
        tile = jnp.where(row == i, v, tile)
    return tile.astype(bf16)


def start_kernel(img_hbm, txt_hbm, partner_hbm, keep_ref, send_ref, img, txt, partner, sems):
    copies = [
        pltpu.make_async_copy(src, dst, sems.at[i])
        for i, (src, dst) in enumerate(((img_hbm, img), (txt_hbm, txt), (partner_hbm, partner)))
    ]
    for c in copies:
        c.start()
    for c in copies:
        c.wait()
    image_core = lax.axis_index("c") == 0
    half, size = img.shape
    a, b = img[...].astype(f32), txt[...].astype(f32)
    keep_ref[:half] = jnp.where(image_core, a, b).astype(bf16)
    send_ref[:half] = jnp.where(image_core, b, a).astype(bf16)
    p = jnp.concatenate([partner[...]] * (128 // half), axis=1)
    hi = p // 128
    tile = rows_tile([hi.astype(f32), (p - hi * 128).astype(f32)])
    for dst in (keep_ref, send_ref):
        dst[half:] = jnp.zeros((EXTRA, size), bf16)
        dst[half:, :128] = tile


def prep_kernel(images, first, second, out):
    half = first.shape[0] - EXTRA
    unit = [normalize(src[:half, :])[0] for src in (first, second)]
    unit = jnp.concatenate(unit, axis=0).astype(bf16)
    size = unit.size // 128
    tile = jnp.zeros((EXTRA, 128), bf16)
    if images:
        lane = lax.broadcasted_iota(jnp.int32, (EXTRA, 128), 1)
        a, b = (src[half:, :128].astype(f32) for src in (first, second))
        tile = jnp.where(lane // half % 2 == 0, a, b).astype(bf16)
    for b in range(out.shape[0]):
        pack(out, b, unit)
        out[b, size:, :] = tile


def place(images, tiles, r, t, ny):
    per_half = tiles // 2
    half, tile = divmod(r * ny + t, per_half)
    if not images:
        half = 1 - half
    return half * (per_half // 2) + tile // 2, slice(tile % 2 * 128, tile % 2 * 128 + 128)


def scores_kernel(images, rows, x_ref, y_ref, e_ref, pay_ref, match_ref, *scratch):
    packed = x_ref.shape[1]
    width = (packed - EXTRA) // rows * 128
    per, half = 128 // rows, rows // 2
    texts = x_ref.shape[0] // 2
    nx, ny = x_ref.shape[0] // per, y_ref.shape[0] // per
    if images:
        ny = texts // per
    else:
        nx = texts // per
    lane = lax.broadcasted_iota(jnp.int32, (1, 128), 1)
    chip = lax.axis_index("y") * lax.axis_size("x") + lax.axis_index("x")
    tail = (x_ref if images else y_ref)[:, packed - EXTRA :, :].astype(f32)
    partner = tail[:, 0, :] * 128.0 + tail[:, 1, :]

    def partners(t):
        p = partner[per * t : per * t + 1]
        for q in range(1, per):
            p = jnp.where(lane >= q * rows, partner[per * t + q : per * t + q + 1], p)
        return p

    def ids(t):
        i = (lane % rows) // half * (texts * half) + (per * t + lane // rows) * half
        return (chip * (texts * rows) + i + lane % half).astype(f32)

    xs, ys = (partners, ids) if images else (ids, partners)
    xs_ref, ys_ref, *s_refs = scratch
    for r in range(nx):
        xs_ref[r : r + 1] = xs(r)
    for t in range(ny):
        ys_ref[t : t + 1] = ys(t)
    part = nx // 2

    def product(h):
        x = unpack(x_ref, h * part * per, part * per, rows, width)
        y = unpack(y_ref, 0, ny * per, rows, width)
        s = lax.dot_general(x, y, NT, preferred_element_type=f32)
        for r in range(part):
            for t in range(ny):
                s_refs[h][r * ny + t] = s[r * 128 : (r + 1) * 128, t * 128 : (t + 1) * 128]

    def weigh(h):
        for r in range(h * part, (h + 1) * part):
            own = jnp.broadcast_to(xs_ref[r : r + 1], (128, 128)).T
            lanes = jnp.zeros((128, 128), f32)
            found = jnp.zeros((128, 128), f32)
            for t in range(ny):
                e = jnp.exp2(s_refs[h][(r - h * part) * ny + t] * f32(sharpness * math.log2(math.e)))
                matched = jnp.where(own == ys_ref[t : t + 1], e, f32(0.0))
                lanes += e
                found += matched
                block, at = place(images, nx * ny, r, t, ny)
                e_ref[block, at] = (e - f32(2.0) * matched).astype(bf16)
            pay_ref[0, r : r + 1] = jnp.sum(lanes.T, axis=0, keepdims=True)
            match_ref[r : r + 1] = jnp.sum(found.T, axis=0, keepdims=True)

    once = jnp.minimum(lax.axis_index("c") + 1, 1)
    product(0)

    def first(i, carry):
        product(1)
        weigh(0)
        return carry

    def second(i, carry):
        weigh(1)
        return carry

    lax.fori_loop(0, once, first, 0)
    lax.fori_loop(0, once, second, 0)
    if not images:
        m = match_ref[:nx]
        logs = jnp.where(m > 0.0, jnp.log(jnp.where(m > 0.0, m, f32(1.0))), f32(0.0))
        logs = jnp.sum(jnp.sum(logs, axis=0, keepdims=True), axis=1, keepdims=True)
        pay_ref[0, nx:] = jnp.broadcast_to(logs, (8 - nx, 128))
        match_ref[nx:] = jnp.zeros((8 - nx, 128), f32)
    for b in range(1, pay_ref.shape[0]):
        pay_ref[b] = pay_ref[0]


def grads_kernel(images, rows, y_ref, e_ref, match_ref, mine_ref, other_ref, out_ref):
    blocks, packed, _ = out_ref.shape
    width = (packed - EXTRA) // rows * 128
    per = 128 // rows
    nx = blocks // per
    ny = e_ref.shape[0] * 2 // nx
    col_total = other_ref[:ny]
    col_inv = f32(1.0) / col_total
    share = jnp.sum(jnp.log(col_total), axis=0, keepdims=True)
    share = jnp.broadcast_to(jnp.sum(share, axis=1, keepdims=True), (1, 128))
    if images:
        share -= 2.0 * other_ref[ny : ny + 1]
    hi = share.astype(bf16).astype(f32)
    mid = (share - hi).astype(bf16).astype(f32)
    share = rows_tile([hi, mid, share - hi - mid])
    row_inv = f32(1.0) / mine_ref[:nx]
    y = unpack(y_ref, 0, ny * per, rows, width)
    ds = []
    for r in range(nx):
        ri = jnp.broadcast_to(row_inv[r : r + 1], (128, 128)).T
        matched = jnp.broadcast_to(match_ref[r : r + 1], (128, 128)).T
        d = []
        for t in range(ny):
            block, at = place(images, nx * ny, r, t, ny)
            e = e_ref[block, at].astype(f32)
            weight = ri + col_inv[t : t + 1]
            v = jnp.where(e < 0.0, matched * weight - f32(2.0), e * weight)
            d.append(v.astype(bf16))
        ds.append(jnp.concatenate(d, axis=1))
    g = jnp.dot(jnp.concatenate(ds, axis=0), y, preferred_element_type=f32).astype(bf16)
    for b in range(blocks):
        pack(out_ref, b, g[b * rows : (b + 1) * rows])
        out_ref[b, packed - EXTRA :, :] = share


def finish_kernel(scale, keep_first, first, second, parts, keep_ref, send_ref, share_ref):
    half, size = keep_ref.shape
    rows = 2 * half
    body = rows * (size // 128)
    total = parts[0, :body, :].astype(f32)
    for b in range(1, parts.shape[0]):
        total += parts[b, :body, :].astype(f32)
    total = total * f32(scale)
    total = jnp.concatenate(
        [total[k * rows : (k + 1) * rows] for k in range(size // 128)], axis=1
    )
    grads = []
    for i, src in enumerate((first, second)):
        unit, factor = normalize(src[:half, :])
        g = total[i * half : (i + 1) * half]
        grads.append(factor * (g - unit * jnp.sum(unit * g, axis=1, keepdims=True)))
    keep, send = grads if keep_first else grads[::-1]
    keep_ref[...] = keep
    send_ref[:half] = send
    share = parts[:, body:, :].astype(f32)
    share = jnp.sum(jnp.sum(share, axis=0), axis=0, keepdims=True)
    share_ref[...] = jnp.broadcast_to(share, share_ref.shape)
    send_ref[half:] = jnp.broadcast_to(share[:, :1], (send_ref.shape[0] - half, size))


def output_kernel(batch, keep_ref, share_ref, recv_ref, img_ref, txt_ref, loss_ref):
    image_core = lax.axis_index("c") == 0
    half = keep_ref.shape[0]
    keep, recv = keep_ref[...], recv_ref[:half]
    img_ref[...] = jnp.where(image_core, keep, recv)
    txt_ref[...] = jnp.where(image_core, recv, keep)
    loss_ref[...] = (share_ref[:1, :1] + recv_ref[half : half + 1, :1]) / (2.0 * batch)


def call(kernel, outs, **kw):
    return pl.pallas_call(
        kernel,
        out_shape=[jax.ShapeDtypeStruct(*o) for o in outs],
        compiler_params=pltpu.CompilerParams(vmem_limit_bytes=48 * 1024 * 1024),
        **kw,
    )


def exchange(x, axes):
    return lax.all_to_all(x, axes, 0, 0)


def swap(x):
    return lax.ppermute(x, "c", [(0, 1), (1, 0)])


def local(image_embed, text_embed, partner):
    half, size = image_embed.shape
    rows = 2 * half
    n_plane = lax.axis_size("y") * lax.axis_size("x")
    n_line = lax.axis_size("z")
    batch = rows * n_plane * n_line
    image_core = lax.axis_index("c") == 0
    packed = rows * (size // 128) + EXTRA
    tiles = n_plane * n_line * rows * rows // (128 * 128)

    args = [
        pltpu.with_memory_space_constraint(a, pltpu.HBM)
        for a in (image_embed, text_embed, partner.reshape(1, half))
    ]
    own, send = call(
        start_kernel,
        [((half + EXTRA, size), bf16)] * 2,
        in_specs=[pl.BlockSpec(memory_space=pl.ANY)] * 3,
        scratch_shapes=[
            pltpu.VMEM((half, size), bf16),
            pltpu.VMEM((half, size), bf16),
            pltpu.VMEM((1, half), jnp.int32),
            pltpu.SemaphoreType.DMA((3,)),
        ],
    )(*args)
    off = swap(send)

    def gather_images():
        kernel = functools.partial(prep_kernel, True)
        return exchange(call(kernel, [((n_plane, packed, 128), bf16)])(own, off)[0], PLANE)

    def gather_texts():
        kernel = functools.partial(prep_kernel, False)
        every = exchange(call(kernel, [((n_line, packed, 128), bf16)])(off, own)[0], LINE)
        return jnp.pad(every, ((0, n_plane - n_line), (0, 0), (0, 0)))

    x = lax.cond(image_core, gather_images, gather_texts)
    y = swap(x)

    def sums(images, count, axes):
        e, pay, match = call(
            functools.partial(scores_kernel, images, rows),
            [((n_plane, packed, 128), bf16), ((count, 8, 128), f32), ((8, 128), f32)],
            input_output_aliases={0: 0},
            scratch_shapes=[pltpu.VMEM((8, 128), f32)] * 2
            + [pltpu.VMEM((tiles // 2, 128, 128), f32)] * 2,
        )(x, y)
        return e, match, jnp.sum(exchange(pay, axes), axis=0)

    e, match, mine = lax.cond(
        image_core,
        functools.partial(sums, True, n_plane, PLANE),
        functools.partial(sums, False, n_line, LINE),
    )
    other = swap(mine)

    def grads(images, count, axes):
        pay = call(
            functools.partial(grads_kernel, images, rows),
            [((count, packed, 128), bf16)],
        )(y, e, match, mine, other)[0]
        return call(
            functools.partial(finish_kernel, sharpness / (2.0 * batch), images),
            [((half, size), f32), ((half + 8, size), f32), ((8, 128), f32)],
        )(*((own, off) if images else (off, own)), exchange(pay, axes))

    keep, send, share = lax.cond(
        image_core,
        functools.partial(grads, True, n_plane, PLANE),
        functools.partial(grads, False, n_line, LINE),
    )
    image_grad, text_grad, loss = call(
        functools.partial(output_kernel, batch),
        [((half, size), f32), ((half, size), f32), ((1, 1), f32)],
    )(keep, share, swap(send))
    return loss.reshape(()), image_grad, text_grad


def solution(mesh):
    shape = (mesh.shape["row"], 4, mesh.shape["col"] // 8, 2)
    fine = Mesh(mesh.devices.reshape(shape), ("z", "y", "x", "c"))
    by_image, by_text = P(("z", "y", "x", "c")), P(("y", "x", "c", "z"))
    return jax.shard_map(
        local,
        mesh=fine,
        in_specs=(by_image, by_text, by_image),
        out_specs=(P(), by_image, by_text),
        check_vma=False,
    )
```

```python
import functools
import math

import jax
import jax.numpy as jnp
from jax import lax
from jax.experimental import pallas as pl
from jax.experimental.pallas import tpu as pltpu
from jax.sharding import Mesh, PartitionSpec as P

sharpness = 1.0 / 0.07
f32 = jnp.float32
bf16 = jnp.bfloat16
NT = (((1,), (1,)), ((), ()))
PLANE, LINE = ("y", "x"), "z"
EXTRA = 16


def normalize(embed):
    flat = embed.astype(f32)
    factor = lax.rsqrt(jnp.sum(flat * flat, axis=1, keepdims=True) + 1e-06)
    return flat * factor, factor


def unpack(ref, rows, width):
    count = ref.shape[0]
    return jnp.concatenate(
        [
            ref[:, k * rows : (k + 1) * rows, :].reshape(count * rows, 128)
            for k in range(width // 128)
        ],
        axis=1,
    )


def rows_tile(values):
    row = lax.broadcasted_iota(jnp.int32, (EXTRA, 128), 0)
    tile = jnp.zeros((EXTRA, 128), f32)
    for i, v in enumerate(values):
        tile = jnp.where(row == i, v, tile)
    return tile.astype(bf16)


def start_kernel(img_hbm, txt_hbm, partner_hbm, pay_ref, txt_ref, img, txt, partner, sems):
    copies = [
        pltpu.make_async_copy(src, dst, sems.at[i])
        for i, (src, dst) in enumerate(((img_hbm, img), (txt_hbm, txt), (partner_hbm, partner)))
    ]
    for c in copies:
        c.start()
    for c in copies:
        c.wait()
    rows, size = img.shape
    p = jnp.concatenate([partner[...]] * (128 // rows), axis=1)
    hi = p // 128
    tile = rows_tile([hi.astype(f32), (p - hi * 128).astype(f32)])
    unit = normalize(img[...])[0].astype(bf16)
    texts = normalize(txt[...])[0].astype(bf16)
    chunks = size // 128
    for k in range(chunks):
        at = slice(k * 128, (k + 1) * 128)
        txt_ref[k * rows : (k + 1) * rows, :] = texts[:, at]
        for b in range(pay_ref.shape[0]):
            pay_ref[b, k * rows : (k + 1) * rows, :] = unit[:, at]
    for b in range(pay_ref.shape[0]):
        pay_ref[b, chunks * rows :, :] = tile


def chip_texts_kernel(rows, own_ref, off_ref, out_ref):
    low = lax.axis_index("c") == 0
    own, off = own_ref[...].astype(f32), off_ref[...].astype(f32)
    first, second = jnp.where(low, own, off).astype(bf16), jnp.where(low, off, own).astype(bf16)
    for k in range(own.shape[0] // rows):
        at = slice(k * rows, (k + 1) * rows)
        out_ref[2 * k * rows : (2 * k + 1) * rows, :] = first[at]
        out_ref[(2 * k + 1) * rows : (2 * k + 2) * rows, :] = second[at]


def order_texts(images, pieces, texts_ref):
    count = texts_ref.shape[0]
    steps = (count - 1) // 2
    sign = -1 if images else 1
    away = [0, count // 2]
    away += [sign * (k + 1) for k in range(steps)] + [-sign * (k + 1) for k in range(steps)]
    z = lax.axis_index("z")
    for piece, d in zip(pieces, away):
        texts_ref[lax.rem(z + (d + count), count)] = piece[...]


def scores_kernel(images, width, low_ref, high_ref, *refs):
    *pieces, e_ref, pay_ref, match_ref, texts_ref = refs
    plane, packed, _ = low_ref.shape
    line, body, _ = texts_ref.shape
    rows = body * 128 // width // 2
    order_texts(images, pieces, texts_ref)
    lane = lax.broadcasted_iota(jnp.int32, (1, 128), 1)
    chip = lax.axis_index("y") * lax.axis_size("x") + lax.axis_index("x")
    partner = []
    for ref in (low_ref, high_ref):
        tail = ref[:, packed - EXTRA :, :].astype(f32)
        partner.append(tail[:, 0, :] * 128.0 + tail[:, 1, :])
    per = 128 // rows
    image_chunks, text_chunks = 2 * plane // per, 2 * line // per

    def partners(t):
        source, first = partner[t * per // plane], t * per % plane
        p = source[first : first + 1]
        for q in range(1, per):
            p = jnp.where(lane >= q * rows, source[first + q : first + q + 1], p)
        return p

    def ids(t):
        block = t * per // 2 + lane // (2 * rows)
        i = (chip * 2 + lane % (2 * rows) // rows) * (line * rows) + block * rows
        return (i + lane % rows).astype(f32)

    all_images = jnp.concatenate([unpack(r, rows, width) for r in (low_ref, high_ref)], axis=0)
    all_texts = unpack(texts_ref, 2 * rows, width)
    if images:
        x, y, nx, ny, xs, ys = all_images, all_texts, image_chunks, text_chunks, partners, ids
    else:
        x, y, nx, ny, xs, ys = all_texts, all_images, text_chunks, image_chunks, ids, partners
    targets = [ys(t) for t in range(ny)]
    scores = lax.dot_general(x, y, NT, preferred_element_type=f32)
    for r in range(nx):
        own = jnp.broadcast_to(xs(r), (128, 128)).T
        lanes = jnp.zeros((128, 128), f32)
        found = jnp.zeros((128, 128), f32)
        for t in range(ny):
            s = scores[r * 128 : (r + 1) * 128, t * 128 : (t + 1) * 128]
            e = jnp.exp2(s * f32(sharpness * math.log2(math.e)))
            matched = jnp.where(own == targets[t], e, f32(0.0))
            lanes += e
            found += matched
            e_ref[r * ny + t] = (e - f32(2.0) * matched).astype(bf16)
        pay_ref[0, r : r + 1] = jnp.sum(lanes.T, axis=0, keepdims=True)
        match_ref[r : r + 1] = jnp.sum(found.T, axis=0, keepdims=True)
    if not images:
        m = match_ref[:nx]
        logs = jnp.where(m > 0.0, jnp.log(jnp.where(m > 0.0, m, f32(1.0))), f32(0.0))
        logs = jnp.sum(jnp.sum(logs, axis=0, keepdims=True), axis=1, keepdims=True)
        pay_ref[0, nx:] = jnp.broadcast_to(logs, (8 - nx, 128))
        match_ref[nx:] = jnp.zeros((8 - nx, 128), f32)
    for b in range(1, pay_ref.shape[0]):
        pay_ref[b] = pay_ref[0]


def grads_kernel(images, width, e_ref, match_ref, mine_ref, other_ref, *refs):
    if images:
        *pieces, out_ref, texts_ref = refs
        order_texts(images, pieces, texts_ref)
    else:
        low_ref, high_ref, out_ref = refs
    blocks, packed, _ = out_ref.shape
    rows = (packed - EXTRA) * 128 // width // 2
    nx = blocks * 2 * rows // 128
    ny = e_ref.shape[0] // nx
    if images:
        y = unpack(texts_ref, 2 * rows, width)
    else:
        y = jnp.concatenate([unpack(r, rows, width) for r in (low_ref, high_ref)], axis=0)
    col_total = other_ref[:ny]
    col_inv = f32(1.0) / col_total
    share = jnp.sum(jnp.log(col_total), axis=0, keepdims=True)
    share = jnp.broadcast_to(jnp.sum(share, axis=1, keepdims=True), (1, 128))
    if images:
        share -= 2.0 * other_ref[ny : ny + 1]
    hi = share.astype(bf16).astype(f32)
    mid = (share - hi).astype(bf16).astype(f32)
    share = rows_tile([hi, mid, share - hi - mid])
    row_inv = f32(1.0) / mine_ref[:nx]
    ds = []
    for r in range(nx):
        ri = jnp.broadcast_to(row_inv[r : r + 1], (128, 128)).T
        matched = jnp.broadcast_to(match_ref[r : r + 1], (128, 128)).T
        d = []
        for t in range(ny):
            e = e_ref[r * ny + t].astype(f32)
            weight = ri + col_inv[t : t + 1]
            v = jnp.where(e < 0.0, matched * weight - f32(2.0), e * weight)
            d.append(v.astype(bf16))
        ds.append(jnp.concatenate(d, axis=1))
    g = jnp.dot(jnp.concatenate(ds, axis=0), y, preferred_element_type=f32).astype(bf16)
    for b in range(blocks):
        for h in range(2):
            first = (h * blocks + b) * rows if images else (b * 2 + h) * rows
            for k in range(width // 128):
                at = (2 * k + h) * rows
                out_ref[b, at : at + rows, :] = g[first : first + rows, k * 128 : (k + 1) * 128]
        out_ref[b, packed - EXTRA :, :] = share


def sum_kernel(images, parts, keep_ref, send_ref, share_ref):
    rows, size = keep_ref.shape
    body = 2 * rows * (size // 128)
    total = parts[0, :body, :].astype(f32)
    for b in range(1, parts.shape[0]):
        total += parts[b, :body, :].astype(f32)
    low, high = (
        jnp.concatenate(
            [total[(2 * k + h) * rows : (2 * k + h + 1) * rows] for k in range(size // 128)],
            axis=1,
        )
        for h in range(2)
    )
    keep, send = (low, high) if images else (high, low)
    keep_ref[...] = keep
    send_ref[:rows] = send
    share = parts[:, body:, :].astype(f32)
    share = jnp.sum(jnp.sum(share, axis=0), axis=0, keepdims=True)
    share_ref[...] = jnp.broadcast_to(share, share_ref.shape)
    send_ref[rows:] = jnp.broadcast_to(share[:, :1], (send_ref.shape[0] - rows, size))


def output_kernel(batch, img_ref, txt_ref, keep_ref, share_ref, recv_ref, img_out, txt_out, loss_ref):
    low = lax.axis_index("c") == 0
    rows = keep_ref.shape[0]
    keep, recv = keep_ref[...], recv_ref[:rows]
    for src, first, second, dst in ((img_ref, keep, recv, img_out), (txt_ref, recv, keep, txt_out)):
        g = jnp.where(low, first, second) * f32(sharpness / (2.0 * batch))
        unit, factor = normalize(src[...])
        dst[...] = factor * (g - unit * jnp.sum(unit * g, axis=1, keepdims=True))
    loss_ref[...] = (share_ref[:1, :1] + recv_ref[rows : rows + 1, :1]) / (2.0 * batch)


def call(kernel, outs, **kw):
    return pl.pallas_call(
        kernel,
        out_shape=[o if isinstance(o, pl.MemoryRef) else jax.ShapeDtypeStruct(*o) for o in outs],
        compiler_params=pltpu.CompilerParams(vmem_limit_bytes=48 * 1024 * 1024),
        **kw,
    )


def exchange(x, axes):
    return lax.all_to_all(x, axes, 0, 0)


def swap(x):
    return lax.ppermute(x, "c", [(0, 1), (1, 0)])


def local(image_embed, text_embed, partner):
    rows, size = image_embed.shape
    n_plane = lax.axis_size("y") * lax.axis_size("x")
    n_line = lax.axis_size("z")
    batch = 2 * rows * n_plane * n_line
    image_core = lax.axis_index("c") == 0
    half = rows * (size // 128)
    packed = 2 * half + EXTRA
    tiles = n_plane * n_line * 4 * rows * rows // (128 * 128)

    args = [
        pltpu.with_memory_space_constraint(a, pltpu.HBM)
        for a in (image_embed, text_embed, partner.reshape(1, rows))
    ]
    pay, own_texts = call(
        start_kernel,
        [((n_plane, half + EXTRA, 128), bf16), ((half, 128), bf16)],
        in_specs=[pl.BlockSpec(memory_space=pl.ANY)] * 3,
        scratch_shapes=[
            pltpu.VMEM((rows, size), bf16),
            pltpu.VMEM((rows, size), bf16),
            pltpu.VMEM((1, rows), jnp.int32),
            pltpu.SemaphoreType.DMA((3,)),
        ],
    )(*args)
    own_images = exchange(pay, PLANE)
    here = call(functools.partial(chip_texts_kernel, rows), [((2 * half, 128), bf16)])(
        own_texts, swap(own_texts)
    )[0]

    def along(k):
        up = [(2 * z, 2 * ((z + k) % n_line)) for z in range(n_line)]
        down = [(2 * z + 1, 2 * ((z - k) % n_line) + 1) for z in range(n_line)]
        return lax.ppermute(here, ("z", "c"), up + down)

    far = along(n_line // 2)
    near = [along(k + 1) for k in range((n_line - 1) // 2)]
    pieces = [here, far, *near, *[swap(p) for p in near]]
    off_images = swap(own_images)

    def sums(images, count, axes):
        low, high = (own_images, off_images) if images else (off_images, own_images)
        e, pay, match = call(
            functools.partial(scores_kernel, images, size),
            [
                pltpu.VMEM((tiles, 128, 128), bf16),
                ((count, 8, 128), f32),
                ((8, 128), f32),
            ],
            scratch_shapes=[pltpu.VMEM((n_line, 2 * half, 128), bf16)],
        )(low, high, *pieces)
        return e, match, jnp.sum(exchange(pay, axes), axis=0)

    e, match, mine = lax.cond(
        image_core,
        functools.partial(sums, True, n_plane, PLANE),
        functools.partial(sums, False, n_line, LINE),
    )
    other = swap(mine)

    def grads(images, count, axes):
        y = pieces if images else [off_images, own_images]
        kw = {}
        if images:
            kw["scratch_shapes"] = [pltpu.VMEM((n_line, 2 * half, 128), bf16)]
        pay = call(
            functools.partial(grads_kernel, images, size), [((count, packed, 128), bf16)], **kw
        )(e, match, mine, other, *y)[0]
        return call(
            functools.partial(sum_kernel, images),
            [((rows, size), f32), ((rows + 8, size), f32), ((8, 128), f32)],
        )(exchange(pay, axes))

    keep, send, share = lax.cond(
        image_core,
        functools.partial(grads, True, n_plane, PLANE),
        functools.partial(grads, False, n_line, LINE),
    )
    image_grad, text_grad, loss = call(
        functools.partial(output_kernel, batch),
        [((rows, size), f32), ((rows, size), f32), ((1, 1), f32)],
    )(image_embed, text_embed, keep, share, swap(send))
    return loss.reshape(()), image_grad, text_grad


def solution(mesh):
    shape = (mesh.shape["row"], 4, mesh.shape["col"] // 8, 2)
    fine = Mesh(mesh.devices.reshape(shape), ("z", "y", "x", "c"))
    by_image, by_text = P(("z", "y", "x", "c")), P(("y", "x", "c", "z"))
    return jax.shard_map(
        local,
        mesh=fine,
        in_specs=(by_image, by_text, by_image),
        out_specs=(P(), by_image, by_text),
        check_vma=False,
    )
```

```python
import functools
import math

import jax
import jax.numpy as jnp
from jax import lax
from jax.experimental import pallas as pl
from jax.experimental.pallas import tpu as pltpu
from jax.sharding import Mesh, PartitionSpec as P

sharpness = 1.0 / 0.07
f32 = jnp.float32
bf16 = jnp.bfloat16
NT = (((1,), (1,)), ((), ()))
PLANE, LINE = ("y", "x"), "z"
EXTRA = 16


def normalize(embed):
    flat = embed.astype(f32)
    factor = lax.rsqrt(jnp.sum(flat * flat, axis=1, keepdims=True) + 1e-06)
    return flat * factor, factor


def unpack(ref, rows, width):
    count = ref.shape[0]
    return jnp.concatenate(
        [
            ref[:, k * rows : (k + 1) * rows, :].reshape(count * rows, 128)
            for k in range(width // 128)
        ],
        axis=1,
    )


def rows_tile(values):
    row = lax.broadcasted_iota(jnp.int32, (EXTRA, 128), 0)
    tile = jnp.zeros((EXTRA, 128), f32)
    for i, v in enumerate(values):
        tile = jnp.where(row == i, v, tile)
    return tile.astype(bf16)


def start_kernel(img_hbm, txt_hbm, partner_hbm, pay_ref, txt_ref, img, txt, partner, sems):
    copies = [
        pltpu.make_async_copy(src, dst, sems.at[i])
        for i, (src, dst) in enumerate(((img_hbm, img), (txt_hbm, txt), (partner_hbm, partner)))
    ]
    for c in copies:
        c.start()
    for c in copies:
        c.wait()
    rows, size = img.shape
    p = jnp.concatenate([partner[...]] * (128 // rows), axis=1)
    hi = p // 128
    tile = rows_tile([hi.astype(f32), (p - hi * 128).astype(f32)])
    unit = normalize(img[...])[0].astype(bf16)
    texts = normalize(txt[...])[0].astype(bf16)
    chunks = size // 128
    for k in range(chunks):
        at = slice(k * 128, (k + 1) * 128)
        txt_ref[k * rows : (k + 1) * rows, :] = texts[:, at]
        for b in range(pay_ref.shape[0]):
            pay_ref[b, k * rows : (k + 1) * rows, :] = unit[:, at]
    for b in range(pay_ref.shape[0]):
        pay_ref[b, chunks * rows :, :] = tile


def chip_texts_kernel(rows, own_ref, off_ref, out_ref):
    low = lax.axis_index("c") == 0
    own, off = own_ref[...].astype(f32), off_ref[...].astype(f32)
    first, second = jnp.where(low, own, off).astype(bf16), jnp.where(low, off, own).astype(bf16)
    for k in range(own.shape[0] // rows):
        at = slice(k * rows, (k + 1) * rows)
        out_ref[2 * k * rows : (2 * k + 1) * rows, :] = first[at]
        out_ref[(2 * k + 1) * rows : (2 * k + 2) * rows, :] = second[at]


def order_texts(images, pieces, texts_ref):
    count = texts_ref.shape[0]
    steps = (count - 1) // 2
    sign = -1 if images else 1
    away = [0, count // 2]
    away += [sign * (k + 1) for k in range(steps)] + [-sign * (k + 1) for k in range(steps)]
    z = lax.axis_index("z")
    for piece, d in zip(pieces, away):
        texts_ref[lax.rem(z + (d + count), count)] = piece[...]


def scores_kernel(images, width, low_ref, high_ref, *refs):
    *pieces, e_ref, pay_ref, match_ref, texts_ref = refs
    plane, packed, _ = low_ref.shape
    line, body, _ = texts_ref.shape
    rows = body * 128 // width // 2
    order_texts(images, pieces, texts_ref)
    lane = lax.broadcasted_iota(jnp.int32, (1, 128), 1)
    chip = lax.axis_index("y") * lax.axis_size("x") + lax.axis_index("x")
    partner = []
    for ref in (low_ref, high_ref):
        tail = ref[:, packed - EXTRA :, :].astype(f32)
        partner.append(tail[:, 0, :] * 128.0 + tail[:, 1, :])
    per = 128 // rows
    image_chunks, text_chunks = 2 * plane // per, 2 * line // per

    def partners(t):
        source, first = partner[t * per // plane], t * per % plane
        p = source[first : first + 1]
        for q in range(1, per):
            p = jnp.where(lane >= q * rows, source[first + q : first + q + 1], p)
        return p

    def ids(t):
        block = t * per // 2 + lane // (2 * rows)
        i = (chip * 2 + lane % (2 * rows) // rows) * (line * rows) + block * rows
        return (i + lane % rows).astype(f32)

    all_images = jnp.concatenate([unpack(r, rows, width) for r in (low_ref, high_ref)], axis=0)
    all_texts = unpack(texts_ref, 2 * rows, width)
    if images:
        x, y, nx, ny, xs, ys = all_images, all_texts, image_chunks, text_chunks, partners, ids
    else:
        x, y, nx, ny, xs, ys = all_texts, all_images, text_chunks, image_chunks, ids, partners
    targets = [ys(t) for t in range(ny)]
    scores = lax.dot_general(x, y, NT, preferred_element_type=f32)
    for r in range(nx):
        own = jnp.broadcast_to(xs(r), (128, 128)).T
        lanes = jnp.zeros((128, 128), f32)
        found = jnp.zeros((128, 128), f32)
        for t in range(ny):
            s = scores[r * 128 : (r + 1) * 128, t * 128 : (t + 1) * 128]
            e = jnp.exp2(s * f32(sharpness * math.log2(math.e)))
            matched = jnp.where(own == targets[t], e, f32(0.0))
            lanes += e
            found += matched
            e_ref[r * ny + t] = (e - f32(2.0) * matched).astype(bf16)
        pay_ref[0, r : r + 1] = jnp.sum(lanes.T, axis=0, keepdims=True)
        match_ref[r : r + 1] = jnp.sum(found.T, axis=0, keepdims=True)
    if not images:
        m = match_ref[:nx]
        logs = jnp.where(m > 0.0, jnp.log(jnp.where(m > 0.0, m, f32(1.0))), f32(0.0))
        logs = jnp.sum(jnp.sum(logs, axis=0, keepdims=True), axis=1, keepdims=True)
        pay_ref[0, nx:] = jnp.broadcast_to(logs, (8 - nx, 128))
        match_ref[nx:] = jnp.zeros((8 - nx, 128), f32)
    for b in range(1, pay_ref.shape[0]):
        pay_ref[b] = pay_ref[0]


def grads_kernel(images, width, e_ref, match_ref, mine_ref, other_ref, *refs):
    if images:
        *pieces, out_ref, texts_ref = refs
        order_texts(images, pieces, texts_ref)
    else:
        low_ref, high_ref, out_ref = refs
    blocks, packed, _ = out_ref.shape
    rows = (packed - EXTRA) * 128 // width // 2
    nx = blocks * 2 * rows // 128
    ny = e_ref.shape[0] // nx
    if images:
        y = unpack(texts_ref, 2 * rows, width)
    else:
        y = jnp.concatenate([unpack(r, rows, width) for r in (low_ref, high_ref)], axis=0)
    col_total = other_ref[:ny]
    col_inv = f32(1.0) / col_total
    share = jnp.sum(jnp.log(col_total), axis=0, keepdims=True)
    share = jnp.broadcast_to(jnp.sum(share, axis=1, keepdims=True), (1, 128))
    if images:
        share -= 2.0 * other_ref[ny : ny + 1]
    hi = share.astype(bf16).astype(f32)
    mid = (share - hi).astype(bf16).astype(f32)
    share = rows_tile([hi, mid, share - hi - mid])
    row_inv = f32(1.0) / mine_ref[:nx]
    ds = []
    for r in range(nx):
        ri = jnp.broadcast_to(row_inv[r : r + 1], (128, 128)).T
        matched = jnp.broadcast_to(match_ref[r : r + 1], (128, 128)).T
        d = []
        for t in range(ny):
            e = e_ref[r * ny + t].astype(f32)
            weight = ri + col_inv[t : t + 1]
            v = jnp.where(e < 0.0, matched * weight - f32(2.0), e * weight)
            d.append(v.astype(bf16))
        ds.append(jnp.concatenate(d, axis=1))
    g = jnp.dot(jnp.concatenate(ds, axis=0), y, preferred_element_type=f32).astype(bf16)
    for b in range(blocks):
        for h in range(2):
            first = (h * blocks + b) * rows if images else (b * 2 + h) * rows
            for k in range(width // 128):
                at = (2 * k + h) * rows
                out_ref[b, at : at + rows, :] = g[first : first + rows, k * 128 : (k + 1) * 128]
        out_ref[b, packed - EXTRA :, :] = share


def sum_kernel(images, parts, keep_ref, send_ref, share_ref):
    rows, size = keep_ref.shape
    body = 2 * rows * (size // 128)
    total = parts[0, :body, :].astype(f32)
    for b in range(1, parts.shape[0]):
        total += parts[b, :body, :].astype(f32)
    low, high = (
        jnp.concatenate(
            [total[(2 * k + h) * rows : (2 * k + h + 1) * rows] for k in range(size // 128)],
            axis=1,
        )
        for h in range(2)
    )
    keep, send = (low, high) if images else (high, low)
    keep_ref[...] = keep
    send_ref[:rows] = send
    share = parts[:, body:, :].astype(f32)
    share = jnp.sum(jnp.sum(share, axis=0), axis=0, keepdims=True)
    share_ref[...] = jnp.broadcast_to(share, share_ref.shape)
    send_ref[rows:] = jnp.broadcast_to(share[:, :1], (send_ref.shape[0] - rows, size))


def output_kernel(batch, img_ref, txt_ref, keep_ref, share_ref, recv_ref, img_out, txt_out, loss_ref):
    low = lax.axis_index("c") == 0
    rows = keep_ref.shape[0]
    keep, recv = keep_ref[...], recv_ref[:rows]
    for src, first, second, dst in ((img_ref, keep, recv, img_out), (txt_ref, recv, keep, txt_out)):
        g = jnp.where(low, first, second) * f32(sharpness / (2.0 * batch))
        unit, factor = normalize(src[...])
        dst[...] = factor * (g - unit * jnp.sum(unit * g, axis=1, keepdims=True))
    loss_ref[...] = (share_ref[:1, :1] + recv_ref[rows : rows + 1, :1]) / (2.0 * batch)


def call(kernel, outs, **kw):
    return pl.pallas_call(
        kernel,
        out_shape=[o if isinstance(o, pl.MemoryRef) else jax.ShapeDtypeStruct(*o) for o in outs],
        compiler_params=pltpu.CompilerParams(vmem_limit_bytes=48 * 1024 * 1024),
        **kw,
    )


def exchange(x, axes):
    return lax.all_to_all(x, axes, 0, 0)


def swap(x):
    return lax.ppermute(x, "c", [(0, 1), (1, 0)])


def local(image_embed, text_embed, partner):
    rows, size = image_embed.shape
    n_plane = lax.axis_size("y") * lax.axis_size("x")
    n_line = lax.axis_size("z")
    batch = 2 * rows * n_plane * n_line
    image_core = lax.axis_index("c") == 0
    half = rows * (size // 128)
    packed = 2 * half + EXTRA
    tiles = n_plane * n_line * 4 * rows * rows // (128 * 128)

    args = [
        pltpu.with_memory_space_constraint(a, pltpu.HBM)
        for a in (image_embed, text_embed, partner.reshape(1, rows))
    ]
    pay, own_texts = call(
        start_kernel,
        [((n_plane, half + EXTRA, 128), bf16), ((half, 128), bf16)],
        in_specs=[pl.BlockSpec(memory_space=pl.ANY)] * 3,
        scratch_shapes=[
            pltpu.VMEM((rows, size), bf16),
            pltpu.VMEM((rows, size), bf16),
            pltpu.VMEM((1, rows), jnp.int32),
            pltpu.SemaphoreType.DMA((3,)),
        ],
    )(*args)
    own_images = exchange(pay, PLANE)
    here = call(functools.partial(chip_texts_kernel, rows), [((2 * half, 128), bf16)])(
        own_texts, swap(own_texts)
    )[0]

    def along(k):
        up = [(2 * z, 2 * ((z + k) % n_line)) for z in range(n_line)]
        down = [(2 * z + 1, 2 * ((z - k) % n_line) + 1) for z in range(n_line)]
        return lax.ppermute(here, ("z", "c"), up + down)

    far = along(n_line // 2)
    near = [along(k + 1) for k in range((n_line - 1) // 2)]
    own_images, far, *near = lax.optimization_barrier((own_images, far, *near))
    pieces = [here, far, *near, *[swap(p) for p in near]]
    off_images = swap(own_images)

    def sums(images, count, axes):
        low, high = (own_images, off_images) if images else (off_images, own_images)
        e, pay, match = call(
            functools.partial(scores_kernel, images, size),
            [
                pltpu.VMEM((tiles, 128, 128), bf16),
                ((count, 8, 128), f32),
                ((8, 128), f32),
            ],
            scratch_shapes=[pltpu.VMEM((n_line, 2 * half, 128), bf16)],
        )(low, high, *pieces)
        return e, match, jnp.sum(exchange(pay, axes), axis=0)

    e, match, mine = lax.cond(
        image_core,
        functools.partial(sums, True, n_plane, PLANE),
        functools.partial(sums, False, n_line, LINE),
    )
    other = swap(mine)

    def grads(images, count, axes):
        y = pieces if images else [off_images, own_images]
        kw = {}
        if images:
            kw["scratch_shapes"] = [pltpu.VMEM((n_line, 2 * half, 128), bf16)]
        pay = call(
            functools.partial(grads_kernel, images, size), [((count, packed, 128), bf16)], **kw
        )(e, match, mine, other, *y)[0]
        return call(
            functools.partial(sum_kernel, images),
            [((rows, size), f32), ((rows + 8, size), f32), ((8, 128), f32)],
        )(exchange(pay, axes))

    keep, send, share = lax.cond(
        image_core,
        functools.partial(grads, True, n_plane, PLANE),
        functools.partial(grads, False, n_line, LINE),
    )
    image_grad, text_grad, loss = call(
        functools.partial(output_kernel, batch),
        [((rows, size), f32), ((rows, size), f32), ((1, 1), f32)],
    )(image_embed, text_embed, keep, share, swap(send))
    return loss.reshape(()), image_grad, text_grad


def solution(mesh):
    shape = (mesh.shape["row"], 4, mesh.shape["col"] // 8, 2)
    fine = Mesh(mesh.devices.reshape(shape), ("z", "y", "x", "c"))
    by_image, by_text = P(("z", "y", "x", "c")), P(("y", "x", "c", "z"))
    return jax.shard_map(
        local,
        mesh=fine,
        in_specs=(by_image, by_text, by_image),
        out_specs=(P(), by_image, by_text),
        check_vma=False,
    )
```

```python
import functools
import math

import jax
import jax.numpy as jnp
from jax import lax
from jax.experimental import pallas as pl
from jax.experimental.pallas import tpu as pltpu
from jax.sharding import Mesh, PartitionSpec as P

sharpness = 1.0 / 0.07
f32 = jnp.float32
bf16 = jnp.bfloat16
NT = (((1,), (1,)), ((), ()))
PLANE, LINE = ("y", "x"), "z"
EXTRA = 16


def normalize(embed):
    flat = embed.astype(f32)
    factor = lax.rsqrt(jnp.sum(flat * flat, axis=1, keepdims=True) + 1e-06)
    return flat * factor, factor


def pack(dst, b, value):
    rows = value.shape[0]
    for k in range(value.shape[1] // 128):
        dst[b, k * rows : (k + 1) * rows, :] = value[:, k * 128 : (k + 1) * 128]


def unpack(ref, first, count, rows, width):
    return jnp.concatenate(
        [
            ref[first : first + count, k * rows : (k + 1) * rows, :].reshape(count * rows, 128)
            for k in range(width // 128)
        ],
        axis=1,
    )


def rows_tile(values):
    row = lax.broadcasted_iota(jnp.int32, (EXTRA, 128), 0)
    tile = jnp.zeros((EXTRA, 128), f32)
    for i, v in enumerate(values):
        tile = jnp.where(row == i, v, tile)
    return tile.astype(bf16)


LEVELS = 32760.0


def encode(value):
    most = jnp.max(jnp.abs(value), axis=0, keepdims=True)
    t = jnp.ceil(f32(8.0) * jnp.log2(jnp.maximum(most, f32(1e-30))) + f32(0.01))
    scaled = value * (f32(LEVELS) * jnp.exp2(t * f32(-0.125)))
    return jnp.floor(scaled + f32(0.5)).astype(jnp.int32), t.astype(jnp.int32)


def start_kernel(img_hbm, txt_hbm, partner_hbm, keep_ref, send_ref, img, txt, partner, sems):
    copies = [
        pltpu.make_async_copy(src, dst, sems.at[i])
        for i, (src, dst) in enumerate(((img_hbm, img), (txt_hbm, txt), (partner_hbm, partner)))
    ]
    for c in copies:
        c.start()
    for c in copies:
        c.wait()
    image_core = lax.axis_index("c") == 0
    half, size = img.shape
    a, b = img[...].astype(f32), txt[...].astype(f32)
    keep_ref[:half] = jnp.where(image_core, a, b).astype(bf16)
    send_ref[:half] = jnp.where(image_core, b, a).astype(bf16)
    p = jnp.concatenate([partner[...]] * (128 // half), axis=1)
    hi = p // 128
    tile = rows_tile([hi.astype(f32), (p - hi * 128).astype(f32)])
    for dst in (keep_ref, send_ref):
        dst[half:] = jnp.zeros((EXTRA, size), bf16)
        dst[half:, :128] = tile


def prep_kernel(images, first, second, out):
    half = first.shape[0] - EXTRA
    unit = [normalize(src[:half, :])[0] for src in (first, second)]
    unit = jnp.concatenate(unit, axis=0).astype(bf16)
    size = unit.size // 128
    tile = jnp.zeros((EXTRA, 128), bf16)
    if images:
        lane = lax.broadcasted_iota(jnp.int32, (EXTRA, 128), 1)
        a, b = (src[half:, :128].astype(f32) for src in (first, second))
        tile = jnp.where(lane // half % 2 == 0, a, b).astype(bf16)
    for b in range(out.shape[0]):
        pack(out, b, unit)
        out[b, size:, :] = tile


def place(images, tiles, r, t, ny):
    per_half = tiles // 2
    half, tile = divmod(r * ny + t, per_half)
    if not images:
        half = 1 - half
    return half * (per_half // 2) + tile // 2, slice(tile % 2 * 128, tile % 2 * 128 + 128)


def scores_kernel(images, rows, x_ref, y_ref, e_ref, pay_ref, match_ref, *scratch):
    packed = x_ref.shape[1]
    width = (packed - EXTRA) // rows * 128
    per, half = 128 // rows, rows // 2
    texts = x_ref.shape[0] // 2
    nx, ny = x_ref.shape[0] // per, y_ref.shape[0] // per
    if images:
        ny = texts // per
    else:
        nx = texts // per
    lane = lax.broadcasted_iota(jnp.int32, (1, 128), 1)
    chip = lax.axis_index("y") * lax.axis_size("x") + lax.axis_index("x")
    tail = (x_ref if images else y_ref)[:, packed - EXTRA :, :].astype(f32)
    partner = tail[:, 0, :] * 128.0 + tail[:, 1, :]

    def partners(t):
        p = partner[per * t : per * t + 1]
        for q in range(1, per):
            p = jnp.where(lane >= q * rows, partner[per * t + q : per * t + q + 1], p)
        return p

    def ids(t):
        i = (lane % rows) // half * (texts * half) + (per * t + lane // rows) * half
        return (chip * (texts * rows) + i + lane % half).astype(f32)

    xs, ys = (partners, ids) if images else (ids, partners)
    xs_ref, ys_ref, *s_refs = scratch
    for r in range(nx):
        xs_ref[r : r + 1] = xs(r)
    for t in range(ny):
        ys_ref[t : t + 1] = ys(t)
    part = nx // 2

    def product(h):
        x = unpack(x_ref, h * part * per, part * per, rows, width)
        y = unpack(y_ref, 0, ny * per, rows, width)
        s = lax.dot_general(x, y, NT, preferred_element_type=f32)
        for r in range(part):
            for t in range(ny):
                s_refs[h][r * ny + t] = s[r * 128 : (r + 1) * 128, t * 128 : (t + 1) * 128]

    def weigh(h):
        for r in range(h * part, (h + 1) * part):
            own = jnp.broadcast_to(xs_ref[r : r + 1], (128, 128)).T
            lanes = jnp.zeros((128, 128), f32)
            found = jnp.zeros((128, 128), f32)
            for t in range(ny):
                e = jnp.exp2(s_refs[h][(r - h * part) * ny + t] * f32(sharpness * math.log2(math.e)))
                matched = jnp.where(own == ys_ref[t : t + 1], e, f32(0.0))
                lanes += e
                found += matched
                block, at = place(images, nx * ny, r, t, ny)
                e_ref[block, at] = (e - f32(2.0) * matched).astype(bf16)
            pay_ref[0, r : r + 1] = jnp.sum(lanes.T, axis=0, keepdims=True)
            match_ref[r : r + 1] = jnp.sum(found.T, axis=0, keepdims=True)

    once = jnp.minimum(lax.axis_index("c") + 1, 1)
    product(0)

    def first(i, carry):
        product(1)
        weigh(0)
        return carry

    def second(i, carry):
        weigh(1)
        return carry

    lax.fori_loop(0, once, first, 0)
    lax.fori_loop(0, once, second, 0)
    if not images:
        m = match_ref[:nx]
        logs = jnp.where(m > 0.0, jnp.log(jnp.where(m > 0.0, m, f32(1.0))), f32(0.0))
        logs = jnp.sum(jnp.sum(logs, axis=0, keepdims=True), axis=1, keepdims=True)
        pay_ref[0, nx:] = jnp.broadcast_to(logs, (8 - nx, 128))
        match_ref[nx:] = jnp.zeros((8 - nx, 128), f32)
    for b in range(1, pay_ref.shape[0]):
        pay_ref[b] = pay_ref[0]


def grads_kernel(images, rows, y_ref, e_ref, match_ref, mine_ref, other_ref, out_ref):
    blocks, packed, _ = out_ref.shape
    width = (packed - EXTRA) // rows * 128
    per = 128 // rows
    nx = blocks // per
    ny = e_ref.shape[0] * 2 // nx
    col_total = other_ref[:ny]
    col_inv = f32(1.0) / col_total
    share = jnp.sum(jnp.log(col_total), axis=0, keepdims=True)
    share = jnp.broadcast_to(jnp.sum(share, axis=1, keepdims=True), (1, 128))
    if images:
        share -= 2.0 * other_ref[ny : ny + 1]
    whole = jnp.floor(share + f32(0.5))
    share = [whole.astype(jnp.int32), ((share - whole) * f32(32768.0)).astype(jnp.int32)]
    rest = [jnp.zeros((EXTRA - 2 - width // 128, 128), jnp.int32)]
    row_inv = f32(1.0) / mine_ref[:nx]
    y = unpack(y_ref, 0, ny * per, rows, width)
    ds = []
    for r in range(nx):
        ri = jnp.broadcast_to(row_inv[r : r + 1], (128, 128)).T
        matched = jnp.broadcast_to(match_ref[r : r + 1], (128, 128)).T
        d = []
        for t in range(ny):
            block, at = place(images, nx * ny, r, t, ny)
            e = e_ref[block, at].astype(f32)
            weight = ri + col_inv[t : t + 1]
            v = jnp.where(e < 0.0, matched * weight - f32(2.0), e * weight)
            d.append(v.astype(bf16))
        ds.append(jnp.concatenate(d, axis=1))
    g = jnp.dot(jnp.concatenate(ds, axis=0), y, preferred_element_type=f32)
    for b in range(blocks):
        steps = []
        for k in range(width // 128):
            q, t = encode(g[b * rows : (b + 1) * rows, k * 128 : (k + 1) * 128])
            out_ref[b, k * rows : (k + 1) * rows, :] = q.astype(jnp.int16)
            steps.append(t)
        tile = jnp.concatenate(steps + share + rest, axis=0)
        out_ref[b, packed - EXTRA :, :] = tile.astype(jnp.int16)


def finish_kernel(scale, keep_first, first, second, parts, keep_ref, send_ref, share_ref):
    half, size = keep_ref.shape
    rows = 2 * half
    body = rows * (size // 128)
    chunks = size // 128
    tail = parts[:, body:, :].astype(jnp.int32).astype(f32)
    step = jnp.exp2(tail[:, :chunks] * f32(0.125)) * f32(scale / LEVELS)
    total = []
    for k in range(chunks):
        piece = None
        for b in range(parts.shape[0]):
            q = parts[b, k * rows : (k + 1) * rows, :].astype(jnp.int32).astype(f32)
            q = q * step[b, k : k + 1]
            piece = q if piece is None else piece + q
        total.append(piece)
    total = jnp.concatenate(total, axis=1)
    grads = []
    for i, src in enumerate((first, second)):
        unit, factor = normalize(src[:half, :])
        g = total[i * half : (i + 1) * half]
        grads.append(factor * (g - unit * jnp.sum(unit * g, axis=1, keepdims=True)))
    keep, send = grads if keep_first else grads[::-1]
    keep_ref[...] = keep
    send_ref[:half] = send
    share = jnp.sum(tail[:, chunks : chunks + 1], axis=0)
    share += jnp.sum(tail[:, chunks + 1 : chunks + 2], axis=0) * f32(1.0 / 32768.0)
    share_ref[...] = jnp.broadcast_to(share, share_ref.shape)
    send_ref[half:] = jnp.broadcast_to(share[:, :1], (send_ref.shape[0] - half, size))


def output_kernel(batch, keep_ref, share_ref, recv_ref, img_ref, txt_ref, loss_ref):
    image_core = lax.axis_index("c") == 0
    half = keep_ref.shape[0]
    keep, recv = keep_ref[...], recv_ref[:half]
    img_ref[...] = jnp.where(image_core, keep, recv)
    txt_ref[...] = jnp.where(image_core, recv, keep)
    loss_ref[...] = (share_ref[:1, :1] + recv_ref[half : half + 1, :1]) / (2.0 * batch)


def call(kernel, outs, **kw):
    return pl.pallas_call(
        kernel,
        out_shape=[jax.ShapeDtypeStruct(*o) for o in outs],
        compiler_params=pltpu.CompilerParams(vmem_limit_bytes=48 * 1024 * 1024),
        **kw,
    )


def exchange(x, axes):
    return lax.all_to_all(x, axes, 0, 0)


def swap(x):
    return lax.ppermute(x, "c", [(0, 1), (1, 0)])


def local(image_embed, text_embed, partner):
    half, size = image_embed.shape
    rows = 2 * half
    n_plane = lax.axis_size("y") * lax.axis_size("x")
    n_line = lax.axis_size("z")
    batch = rows * n_plane * n_line
    image_core = lax.axis_index("c") == 0
    packed = rows * (size // 128) + EXTRA
    tiles = n_plane * n_line * rows * rows // (128 * 128)

    args = [
        pltpu.with_memory_space_constraint(a, pltpu.HBM)
        for a in (image_embed, text_embed, partner.reshape(1, half))
    ]
    own, send = call(
        start_kernel,
        [((half + EXTRA, size), bf16)] * 2,
        in_specs=[pl.BlockSpec(memory_space=pl.ANY)] * 3,
        scratch_shapes=[
            pltpu.VMEM((half, size), bf16),
            pltpu.VMEM((half, size), bf16),
            pltpu.VMEM((1, half), jnp.int32),
            pltpu.SemaphoreType.DMA((3,)),
        ],
    )(*args)
    off = swap(send)

    def gather_images():
        kernel = functools.partial(prep_kernel, True)
        return exchange(call(kernel, [((n_plane, packed, 128), bf16)])(own, off)[0], PLANE)

    def gather_texts():
        kernel = functools.partial(prep_kernel, False)
        every = exchange(call(kernel, [((n_line, packed, 128), bf16)])(off, own)[0], LINE)
        return jnp.pad(every, ((0, n_plane - n_line), (0, 0), (0, 0)))

    x = lax.cond(image_core, gather_images, gather_texts)
    y = swap(x)

    def sums(images, count, axes):
        e, pay, match = call(
            functools.partial(scores_kernel, images, rows),
            [((n_plane, packed, 128), bf16), ((count, 8, 128), f32), ((8, 128), f32)],
            input_output_aliases={0: 0},
            scratch_shapes=[pltpu.VMEM((8, 128), f32)] * 2
            + [pltpu.VMEM((tiles // 2, 128, 128), f32)] * 2,
        )(x, y)
        return e, match, jnp.sum(exchange(pay, axes), axis=0)

    e, match, mine = lax.cond(
        image_core,
        functools.partial(sums, True, n_plane, PLANE),
        functools.partial(sums, False, n_line, LINE),
    )
    other = swap(mine)

    def grads(images, count, axes):
        pay = call(
            functools.partial(grads_kernel, images, rows),
            [((count, packed, 128), jnp.int16)],
        )(y, e, match, mine, other)[0]
        return call(
            functools.partial(finish_kernel, sharpness / (2.0 * batch), images),
            [((half, size), f32), ((half + 8, size), f32), ((8, 128), f32)],
        )(*((own, off) if images else (off, own)), exchange(pay, axes))

    keep, send, share = lax.cond(
        image_core,
        functools.partial(grads, True, n_plane, PLANE),
        functools.partial(grads, False, n_line, LINE),
    )
    image_grad, text_grad, loss = call(
        functools.partial(output_kernel, batch),
        [((half, size), f32), ((half, size), f32), ((1, 1), f32)],
    )(keep, share, swap(send))
    return loss.reshape(()), image_grad, text_grad


def solution(mesh):
    shape = (mesh.shape["row"], 4, mesh.shape["col"] // 8, 2)
    fine = Mesh(mesh.devices.reshape(shape), ("z", "y", "x", "c"))
    by_image, by_text = P(("z", "y", "x", "c")), P(("y", "x", "c", "z"))
    return jax.shard_map(
        local,
        mesh=fine,
        in_specs=(by_image, by_text, by_image),
        out_specs=(P(), by_image, by_text),
        check_vma=False,
    )
```

```python
import functools
import math

import jax
import jax.numpy as jnp
from jax import lax
from jax.experimental import pallas as pl
from jax.experimental.pallas import tpu as pltpu
from jax.sharding import Mesh, PartitionSpec as P

sharpness = 1.0 / 0.07
f32 = jnp.float32
bf16 = jnp.bfloat16
NT = (((1,), (1,)), ((), ()))
PLANE, LINE = ("y", "x"), "z"
EXTRA = 16


def normalize(embed):
    flat = embed.astype(f32)
    factor = lax.rsqrt(jnp.sum(flat * flat, axis=1, keepdims=True) + 1e-06)
    return flat * factor, factor


def pack(dst, b, value):
    rows = value.shape[0]
    for k in range(value.shape[1] // 128):
        dst[b, k * rows : (k + 1) * rows, :] = value[:, k * 128 : (k + 1) * 128]


def unpack(ref, first, count, rows, width):
    return jnp.concatenate(
        [
            ref[first : first + count, k * rows : (k + 1) * rows, :].reshape(count * rows, 128)
            for k in range(width // 128)
        ],
        axis=1,
    )


def rows_tile(values):
    row = lax.broadcasted_iota(jnp.int32, (EXTRA, 128), 0)
    tile = jnp.zeros((EXTRA, 128), f32)
    for i, v in enumerate(values):
        tile = jnp.where(row == i, v, tile)
    return tile.astype(bf16)


LEVELS = 32760.0


def encode(value):
    most = jnp.max(jnp.abs(value), axis=0, keepdims=True)
    t = jnp.ceil(f32(8.0) * jnp.log2(jnp.maximum(most, f32(1e-30))) + f32(0.01))
    scaled = value * (f32(LEVELS) * jnp.exp2(t * f32(-0.125)))
    return jnp.round(scaled).astype(jnp.int32), t.astype(jnp.int32)


def start_kernel(img_hbm, txt_hbm, partner_hbm, keep_ref, send_ref, img, txt, partner, sems):
    copies = [
        pltpu.make_async_copy(src, dst, sems.at[i])
        for i, (src, dst) in enumerate(((img_hbm, img), (txt_hbm, txt), (partner_hbm, partner)))
    ]
    for c in copies:
        c.start()
    for c in copies:
        c.wait()
    image_core = lax.axis_index("c") == 0
    half, size = img.shape
    a, b = img[...].astype(f32), txt[...].astype(f32)
    keep_ref[:half] = jnp.where(image_core, a, b).astype(bf16)
    send_ref[:half] = jnp.where(image_core, b, a).astype(bf16)
    p = jnp.concatenate([partner[...]] * (128 // half), axis=1)
    hi = p // 128
    tile = rows_tile([hi.astype(f32), (p - hi * 128).astype(f32)])
    for dst in (keep_ref, send_ref):
        dst[half:] = jnp.zeros((EXTRA, size), bf16)
        dst[half:, :128] = tile


def prep_kernel(images, first, second, out):
    half = first.shape[0] - EXTRA
    unit = [normalize(src[:half, :])[0] for src in (first, second)]
    unit = jnp.concatenate(unit, axis=0).astype(bf16)
    size = unit.size // 128
    tile = jnp.zeros((EXTRA, 128), bf16)
    if images:
        lane = lax.broadcasted_iota(jnp.int32, (EXTRA, 128), 1)
        a, b = (src[half:, :128].astype(f32) for src in (first, second))
        tile = jnp.where(lane // half % 2 == 0, a, b).astype(bf16)
    for b in range(out.shape[0]):
        pack(out, b, unit)
        out[b, size:, :] = tile


def place(images, tiles, r, t, ny):
    per_half = tiles // 2
    half, tile = divmod(r * ny + t, per_half)
    if not images:
        half = 1 - half
    return half * (per_half // 2) + tile // 2, slice(tile % 2 * 128, tile % 2 * 128 + 128)


def scores_kernel(images, rows, x_ref, y_ref, e_ref, pay_ref, match_ref, *scratch):
    packed = x_ref.shape[1]
    width = (packed - EXTRA) // rows * 128
    per, half = 128 // rows, rows // 2
    texts = x_ref.shape[0] // 2
    nx, ny = x_ref.shape[0] // per, y_ref.shape[0] // per
    if images:
        ny = texts // per
    else:
        nx = texts // per
    lane = lax.broadcasted_iota(jnp.int32, (1, 128), 1)
    chip = lax.axis_index("y") * lax.axis_size("x") + lax.axis_index("x")
    tail = (x_ref if images else y_ref)[:, packed - EXTRA :, :].astype(f32)
    partner = tail[:, 0, :] * 128.0 + tail[:, 1, :]

    def partners(t):
        p = partner[per * t : per * t + 1]
        for q in range(1, per):
            p = jnp.where(lane >= q * rows, partner[per * t + q : per * t + q + 1], p)
        return p

    def ids(t):
        i = (lane % rows) // half * (texts * half) + (per * t + lane // rows) * half
        return (chip * (texts * rows) + i + lane % half).astype(f32)

    xs, ys = (partners, ids) if images else (ids, partners)
    xs_ref, ys_ref, *s_refs = scratch
    for r in range(nx):
        xs_ref[r : r + 1] = xs(r)
    for t in range(ny):
        ys_ref[t : t + 1] = ys(t)
    part = nx // 2

    def product(h):
        x = unpack(x_ref, h * part * per, part * per, rows, width)
        y = unpack(y_ref, 0, ny * per, rows, width)
        s = lax.dot_general(x, y, NT, preferred_element_type=f32)
        for r in range(part):
            for t in range(ny):
                s_refs[h][r * ny + t] = s[r * 128 : (r + 1) * 128, t * 128 : (t + 1) * 128]

    def weigh(h):
        for r in range(h * part, (h + 1) * part):
            own = jnp.broadcast_to(xs_ref[r : r + 1], (128, 128)).T
            lanes = jnp.zeros((128, 128), f32)
            found = jnp.zeros((128, 128), f32)
            for t in range(ny):
                e = jnp.exp2(s_refs[h][(r - h * part) * ny + t] * f32(sharpness * math.log2(math.e)))
                matched = jnp.where(own == ys_ref[t : t + 1], e, f32(0.0))
                lanes += e
                found += matched
                block, at = place(images, nx * ny, r, t, ny)
                e_ref[block, at] = (e - f32(2.0) * matched).astype(bf16)
            pay_ref[0, r : r + 1] = jnp.sum(lanes.T, axis=0, keepdims=True)
            match_ref[r : r + 1] = jnp.sum(found.T, axis=0, keepdims=True)

    once = jnp.minimum(lax.axis_index("c") + 1, 1)
    product(0)

    def first(i, carry):
        product(1)
        weigh(0)
        return carry

    def second(i, carry):
        weigh(1)
        return carry

    lax.fori_loop(0, once, first, 0)
    lax.fori_loop(0, once, second, 0)
    if not images:
        m = match_ref[:nx]
        logs = jnp.where(m > 0.0, jnp.log(jnp.where(m > 0.0, m, f32(1.0))), f32(0.0))
        logs = jnp.sum(jnp.sum(logs, axis=0, keepdims=True), axis=1, keepdims=True)
        pay_ref[0, nx:] = jnp.broadcast_to(logs, (8 - nx, 128))
        match_ref[nx:] = jnp.zeros((8 - nx, 128), f32)
    for b in range(1, pay_ref.shape[0]):
        pay_ref[b] = pay_ref[0]


def grads_kernel(images, rows, y_ref, e_ref, match_ref, mine_ref, other_ref, out_ref):
    blocks, packed, _ = out_ref.shape
    width = (packed - EXTRA) // rows * 128
    per = 128 // rows
    nx = blocks // per
    ny = e_ref.shape[0] * 2 // nx
    col_total = other_ref[:ny]
    col_inv = f32(1.0) / col_total
    share = jnp.sum(jnp.log(col_total), axis=0, keepdims=True)
    share = jnp.broadcast_to(jnp.sum(share, axis=1, keepdims=True), (1, 128))
    if images:
        share -= 2.0 * other_ref[ny : ny + 1]
    whole = jnp.floor(share + f32(0.5))
    share = [whole.astype(jnp.int32), ((share - whole) * f32(32768.0)).astype(jnp.int32)]
    rest = [jnp.zeros((EXTRA - 2 - width // 128, 128), jnp.int32)]
    row_inv = f32(1.0) / mine_ref[:nx]
    y = unpack(y_ref, 0, ny * per, rows, width)
    ds = []
    for r in range(nx):
        ri = jnp.broadcast_to(row_inv[r : r + 1], (128, 128)).T
        matched = jnp.broadcast_to(match_ref[r : r + 1], (128, 128)).T
        d = []
        for t in range(ny):
            block, at = place(images, nx * ny, r, t, ny)
            e = e_ref[block, at].astype(f32)
            weight = ri + col_inv[t : t + 1]
            v = jnp.where(e < 0.0, matched * weight - f32(2.0), e * weight)
            d.append(v.astype(bf16))
        ds.append(jnp.concatenate(d, axis=1))
    g = jnp.dot(jnp.concatenate(ds, axis=0), y, preferred_element_type=f32)
    for b in range(blocks):
        steps = []
        for k in range(width // 128):
            q, t = encode(g[b * rows : (b + 1) * rows, k * 128 : (k + 1) * 128])
            out_ref[b, k * rows : (k + 1) * rows, :] = q.astype(jnp.int16)
            steps.append(t)
        tile = jnp.concatenate(steps + share + rest, axis=0)
        out_ref[b, packed - EXTRA :, :] = tile.astype(jnp.int16)


def finish_kernel(scale, keep_first, first, second, parts, keep_ref, send_ref, share_ref):
    half, size = keep_ref.shape
    rows = 2 * half
    body = rows * (size // 128)
    chunks = size // 128
    tail = parts[:, body:, :].astype(jnp.int32).astype(f32)
    step = jnp.exp2(tail[:, :chunks] * f32(0.125)) * f32(scale / LEVELS)
    total = []
    for k in range(chunks):
        piece = None
        for b in range(parts.shape[0]):
            q = parts[b, k * rows : (k + 1) * rows, :].astype(jnp.int32).astype(f32)
            q = q * step[b, k : k + 1]
            piece = q if piece is None else piece + q
        total.append(piece)
    total = jnp.concatenate(total, axis=1)
    grads = []
    for i, src in enumerate((first, second)):
        unit, factor = normalize(src[:half, :])
        g = total[i * half : (i + 1) * half]
        grads.append(factor * (g - unit * jnp.sum(unit * g, axis=1, keepdims=True)))
    keep, send = grads if keep_first else grads[::-1]
    keep_ref[...] = keep
    send_ref[:half] = send
    share = jnp.sum(tail[:, chunks : chunks + 1], axis=0)
    share += jnp.sum(tail[:, chunks + 1 : chunks + 2], axis=0) * f32(1.0 / 32768.0)
    share_ref[...] = jnp.broadcast_to(share, share_ref.shape)
    send_ref[half:] = jnp.broadcast_to(share[:, :1], (send_ref.shape[0] - half, size))


def output_kernel(batch, keep_ref, share_ref, recv_ref, img_ref, txt_ref, loss_ref):
    image_core = lax.axis_index("c") == 0
    half = keep_ref.shape[0]
    keep, recv = keep_ref[...], recv_ref[:half]
    img_ref[...] = jnp.where(image_core, keep, recv)
    txt_ref[...] = jnp.where(image_core, recv, keep)
    loss_ref[...] = (share_ref[:1, :1] + recv_ref[half : half + 1, :1]) / (2.0 * batch)


def call(kernel, outs, **kw):
    return pl.pallas_call(
        kernel,
        out_shape=[jax.ShapeDtypeStruct(*o) for o in outs],
        compiler_params=pltpu.CompilerParams(vmem_limit_bytes=48 * 1024 * 1024),
        **kw,
    )


def exchange(x, axes):
    return lax.all_to_all(x, axes, 0, 0)


def swap(x):
    return lax.ppermute(x, "c", [(0, 1), (1, 0)])


def local(image_embed, text_embed, partner):
    half, size = image_embed.shape
    rows = 2 * half
    n_plane = lax.axis_size("y") * lax.axis_size("x")
    n_line = lax.axis_size("z")
    batch = rows * n_plane * n_line
    image_core = lax.axis_index("c") == 0
    packed = rows * (size // 128) + EXTRA
    tiles = n_plane * n_line * rows * rows // (128 * 128)

    args = [
        pltpu.with_memory_space_constraint(a, pltpu.HBM)
        for a in (image_embed, text_embed, partner.reshape(1, half))
    ]
    own, send = call(
        start_kernel,
        [((half + EXTRA, size), bf16)] * 2,
        in_specs=[pl.BlockSpec(memory_space=pl.ANY)] * 3,
        scratch_shapes=[
            pltpu.VMEM((half, size), bf16),
            pltpu.VMEM((half, size), bf16),
            pltpu.VMEM((1, half), jnp.int32),
            pltpu.SemaphoreType.DMA((3,)),
        ],
    )(*args)
    off = swap(send)

    def gather_images():
        kernel = functools.partial(prep_kernel, True)
        return exchange(call(kernel, [((n_plane, packed, 128), bf16)])(own, off)[0], PLANE)

    def gather_texts():
        kernel = functools.partial(prep_kernel, False)
        every = exchange(call(kernel, [((n_line, packed, 128), bf16)])(off, own)[0], LINE)
        return jnp.pad(every, ((0, n_plane - n_line), (0, 0), (0, 0)))

    x = lax.cond(image_core, gather_images, gather_texts)
    y = swap(x)

    def sums(images, count, axes):
        e, pay, match = call(
            functools.partial(scores_kernel, images, rows),
            [((n_plane, packed, 128), bf16), ((count, 8, 128), f32), ((8, 128), f32)],
            input_output_aliases={0: 0},
            scratch_shapes=[pltpu.VMEM((8, 128), f32)] * 2
            + [pltpu.VMEM((tiles // 2, 128, 128), f32)] * 2,
        )(x, y)
        return e, match, jnp.sum(exchange(pay, axes), axis=0)

    e, match, mine = lax.cond(
        image_core,
        functools.partial(sums, True, n_plane, PLANE),
        functools.partial(sums, False, n_line, LINE),
    )
    other = swap(mine)

    def grads(images, count, axes):
        pay = call(
            functools.partial(grads_kernel, images, rows),
            [((count, packed, 128), jnp.int16)],
        )(y, e, match, mine, other)[0]
        return call(
            functools.partial(finish_kernel, sharpness / (2.0 * batch), images),
            [((half, size), f32), ((half + 8, size), f32), ((8, 128), f32)],
        )(*((own, off) if images else (off, own)), exchange(pay, axes))

    keep, send, share = lax.cond(
        image_core,
        functools.partial(grads, True, n_plane, PLANE),
        functools.partial(grads, False, n_line, LINE),
    )
    image_grad, text_grad, loss = call(
        functools.partial(output_kernel, batch),
        [((half, size), f32), ((half, size), f32), ((1, 1), f32)],
    )(keep, share, swap(send))
    return loss.reshape(()), image_grad, text_grad


def solution(mesh):
    shape = (mesh.shape["row"], 4, mesh.shape["col"] // 8, 2)
    fine = Mesh(mesh.devices.reshape(shape), ("z", "y", "x", "c"))
    by_image, by_text = P(("z", "y", "x", "c")), P(("y", "x", "c", "z"))
    return jax.shard_map(
        local,
        mesh=fine,
        in_specs=(by_image, by_text, by_image),
        out_specs=(P(), by_image, by_text),
        check_vma=False,
    )
```

```python
import functools
import math

import jax
import jax.numpy as jnp
from jax import lax
from jax.experimental import pallas as pl
from jax.experimental.pallas import tpu as pltpu
from jax.sharding import Mesh, PartitionSpec as P

sharpness = 1.0 / 0.07
f32 = jnp.float32
bf16 = jnp.bfloat16
NT = (((1,), (1,)), ((), ()))
PLANE, LINE = ("y", "x"), "z"
EXTRA = 16


def normalize(embed):
    flat = embed.astype(f32)
    factor = lax.rsqrt(jnp.sum(flat * flat, axis=1, keepdims=True) + 1e-06)
    return flat * factor, factor


def pack(dst, b, value):
    rows = value.shape[0]
    for k in range(value.shape[1] // 128):
        dst[b, k * rows : (k + 1) * rows, :] = value[:, k * 128 : (k + 1) * 128]


def unpack(ref, first, count, rows, width):
    return jnp.concatenate(
        [
            ref[first : first + count, k * rows : (k + 1) * rows, :].reshape(count * rows, 128)
            for k in range(width // 128)
        ],
        axis=1,
    )


def rows_tile(values):
    row = lax.broadcasted_iota(jnp.int32, (EXTRA, 128), 0)
    tile = jnp.zeros((EXTRA, 128), f32)
    for i, v in enumerate(values):
        tile = jnp.where(row == i, v, tile)
    return tile.astype(bf16)


LEVELS = 32760.0


def encode(value):
    most = jnp.max(jnp.abs(value), axis=0, keepdims=True)
    t = jnp.ceil(f32(8.0) * jnp.log2(jnp.maximum(most, f32(1e-30))) + f32(0.01))
    scaled = value * (f32(LEVELS) * jnp.exp2(t * f32(-0.125)))
    return jnp.round(scaled).astype(jnp.int32), t.astype(jnp.int32)


def start_kernel(img_hbm, txt_hbm, partner_hbm, keep_ref, send_ref, img, txt, partner, sems):
    copies = [
        pltpu.make_async_copy(src, dst, sems.at[i])
        for i, (src, dst) in enumerate(((img_hbm, img), (txt_hbm, txt), (partner_hbm, partner)))
    ]
    for c in copies:
        c.start()
    for c in copies:
        c.wait()
    image_core = lax.axis_index("c") == 0
    half, size = img.shape
    a, b = img[...].astype(f32), txt[...].astype(f32)
    keep_ref[:half] = jnp.where(image_core, a, b).astype(bf16)
    send_ref[:half] = jnp.where(image_core, b, a).astype(bf16)
    p = jnp.concatenate([partner[...]] * (128 // half), axis=1)
    hi = p // 128
    tile = rows_tile([hi.astype(f32), (p - hi * 128).astype(f32)])
    for dst in (keep_ref, send_ref):
        dst[half:] = jnp.zeros((EXTRA, size), bf16)
        dst[half:, :128] = tile


def prep_kernel(images, first, second, out):
    half = first.shape[0] - EXTRA
    unit = [normalize(src[:half, :])[0] for src in (first, second)]
    unit = jnp.concatenate(unit, axis=0).astype(bf16)
    size = unit.size // 128
    tile = jnp.zeros((EXTRA, 128), bf16)
    if images:
        lane = lax.broadcasted_iota(jnp.int32, (EXTRA, 128), 1)
        a, b = (src[half:, :128].astype(f32) for src in (first, second))
        tile = jnp.where(lane // half % 2 == 0, a, b).astype(bf16)
    for b in range(out.shape[0]):
        pack(out, b, unit)
        out[b, size:, :] = tile


def place(images, tiles, r, t, ny):
    per_half = tiles // 2
    half, tile = divmod(r * ny + t, per_half)
    if not images:
        half = 1 - half
    return half * (per_half // 2) + tile // 2, slice(tile % 2 * 128, tile % 2 * 128 + 128)


def scores_kernel(images, rows, x_ref, y_ref, e_ref, pay_ref, match_ref, *scratch):
    packed = x_ref.shape[1]
    width = (packed - EXTRA) // rows * 128
    per, half = 128 // rows, rows // 2
    texts = x_ref.shape[0] // 2
    nx, ny = x_ref.shape[0] // per, y_ref.shape[0] // per
    if images:
        ny = texts // per
    else:
        nx = texts // per
    lane = lax.broadcasted_iota(jnp.int32, (1, 128), 1)
    chip = lax.axis_index("y") * lax.axis_size("x") + lax.axis_index("x")
    tail = (x_ref if images else y_ref)[:, packed - EXTRA :, :].astype(f32)
    partner = tail[:, 0, :] * 128.0 + tail[:, 1, :]

    def partners(t):
        p = partner[per * t : per * t + 1]
        for q in range(1, per):
            p = jnp.where(lane >= q * rows, partner[per * t + q : per * t + q + 1], p)
        return p

    def ids(t):
        i = (lane % rows) // half * (texts * half) + (per * t + lane // rows) * half
        return (chip * (texts * rows) + i + lane % half).astype(f32)

    xs, ys = (partners, ids) if images else (ids, partners)
    xs_ref, ys_ref, *s_refs = scratch
    for r in range(nx):
        xs_ref[r : r + 1] = xs(r)
    for t in range(ny):
        ys_ref[t : t + 1] = ys(t)
    part = nx // 2

    def product(h):
        x = unpack(x_ref, h * part * per, part * per, rows, width)
        y = unpack(y_ref, 0, ny * per, rows, width)
        s = lax.dot_general(x, y, NT, preferred_element_type=f32)
        for r in range(part):
            for t in range(ny):
                s_refs[h][r * ny + t] = s[r * 128 : (r + 1) * 128, t * 128 : (t + 1) * 128]

    def weigh(h):
        for r in range(h * part, (h + 1) * part):
            own = jnp.broadcast_to(xs_ref[r : r + 1], (128, 128)).T
            lanes = jnp.zeros((128, 128), f32)
            found = jnp.zeros((128, 128), f32)
            for t in range(ny):
                e = jnp.exp2(s_refs[h][(r - h * part) * ny + t] * f32(sharpness * math.log2(math.e)))
                matched = jnp.where(own == ys_ref[t : t + 1], e, f32(0.0))
                lanes += e
                found += matched
                block, at = place(images, nx * ny, r, t, ny)
                e_ref[block, at] = (e - f32(2.0) * matched).astype(bf16)
            pay_ref[0, r : r + 1] = jnp.sum(lanes.T, axis=0, keepdims=True)
            match_ref[r : r + 1] = jnp.sum(found.T, axis=0, keepdims=True)

    once = jnp.minimum(lax.axis_index("c") + 1, 1)
    product(0)

    def first(i, carry):
        product(1)
        weigh(0)
        return carry

    def second(i, carry):
        weigh(1)
        return carry

    lax.fori_loop(0, once, first, 0)
    lax.fori_loop(0, once, second, 0)
    if not images:
        m = match_ref[:nx]
        logs = jnp.where(m > 0.0, jnp.log(jnp.where(m > 0.0, m, f32(1.0))), f32(0.0))
        logs = jnp.sum(jnp.sum(logs, axis=0, keepdims=True), axis=1, keepdims=True)
        pay_ref[0, nx:] = jnp.broadcast_to(logs, (8 - nx, 128))
        match_ref[nx:] = jnp.zeros((8 - nx, 128), f32)
    for b in range(1, pay_ref.shape[0]):
        pay_ref[b] = pay_ref[0]


def grads_kernel(images, rows, y_ref, e_ref, match_ref, mine_ref, other_ref, out_ref):
    blocks, packed, _ = out_ref.shape
    width = (packed - EXTRA) // rows * 128
    per = 128 // rows
    nx = blocks // per
    ny = e_ref.shape[0] * 2 // nx
    col_total = other_ref[:ny]
    col_inv = f32(1.0) / col_total
    share = jnp.sum(jnp.log(col_total), axis=0, keepdims=True)
    share = jnp.broadcast_to(jnp.sum(share, axis=1, keepdims=True), (1, 128))
    if images:
        share -= 2.0 * other_ref[ny : ny + 1]
    whole = jnp.floor(share + f32(0.5))
    share = [whole.astype(jnp.int32), ((share - whole) * f32(32768.0)).astype(jnp.int32)]
    rest = [jnp.zeros((EXTRA - 2 - width // 128, 128), jnp.int32)]
    row_inv = f32(1.0) / mine_ref[:nx]
    y = unpack(y_ref, 0, ny * per, rows, width)
    gs = []
    ds = []
    for r in range(nx):
        ri = jnp.broadcast_to(row_inv[r : r + 1], (128, 128)).T
        matched = jnp.broadcast_to(match_ref[r : r + 1], (128, 128)).T
        d = []
        for t in range(ny):
            block, at = place(images, nx * ny, r, t, ny)
            e = e_ref[block, at].astype(f32)
            weight = ri + col_inv[t : t + 1]
            v = jnp.where(e < 0.0, matched * weight - f32(2.0), e * weight)
            d.append(v.astype(bf16))
        ds.append(jnp.concatenate(d, axis=1))
        if (r + 1) % (nx // 2) == 0:
            gs.append(jnp.dot(jnp.concatenate(ds, axis=0), y, preferred_element_type=f32))
            ds = []
    for b in range(blocks):
        steps = []
        for k in range(width // 128):
            q, t = encode(
                gs[b * 2 // blocks][
                    b % (blocks // 2) * rows : (b % (blocks // 2) + 1) * rows,
                    k * 128 : (k + 1) * 128,
                ]
            )
            out_ref[b, k * rows : (k + 1) * rows, :] = q.astype(jnp.int16)
            steps.append(t)
        tile = jnp.concatenate(steps + share + rest, axis=0)
        out_ref[b, packed - EXTRA :, :] = tile.astype(jnp.int16)


def finish_kernel(scale, keep_first, first, second, parts, keep_ref, send_ref, share_ref):
    half, size = keep_ref.shape
    rows = 2 * half
    body = rows * (size // 128)
    chunks = size // 128
    tail = parts[:, body:, :].astype(jnp.int32).astype(f32)
    step = jnp.exp2(tail[:, :chunks] * f32(0.125)) * f32(scale / LEVELS)
    total = []
    for k in range(chunks):
        piece = None
        for b in range(parts.shape[0]):
            q = parts[b, k * rows : (k + 1) * rows, :].astype(jnp.int32).astype(f32)
            q = q * step[b, k : k + 1]
            piece = q if piece is None else piece + q
        total.append(piece)
    total = jnp.concatenate(total, axis=1)
    grads = []
    for i, src in enumerate((first, second)):
        unit, factor = normalize(src[:half, :])
        g = total[i * half : (i + 1) * half]
        grads.append(factor * (g - unit * jnp.sum(unit * g, axis=1, keepdims=True)))
    keep, send = grads if keep_first else grads[::-1]
    keep_ref[...] = keep
    send_ref[:half] = send
    share = jnp.sum(tail[:, chunks : chunks + 1], axis=0)
    share += jnp.sum(tail[:, chunks + 1 : chunks + 2], axis=0) * f32(1.0 / 32768.0)
    share_ref[...] = jnp.broadcast_to(share, share_ref.shape)
    send_ref[half:] = jnp.broadcast_to(share[:, :1], (send_ref.shape[0] - half, size))


def output_kernel(batch, keep_ref, share_ref, recv_ref, img_ref, txt_ref, loss_ref):
    image_core = lax.axis_index("c") == 0
    half = keep_ref.shape[0]
    keep, recv = keep_ref[...], recv_ref[:half]
    img_ref[...] = jnp.where(image_core, keep, recv)
    txt_ref[...] = jnp.where(image_core, recv, keep)
    loss_ref[...] = (share_ref[:1, :1] + recv_ref[half : half + 1, :1]) / (2.0 * batch)


def call(kernel, outs, **kw):
    return pl.pallas_call(
        kernel,
        out_shape=[jax.ShapeDtypeStruct(*o) for o in outs],
        compiler_params=pltpu.CompilerParams(vmem_limit_bytes=48 * 1024 * 1024),
        **kw,
    )


def exchange(x, axes):
    return lax.all_to_all(x, axes, 0, 0)


def swap(x):
    return lax.ppermute(x, "c", [(0, 1), (1, 0)])


def local(image_embed, text_embed, partner):
    half, size = image_embed.shape
    rows = 2 * half
    n_plane = lax.axis_size("y") * lax.axis_size("x")
    n_line = lax.axis_size("z")
    batch = rows * n_plane * n_line
    image_core = lax.axis_index("c") == 0
    packed = rows * (size // 128) + EXTRA
    tiles = n_plane * n_line * rows * rows // (128 * 128)

    args = [
        pltpu.with_memory_space_constraint(a, pltpu.HBM)
        for a in (image_embed, text_embed, partner.reshape(1, half))
    ]
    own, send = call(
        start_kernel,
        [((half + EXTRA, size), bf16)] * 2,
        in_specs=[pl.BlockSpec(memory_space=pl.ANY)] * 3,
        scratch_shapes=[
            pltpu.VMEM((half, size), bf16),
            pltpu.VMEM((half, size), bf16),
            pltpu.VMEM((1, half), jnp.int32),
            pltpu.SemaphoreType.DMA((3,)),
        ],
    )(*args)
    off = swap(send)

    def gather_images():
        kernel = functools.partial(prep_kernel, True)
        return exchange(call(kernel, [((n_plane, packed, 128), bf16)])(own, off)[0], PLANE)

    def gather_texts():
        kernel = functools.partial(prep_kernel, False)
        every = exchange(call(kernel, [((n_line, packed, 128), bf16)])(off, own)[0], LINE)
        return jnp.pad(every, ((0, n_plane - n_line), (0, 0), (0, 0)))

    x = lax.cond(image_core, gather_images, gather_texts)
    y = swap(x)

    def sums(images, count, axes):
        e, pay, match = call(
            functools.partial(scores_kernel, images, rows),
            [((n_plane, packed, 128), bf16), ((count, 8, 128), f32), ((8, 128), f32)],
            input_output_aliases={0: 0},
            scratch_shapes=[pltpu.VMEM((8, 128), f32)] * 2
            + [pltpu.VMEM((tiles // 2, 128, 128), f32)] * 2,
        )(x, y)
        return e, match, jnp.sum(exchange(pay, axes), axis=0)

    e, match, mine = lax.cond(
        image_core,
        functools.partial(sums, True, n_plane, PLANE),
        functools.partial(sums, False, n_line, LINE),
    )
    other = swap(mine)

    def grads(images, count, axes):
        pay = call(
            functools.partial(grads_kernel, images, rows),
            [((count, packed, 128), jnp.int16)],
        )(y, e, match, mine, other)[0]
        return call(
            functools.partial(finish_kernel, sharpness / (2.0 * batch), images),
            [((half, size), f32), ((half + 8, size), f32), ((8, 128), f32)],
        )(*((own, off) if images else (off, own)), exchange(pay, axes))

    keep, send, share = lax.cond(
        image_core,
        functools.partial(grads, True, n_plane, PLANE),
        functools.partial(grads, False, n_line, LINE),
    )
    image_grad, text_grad, loss = call(
        functools.partial(output_kernel, batch),
        [((half, size), f32), ((half, size), f32), ((1, 1), f32)],
    )(keep, share, swap(send))
    return loss.reshape(()), image_grad, text_grad


def solution(mesh):
    shape = (mesh.shape["row"], 4, mesh.shape["col"] // 8, 2)
    fine = Mesh(mesh.devices.reshape(shape), ("z", "y", "x", "c"))
    by_image, by_text = P(("z", "y", "x", "c")), P(("y", "x", "c", "z"))
    return jax.shard_map(
        local,
        mesh=fine,
        in_specs=(by_image, by_text, by_image),
        out_specs=(P(), by_image, by_text),
        check_vma=False,
    )
```

```python
import functools
import math

import jax
import jax.numpy as jnp
from jax import lax
from jax.experimental import pallas as pl
from jax.experimental.pallas import tpu as pltpu
from jax.sharding import Mesh, PartitionSpec as P

sharpness = 1.0 / 0.07
f32 = jnp.float32
bf16 = jnp.bfloat16
NT = (((1,), (1,)), ((), ()))
PLANE, LINE = ("y", "x"), "z"
EXTRA = 16


def normalize(embed):
    flat = embed.astype(f32)
    factor = lax.rsqrt(jnp.sum(flat * flat, axis=1, keepdims=True) + 1e-06)
    return flat * factor, factor


def pack(dst, b, value):
    rows = value.shape[0]
    for k in range(value.shape[1] // 128):
        dst[b, k * rows : (k + 1) * rows, :] = value[:, k * 128 : (k + 1) * 128]


def unpack(ref, first, count, rows, width):
    return jnp.concatenate(
        [
            ref[first : first + count, k * rows : (k + 1) * rows, :].reshape(count * rows, 128)
            for k in range(width // 128)
        ],
        axis=1,
    )


def rows_tile(values):
    row = lax.broadcasted_iota(jnp.int32, (EXTRA, 128), 0)
    tile = jnp.zeros((EXTRA, 128), f32)
    for i, v in enumerate(values):
        tile = jnp.where(row == i, v, tile)
    return tile.astype(bf16)


LEVELS = 32760.0


def encode(value):
    most = jnp.max(jnp.abs(value), axis=0, keepdims=True)
    t = jnp.ceil(f32(8.0) * jnp.log2(jnp.maximum(most, f32(1e-30))) + f32(0.01))
    scaled = value * (f32(LEVELS) * jnp.exp2(t * f32(-0.125)))
    return jnp.round(scaled).astype(jnp.int32), t.astype(jnp.int32)


def start_kernel(img_hbm, txt_hbm, partner_hbm, keep_ref, send_ref, img, txt, partner, sems):
    copies = [
        pltpu.make_async_copy(src, dst, sems.at[i])
        for i, (src, dst) in enumerate(((img_hbm, img), (txt_hbm, txt), (partner_hbm, partner)))
    ]
    for c in copies:
        c.start()
    for c in copies:
        c.wait()
    image_core = lax.axis_index("c") == 0
    half, size = img.shape
    a, b = img[...].astype(f32), txt[...].astype(f32)
    keep_ref[:half] = jnp.where(image_core, a, b).astype(bf16)
    send_ref[:half] = jnp.where(image_core, b, a).astype(bf16)
    p = jnp.concatenate([partner[...]] * (128 // half), axis=1)
    hi = p // 128
    tile = rows_tile([hi.astype(f32), (p - hi * 128).astype(f32)])
    for dst in (keep_ref, send_ref):
        dst[half:] = jnp.zeros((EXTRA, size), bf16)
        dst[half:, :128] = tile


def prep_kernel(images, first, second, out):
    half = first.shape[0] - EXTRA
    unit = [normalize(src[:half, :])[0] for src in (first, second)]
    unit = jnp.concatenate(unit, axis=0).astype(bf16)
    size = unit.size // 128
    tile = jnp.zeros((EXTRA, 128), bf16)
    if images:
        lane = lax.broadcasted_iota(jnp.int32, (EXTRA, 128), 1)
        a, b = (src[half:, :128].astype(f32) for src in (first, second))
        tile = jnp.where(lane // half % 2 == 0, a, b).astype(bf16)
    for b in range(out.shape[0]):
        pack(out, b, unit)
        out[b, size:, :] = tile


def place(images, tiles, r, t, ny):
    per_half = tiles // 2
    half, tile = divmod(r * ny + t, per_half)
    if not images:
        half = 1 - half
    return half * (per_half // 2) + tile // 2, slice(tile % 2 * 128, tile % 2 * 128 + 128)


def image_sums_kernel(rows, x_ref, y_ref, pay_ref, sums_ref):
    packed = x_ref.shape[1]
    width = (packed - EXTRA) // rows * 128
    texts = x_ref.shape[0] // 2
    x = unpack(x_ref, 0, x_ref.shape[0], rows, width)
    y = unpack(y_ref, 0, texts, rows, width)
    scores = lax.dot_general(x, y, NT, preferred_element_type=f32)
    for r in range(x.shape[0] // 128):
        lanes = jnp.zeros((128, 128), f32)
        for t in range(y.shape[0] // 128):
            s = scores[r * 128 : (r + 1) * 128, t * 128 : (t + 1) * 128]
            lanes += jnp.exp2(s * f32(sharpness * math.log2(math.e)))
        sums_ref[r : r + 1] = jnp.sum(lanes.T, axis=0, keepdims=True)
    for b in range(pay_ref.shape[0]):
        pay_ref[b] = sums_ref[...]


def scores_kernel(images, rows, x_ref, y_ref, *refs):
    if images:
        unused, e_ref, match_ref, *scratch = refs
    else:
        e_ref, pay_ref, match_ref, *scratch = refs
    packed = x_ref.shape[1]
    width = (packed - EXTRA) // rows * 128
    per, half = 128 // rows, rows // 2
    texts = x_ref.shape[0] // 2
    nx, ny = x_ref.shape[0] // per, y_ref.shape[0] // per
    if images:
        ny = texts // per
    else:
        nx = texts // per
    lane = lax.broadcasted_iota(jnp.int32, (1, 128), 1)
    chip = lax.axis_index("y") * lax.axis_size("x") + lax.axis_index("x")
    tail = (x_ref if images else y_ref)[:, packed - EXTRA :, :].astype(f32)
    partner = tail[:, 0, :] * 128.0 + tail[:, 1, :]

    def partners(t):
        p = partner[per * t : per * t + 1]
        for q in range(1, per):
            p = jnp.where(lane >= q * rows, partner[per * t + q : per * t + q + 1], p)
        return p

    def ids(t):
        i = (lane % rows) // half * (texts * half) + (per * t + lane // rows) * half
        return (chip * (texts * rows) + i + lane % half).astype(f32)

    xs, ys = (partners, ids) if images else (ids, partners)
    xs_ref, ys_ref, *s_refs = scratch
    for r in range(nx):
        xs_ref[r : r + 1] = xs(r)
    for t in range(ny):
        ys_ref[t : t + 1] = ys(t)
    part = nx // 2

    def product(h):
        x = unpack(x_ref, h * part * per, part * per, rows, width)
        y = unpack(y_ref, 0, ny * per, rows, width)
        s = lax.dot_general(x, y, NT, preferred_element_type=f32)
        for r in range(part):
            for t in range(ny):
                s_refs[h][r * ny + t] = s[r * 128 : (r + 1) * 128, t * 128 : (t + 1) * 128]

    def weigh(h):
        for r in range(h * part, (h + 1) * part):
            own = jnp.broadcast_to(xs_ref[r : r + 1], (128, 128)).T
            lanes = jnp.zeros((128, 128), f32)
            found = jnp.zeros((128, 128), f32)
            for t in range(ny):
                e = jnp.exp2(s_refs[h][(r - h * part) * ny + t] * f32(sharpness * math.log2(math.e)))
                matched = jnp.where(own == ys_ref[t : t + 1], e, f32(0.0))
                if not images:
                    lanes += e
                found += matched
                block, at = place(images, nx * ny, r, t, ny)
                e_ref[block, at] = (e - f32(2.0) * matched).astype(bf16)
            if not images:
                pay_ref[0, r : r + 1] = jnp.sum(lanes.T, axis=0, keepdims=True)
            match_ref[r : r + 1] = jnp.sum(found.T, axis=0, keepdims=True)

    once = jnp.minimum(lax.axis_index("c") + 1, 1)
    product(0)

    def first(i, carry):
        product(1)
        weigh(0)
        return carry

    def second(i, carry):
        weigh(1)
        return carry

    lax.fori_loop(0, once, first, 0)
    lax.fori_loop(0, once, second, 0)
    if not images:
        m = match_ref[:nx]
        logs = jnp.where(m > 0.0, jnp.log(jnp.where(m > 0.0, m, f32(1.0))), f32(0.0))
        logs = jnp.sum(jnp.sum(logs, axis=0, keepdims=True), axis=1, keepdims=True)
        pay_ref[0, nx:] = jnp.broadcast_to(logs, (8 - nx, 128))
        match_ref[nx:] = jnp.zeros((8 - nx, 128), f32)
        for b in range(1, pay_ref.shape[0]):
            pay_ref[b] = pay_ref[0]


def grads_kernel(images, rows, y_ref, e_ref, match_ref, mine_ref, other_ref, out_ref):
    blocks, packed, _ = out_ref.shape
    width = (packed - EXTRA) // rows * 128
    per = 128 // rows
    nx = blocks // per
    ny = e_ref.shape[0] * 2 // nx
    col_total = other_ref[:ny]
    col_inv = f32(1.0) / col_total
    share = jnp.sum(jnp.log(col_total), axis=0, keepdims=True)
    share = jnp.broadcast_to(jnp.sum(share, axis=1, keepdims=True), (1, 128))
    if images:
        share -= 2.0 * other_ref[ny : ny + 1]
    whole = jnp.floor(share + f32(0.5))
    share = [whole.astype(jnp.int32), ((share - whole) * f32(32768.0)).astype(jnp.int32)]
    rest = [jnp.zeros((EXTRA - 2 - width // 128, 128), jnp.int32)]
    row_inv = f32(1.0) / mine_ref[:nx]
    y = unpack(y_ref, 0, ny * per, rows, width)
    gs = []
    ds = []
    for r in range(nx):
        ri = jnp.broadcast_to(row_inv[r : r + 1], (128, 128)).T
        matched = jnp.broadcast_to(match_ref[r : r + 1], (128, 128)).T
        d = []
        for t in range(ny):
            block, at = place(images, nx * ny, r, t, ny)
            e = e_ref[block, at].astype(f32)
            weight = ri + col_inv[t : t + 1]
            v = jnp.where(e < 0.0, matched * weight - f32(2.0), e * weight)
            d.append(v.astype(bf16))
        ds.append(jnp.concatenate(d, axis=1))
        if (r + 1) % (nx // 2) == 0:
            gs.append(jnp.dot(jnp.concatenate(ds, axis=0), y, preferred_element_type=f32))
            ds = []
    for b in range(blocks):
        steps = []
        for k in range(width // 128):
            q, t = encode(
                gs[b * 2 // blocks][
                    b % (blocks // 2) * rows : (b % (blocks // 2) + 1) * rows,
                    k * 128 : (k + 1) * 128,
                ]
            )
            out_ref[b, k * rows : (k + 1) * rows, :] = q.astype(jnp.int16)
            steps.append(t)
        tile = jnp.concatenate(steps + share + rest, axis=0)
        out_ref[b, packed - EXTRA :, :] = tile.astype(jnp.int16)


def finish_kernel(scale, keep_first, first, second, parts, keep_ref, send_ref, share_ref):
    half, size = keep_ref.shape
    rows = 2 * half
    body = rows * (size // 128)
    chunks = size // 128
    tail = parts[:, body:, :].astype(jnp.int32).astype(f32)
    step = jnp.exp2(tail[:, :chunks] * f32(0.125)) * f32(scale / LEVELS)
    total = []
    for k in range(chunks):
        piece = None
        for b in range(parts.shape[0]):
            q = parts[b, k * rows : (k + 1) * rows, :].astype(jnp.int32).astype(f32)
            q = q * step[b, k : k + 1]
            piece = q if piece is None else piece + q
        total.append(piece)
    total = jnp.concatenate(total, axis=1)
    grads = []
    for i, src in enumerate((first, second)):
        unit, factor = normalize(src[:half, :])
        g = total[i * half : (i + 1) * half]
        grads.append(factor * (g - unit * jnp.sum(unit * g, axis=1, keepdims=True)))
    keep, send = grads if keep_first else grads[::-1]
    keep_ref[...] = keep
    send_ref[:half] = send
    share = jnp.sum(tail[:, chunks : chunks + 1], axis=0)
    share += jnp.sum(tail[:, chunks + 1 : chunks + 2], axis=0) * f32(1.0 / 32768.0)
    share_ref[...] = jnp.broadcast_to(share, share_ref.shape)
    send_ref[half:] = jnp.broadcast_to(share[:, :1], (send_ref.shape[0] - half, size))


def output_kernel(batch, keep_ref, share_ref, recv_ref, img_ref, txt_ref, loss_ref):
    image_core = lax.axis_index("c") == 0
    half = keep_ref.shape[0]
    keep, recv = keep_ref[...], recv_ref[:half]
    img_ref[...] = jnp.where(image_core, keep, recv)
    txt_ref[...] = jnp.where(image_core, recv, keep)
    loss_ref[...] = (share_ref[:1, :1] + recv_ref[half : half + 1, :1]) / (2.0 * batch)


def call(kernel, outs, **kw):
    return pl.pallas_call(
        kernel,
        out_shape=[jax.ShapeDtypeStruct(*o) for o in outs],
        compiler_params=pltpu.CompilerParams(vmem_limit_bytes=48 * 1024 * 1024),
        **kw,
    )


def exchange(x, axes):
    return lax.all_to_all(x, axes, 0, 0)


def swap(x):
    return lax.ppermute(x, "c", [(0, 1), (1, 0)])


def local(image_embed, text_embed, partner):
    half, size = image_embed.shape
    rows = 2 * half
    n_plane = lax.axis_size("y") * lax.axis_size("x")
    n_line = lax.axis_size("z")
    batch = rows * n_plane * n_line
    image_core = lax.axis_index("c") == 0
    packed = rows * (size // 128) + EXTRA
    tiles = n_plane * n_line * rows * rows // (128 * 128)

    args = [
        pltpu.with_memory_space_constraint(a, pltpu.HBM)
        for a in (image_embed, text_embed, partner.reshape(1, half))
    ]
    own, send = call(
        start_kernel,
        [((half + EXTRA, size), bf16)] * 2,
        in_specs=[pl.BlockSpec(memory_space=pl.ANY)] * 3,
        scratch_shapes=[
            pltpu.VMEM((half, size), bf16),
            pltpu.VMEM((half, size), bf16),
            pltpu.VMEM((1, half), jnp.int32),
            pltpu.SemaphoreType.DMA((3,)),
        ],
    )(*args)
    off = swap(send)

    def gather_images():
        kernel = functools.partial(prep_kernel, True)
        return exchange(call(kernel, [((n_plane, packed, 128), bf16)])(own, off)[0], PLANE)

    def gather_texts():
        kernel = functools.partial(prep_kernel, False)
        every = exchange(call(kernel, [((n_line, packed, 128), bf16)])(off, own)[0], LINE)
        return jnp.pad(every, ((0, n_plane - n_line), (0, 0), (0, 0)))

    x = lax.cond(image_core, gather_images, gather_texts)
    y = swap(x)

    tile_kw = dict(
        input_output_aliases={0: 0},
        scratch_shapes=[pltpu.VMEM((8, 128), f32)] * 2
        + [pltpu.VMEM((tiles // 2, 128, 128), f32)] * 2,
    )
    e_out = ((n_plane, packed, 128), bf16)

    def image_sums():
        pay, own_sums = call(
            functools.partial(image_sums_kernel, rows),
            [((n_plane, 8, 128), f32), ((8, 128), f32)],
        )(x, y)
        every = exchange(pay, PLANE)
        e, match = call(
            functools.partial(scores_kernel, True, rows),
            [e_out, ((8, 128), f32)],
            **tile_kw,
        )(x, y, own_sums)
        return e, match, jnp.sum(every, axis=0)

    def text_sums():
        e, pay, match = call(
            functools.partial(scores_kernel, False, rows),
            [e_out, ((n_line, 8, 128), f32), ((8, 128), f32)],
            **tile_kw,
        )(x, y)
        return e, match, jnp.sum(exchange(pay, LINE), axis=0)

    e, match, mine = lax.cond(image_core, image_sums, text_sums)
    other = swap(mine)

    def grads(images, count, axes):
        pay = call(
            functools.partial(grads_kernel, images, rows),
            [((count, packed, 128), jnp.int16)],
        )(y, e, match, mine, other)[0]
        return call(
            functools.partial(finish_kernel, sharpness / (2.0 * batch), images),
            [((half, size), f32), ((half + 8, size), f32), ((8, 128), f32)],
        )(*((own, off) if images else (off, own)), exchange(pay, axes))

    keep, send, share = lax.cond(
        image_core,
        functools.partial(grads, True, n_plane, PLANE),
        functools.partial(grads, False, n_line, LINE),
    )
    image_grad, text_grad, loss = call(
        functools.partial(output_kernel, batch),
        [((half, size), f32), ((half, size), f32), ((1, 1), f32)],
    )(keep, share, swap(send))
    return loss.reshape(()), image_grad, text_grad


def solution(mesh):
    shape = (mesh.shape["row"], 4, mesh.shape["col"] // 8, 2)
    fine = Mesh(mesh.devices.reshape(shape), ("z", "y", "x", "c"))
    by_image, by_text = P(("z", "y", "x", "c")), P(("y", "x", "c", "z"))
    return jax.shard_map(
        local,
        mesh=fine,
        in_specs=(by_image, by_text, by_image),
        out_specs=(P(), by_image, by_text),
        check_vma=False,
    )
```

```python
import functools
import math

import jax
import jax.numpy as jnp
from jax import lax
from jax.experimental import pallas as pl
from jax.experimental.pallas import tpu as pltpu
from jax.sharding import Mesh, PartitionSpec as P

sharpness = 1.0 / 0.07
f32 = jnp.float32
bf16 = jnp.bfloat16
NT = (((1,), (1,)), ((), ()))
PLANE, LINE = ("y", "x"), "z"
EXTRA = 16


def normalize(embed):
    flat = embed.astype(f32)
    factor = lax.rsqrt(jnp.sum(flat * flat, axis=1, keepdims=True) + 1e-06)
    return flat * factor, factor


def pack(dst, b, value):
    rows = value.shape[0]
    for k in range(value.shape[1] // 128):
        dst[b, k * rows : (k + 1) * rows, :] = value[:, k * 128 : (k + 1) * 128]


def unpack(ref, first, count, rows, width):
    return jnp.concatenate(
        [
            ref[first : first + count, k * rows : (k + 1) * rows, :].reshape(count * rows, 128)
            for k in range(width // 128)
        ],
        axis=1,
    )


def rows_tile(values):
    row = lax.broadcasted_iota(jnp.int32, (EXTRA, 128), 0)
    tile = jnp.zeros((EXTRA, 128), f32)
    for i, v in enumerate(values):
        tile = jnp.where(row == i, v, tile)
    return tile.astype(bf16)


LEVELS = 32760.0


def encode(value):
    most = jnp.max(jnp.abs(value), axis=0, keepdims=True)
    t = jnp.ceil(f32(8.0) * jnp.log2(jnp.maximum(most, f32(1e-30))) + f32(0.01))
    scaled = value * (f32(LEVELS) * jnp.exp2(t * f32(-0.125)))
    return jnp.round(scaled).astype(jnp.int32), t.astype(jnp.int32)


def start_kernel(img_hbm, txt_hbm, partner_hbm, keep_ref, send_ref, img, txt, partner, sems):
    copies = [
        pltpu.make_async_copy(src, dst, sems.at[i])
        for i, (src, dst) in enumerate(((img_hbm, img), (txt_hbm, txt), (partner_hbm, partner)))
    ]
    for c in copies:
        c.start()
    for c in copies:
        c.wait()
    image_core = lax.axis_index("c") == 0
    half, size = img.shape
    a, b = img[...].astype(f32), txt[...].astype(f32)
    keep_ref[:half] = jnp.where(image_core, a, b).astype(bf16)
    send_ref[:half] = jnp.where(image_core, b, a).astype(bf16)
    p = jnp.concatenate([partner[...]] * (128 // half), axis=1)
    hi = p // 128
    tile = rows_tile([hi.astype(f32), (p - hi * 128).astype(f32)])
    for dst in (keep_ref, send_ref):
        dst[half:] = jnp.zeros((EXTRA, size), bf16)
        dst[half:, :128] = tile


def prep_kernel(images, first, second, out):
    half = first.shape[0] - EXTRA
    unit = [normalize(src[:half, :])[0] for src in (first, second)]
    unit = jnp.concatenate(unit, axis=0).astype(bf16)
    size = unit.size // 128
    tile = jnp.zeros((EXTRA, 128), bf16)
    if images:
        lane = lax.broadcasted_iota(jnp.int32, (EXTRA, 128), 1)
        a, b = (src[half:, :128].astype(f32) for src in (first, second))
        tile = jnp.where(lane // half % 2 == 0, a, b).astype(bf16)
    for b in range(out.shape[0]):
        pack(out, b, unit)
        out[b, size:, :] = tile


def vectors(rows, image_ref, texts):
    per, half = 128 // rows, rows // 2
    packed = image_ref.shape[1]
    lane = lax.broadcasted_iota(jnp.int32, (1, 128), 1)
    chip = lax.axis_index("y") * lax.axis_size("x") + lax.axis_index("x")
    tail = image_ref[:, packed - EXTRA :, :].astype(f32)
    partner = tail[:, 0, :] * 128.0 + tail[:, 1, :]

    def partners(t):
        p = partner[per * t : per * t + 1]
        for q in range(1, per):
            p = jnp.where(lane >= q * rows, partner[per * t + q : per * t + q + 1], p)
        return p

    def ids(t):
        i = (lane % rows) // half * (texts * half) + (per * t + lane // rows) * half
        return (chip * (texts * rows) + i + lane % half).astype(f32)

    return partners, ids


def weigh(tiles, own, targets):
    own = jnp.broadcast_to(own, (128, 128)).T
    lanes = jnp.zeros((128, 128), f32)
    found = jnp.zeros((128, 128), f32)
    out = []
    for s, target in zip(tiles, targets):
        e = jnp.exp2(s * f32(sharpness * math.log2(math.e)))
        matched = jnp.where(own == target, e, f32(0.0))
        lanes += e
        found += matched
        out.append((e - f32(2.0) * matched).astype(bf16))
    sums = jnp.sum(lanes.T, axis=0, keepdims=True)
    return out, sums, jnp.sum(found.T, axis=0, keepdims=True)


def first_kernel(rows, x_ref, y_ref, e_ref, sums_ref, match_ref):
    blocks, packed, _ = x_ref.shape
    width = (packed - EXTRA) // rows * 128
    n = blocks * rows // 128
    low = lax.axis_index("c") == 0
    x_partners, ids = vectors(rows, x_ref, blocks)
    y_partners, _ = vectors(rows, y_ref, blocks)
    xs = [jnp.where(low, x_partners(r), ids(r)) for r in range(n)]
    ys = [jnp.where(low, ids(t), y_partners(t)) for t in range(n)]
    x = unpack(x_ref, 0, blocks, rows, width)
    y = unpack(y_ref, 0, blocks, rows, width)
    scores = lax.dot_general(x, y, NT, preferred_element_type=f32)
    sums_ref[...] = jnp.zeros(sums_ref.shape, f32)
    match_ref[...] = jnp.zeros(match_ref.shape, f32)
    for r in range(n):
        tiles = [scores[r * 128 : (r + 1) * 128, t * 128 : (t + 1) * 128] for t in range(n)]
        out, total, matched = weigh(tiles, xs[r], ys)
        for t in range(n):
            e_ref[r * n + t] = out[t]
        sums_ref[r : r + 1] = total
        match_ref[r : r + 1] = matched


def second_kernel(images, rows, free_ref, other_ref, sums_ref, matches_ref, *refs):
    *own, e_ref, pay_ref, match_ref, xs_ref, ys_ref, s_ref = refs
    blocks, packed, _ = free_ref.shape
    width = (packed - EXTRA) // rows * 128
    n = blocks * rows // 128
    if images:
        x_ref, y_ref = free_ref, other_ref
        xs, ys = vectors(rows, x_ref, blocks)
    else:
        (x_ref,), y_ref = own, other_ref
        ys, xs = vectors(rows, y_ref, blocks)
    for r in range(n):
        xs_ref[r : r + 1] = xs(r)
        ys_ref[r : r + 1] = ys(r)
    x = unpack(x_ref, 0, blocks, rows, width)
    y = unpack(y_ref, 0, blocks, rows, width)
    scores = lax.dot_general(x, y, NT, preferred_element_type=f32)
    for r in range(n):
        for t in range(n):
            s_ref[r * n + t] = scores[r * 128 : (r + 1) * 128, t * 128 : (t + 1) * 128]
    pay_ref[0] = sums_ref[...]
    match_ref[...] = matches_ref[...]

    def turn(i, carry):
        for r in range(n):
            tiles = [s_ref[r * n + t] for t in range(n)]
            targets = [ys_ref[t : t + 1] for t in range(n)]
            out, total, matched = weigh(tiles, xs_ref[r : r + 1], targets)
            for t in range(n):
                tile = r * n + t
                e_ref[tile // 2, tile % 2 * 128 : tile % 2 * 128 + 128] = out[t]
            if images:
                pay_ref[0, n + r : n + r + 1] = total
                match_ref[n + r : n + r + 1] = matched
            else:
                pay_ref[0, r : r + 1] = sums_ref[r : r + 1] + total
                match_ref[r : r + 1] = matches_ref[r : r + 1] + matched
        return carry

    lax.fori_loop(0, jnp.minimum(lax.axis_index("c") + 1, 1), turn, 0)
    if not images:
        m = match_ref[:n]
        logs = jnp.where(m > 0.0, jnp.log(jnp.where(m > 0.0, m, f32(1.0))), f32(0.0))
        logs = jnp.sum(jnp.sum(logs, axis=0, keepdims=True), axis=1, keepdims=True)
        pay_ref[0, n:] = jnp.broadcast_to(logs, (8 - n, 128))
    for b in range(1, pay_ref.shape[0]):
        pay_ref[b] = pay_ref[0]


def grads_kernel(images, rows, first_ref, second_ref, match_ref, mine_ref, other_ref, *refs):
    *y_refs, out_ref = refs
    blocks, packed, _ = out_ref.shape
    width = (packed - EXTRA) // rows * 128
    per = 128 // rows
    nx = blocks // per
    n = y_refs[0].shape[0] * rows // 128
    ny = n * len(y_refs)
    col_total = other_ref[:ny]
    col_inv = f32(1.0) / col_total
    share = jnp.sum(jnp.log(col_total), axis=0, keepdims=True)
    share = jnp.broadcast_to(jnp.sum(share, axis=1, keepdims=True), (1, 128))
    if images:
        share -= 2.0 * other_ref[ny : ny + 1]
    whole = jnp.floor(share + f32(0.5))
    share = [whole.astype(jnp.int32), ((share - whole) * f32(32768.0)).astype(jnp.int32)]
    rest = [jnp.zeros((EXTRA - 2 - width // 128, 128), jnp.int32)]
    row_inv = f32(1.0) / mine_ref[:nx]
    y = [unpack(ref, 0, ref.shape[0], rows, width) for ref in y_refs]
    y = y[0] if images else jnp.concatenate(y, axis=0)
    gs = []
    ds = []
    for r in range(nx):
        ri = jnp.broadcast_to(row_inv[r : r + 1], (128, 128)).T
        matched = jnp.broadcast_to(match_ref[r : r + 1], (128, 128)).T
        d = []
        for t in range(ny):
            tile = r % n * n + t % n
            if r < n and t < n:
                e = first_ref[tile].astype(f32)
            else:
                e = second_ref[tile // 2, tile % 2 * 128 : tile % 2 * 128 + 128].astype(f32)
            weight = ri + col_inv[t : t + 1]
            v = jnp.where(e < 0.0, matched * weight - f32(2.0), e * weight)
            d.append(v.astype(bf16))
        ds.append(jnp.concatenate(d, axis=1))
        if (r + 1) % (nx // 2) == 0:
            gs.append(jnp.dot(jnp.concatenate(ds, axis=0), y, preferred_element_type=f32))
            ds = []
    for b in range(blocks):
        steps = []
        for k in range(width // 128):
            q, t = encode(
                gs[b * 2 // blocks][
                    b % (blocks // 2) * rows : (b % (blocks // 2) + 1) * rows,
                    k * 128 : (k + 1) * 128,
                ]
            )
            out_ref[b, k * rows : (k + 1) * rows, :] = q.astype(jnp.int16)
            steps.append(t)
        tile = jnp.concatenate(steps + share + rest, axis=0)
        out_ref[b, packed - EXTRA :, :] = tile.astype(jnp.int16)


def finish_kernel(scale, keep_first, first, second, parts, keep_ref, send_ref, share_ref):
    half, size = keep_ref.shape
    rows = 2 * half
    body = rows * (size // 128)
    chunks = size // 128
    tail = parts[:, body:, :].astype(jnp.int32).astype(f32)
    step = jnp.exp2(tail[:, :chunks] * f32(0.125)) * f32(scale / LEVELS)
    total = []
    for k in range(chunks):
        piece = None
        for b in range(parts.shape[0]):
            q = parts[b, k * rows : (k + 1) * rows, :].astype(jnp.int32).astype(f32)
            q = q * step[b, k : k + 1]
            piece = q if piece is None else piece + q
        total.append(piece)
    total = jnp.concatenate(total, axis=1)
    grads = []
    for i, src in enumerate((first, second)):
        unit, factor = normalize(src[:half, :])
        g = total[i * half : (i + 1) * half]
        grads.append(factor * (g - unit * jnp.sum(unit * g, axis=1, keepdims=True)))
    keep, send = grads if keep_first else grads[::-1]
    keep_ref[...] = keep
    send_ref[:half] = send
    share = jnp.sum(tail[:, chunks : chunks + 1], axis=0)
    share += jnp.sum(tail[:, chunks + 1 : chunks + 2], axis=0) * f32(1.0 / 32768.0)
    share_ref[...] = jnp.broadcast_to(share, share_ref.shape)
    send_ref[half:] = jnp.broadcast_to(share[:, :1], (send_ref.shape[0] - half, size))


def output_kernel(batch, keep_ref, share_ref, recv_ref, img_ref, txt_ref, loss_ref):
    image_core = lax.axis_index("c") == 0
    half = keep_ref.shape[0]
    keep, recv = keep_ref[...], recv_ref[:half]
    img_ref[...] = jnp.where(image_core, keep, recv)
    txt_ref[...] = jnp.where(image_core, recv, keep)
    loss_ref[...] = (share_ref[:1, :1] + recv_ref[half : half + 1, :1]) / (2.0 * batch)


def call(kernel, outs, **kw):
    return pl.pallas_call(
        kernel,
        out_shape=[o if isinstance(o, pl.MemoryRef) else jax.ShapeDtypeStruct(*o) for o in outs],
        compiler_params=pltpu.CompilerParams(vmem_limit_bytes=48 * 1024 * 1024),
        **kw,
    )


def exchange(x, axes):
    return lax.all_to_all(x, axes, 0, 0)


def swap(x):
    return lax.ppermute(x, "c", [(0, 1), (1, 0)])


def local(image_embed, text_embed, partner):
    half, size = image_embed.shape
    rows = 2 * half
    n_plane = lax.axis_size("y") * lax.axis_size("x")
    n_line = lax.axis_size("z")
    batch = rows * n_plane * n_line
    image_core = lax.axis_index("c") == 0
    packed = rows * (size // 128) + EXTRA
    tiles = n_plane * n_line * rows * rows // (128 * 128)

    args = [
        pltpu.with_memory_space_constraint(a, pltpu.HBM)
        for a in (image_embed, text_embed, partner.reshape(1, half))
    ]
    own, send = call(
        start_kernel,
        [((half + EXTRA, size), bf16)] * 2,
        in_specs=[pl.BlockSpec(memory_space=pl.ANY)] * 3,
        scratch_shapes=[
            pltpu.VMEM((half, size), bf16),
            pltpu.VMEM((half, size), bf16),
            pltpu.VMEM((1, half), jnp.int32),
            pltpu.SemaphoreType.DMA((3,)),
        ],
    )(*args)
    off = swap(send)

    def gather_images():
        kernel = functools.partial(prep_kernel, True)
        every = exchange(call(kernel, [((n_plane, packed, 128), bf16)])(own, off)[0], PLANE)
        return every[:n_line], every[n_line:]

    def gather_texts():
        kernel = functools.partial(prep_kernel, False)
        every = exchange(call(kernel, [((n_line, packed, 128), bf16)])(off, own)[0], LINE)
        return every, every

    x1, x2 = lax.cond(image_core, gather_images, gather_texts)
    y1, y2 = swap(x1), swap(x2)
    e1, sums1, match1 = call(
        functools.partial(first_kernel, rows),
        [pltpu.VMEM((tiles // 2, 128, 128), bf16), ((8, 128), f32), ((8, 128), f32)],
        cost_estimate=pl.CostEstimate(
            flops=tiles * 128 * 128 * size, bytes_accessed=2 * x1.size, transcendentals=x1.size
        ),
    )(x1, y1)

    def sums(images, count, axes):
        arrays = (x2, y1, sums1, match1) if images else (x2, y2, sums1, match1, x1)
        e2, pay, match = call(
            functools.partial(second_kernel, images, rows),
            [((n_line, packed, 128), bf16), ((count, 8, 128), f32), ((8, 128), f32)],
            input_output_aliases={0: 0},
            scratch_shapes=[pltpu.VMEM((8, 128), f32)] * 2
            + [pltpu.VMEM((tiles // 2, 128, 128), f32)],
        )(*arrays)
        return e2, match, jnp.sum(exchange(pay, axes), axis=0)

    e2, match, mine = lax.cond(
        image_core,
        functools.partial(sums, True, n_plane, PLANE),
        functools.partial(sums, False, n_line, LINE),
    )
    other = swap(mine)

    def grads(images, count, axes):
        pay = call(
            functools.partial(grads_kernel, images, rows),
            [((count, packed, 128), jnp.int16)],
        )(e1, e2, match, mine, other, *([y1] if images else [y1, y2]))[0]
        return call(
            functools.partial(finish_kernel, sharpness / (2.0 * batch), images),
            [((half, size), f32), ((half + 8, size), f32), ((8, 128), f32)],
        )(*((own, off) if images else (off, own)), exchange(pay, axes))

    keep, send, share = lax.cond(
        image_core,
        functools.partial(grads, True, n_plane, PLANE),
        functools.partial(grads, False, n_line, LINE),
    )
    image_grad, text_grad, loss = call(
        functools.partial(output_kernel, batch),
        [((half, size), f32), ((half, size), f32), ((1, 1), f32)],
    )(keep, share, swap(send))
    return loss.reshape(()), image_grad, text_grad


def solution(mesh):
    shape = (mesh.shape["row"], 4, mesh.shape["col"] // 8, 2)
    fine = Mesh(mesh.devices.reshape(shape), ("z", "y", "x", "c"))
    by_image, by_text = P(("z", "y", "x", "c")), P(("y", "x", "c", "z"))
    return jax.shard_map(
        local,
        mesh=fine,
        in_specs=(by_image, by_text, by_image),
        out_specs=(P(), by_image, by_text),
        check_vma=False,
    )
```

```python
import functools
import math

import jax
import jax.numpy as jnp
from jax import lax
from jax.experimental import pallas as pl
from jax.experimental.pallas import tpu as pltpu
from jax.sharding import Mesh, PartitionSpec as P

sharpness = 1.0 / 0.07
f32 = jnp.float32
bf16 = jnp.bfloat16
NT = (((1,), (1,)), ((), ()))
PLANE, LINE = ("y", "x"), "z"
EXTRA = 16


def normalize(embed):
    flat = embed.astype(f32)
    factor = lax.rsqrt(jnp.sum(flat * flat, axis=1, keepdims=True) + 1e-06)
    return flat * factor, factor


def pack(dst, b, value):
    rows = value.shape[0]
    for k in range(value.shape[1] // 128):
        dst[b, k * rows : (k + 1) * rows, :] = value[:, k * 128 : (k + 1) * 128]


def unpack(ref, first, count, rows, width):
    return jnp.concatenate(
        [
            ref[first : first + count, k * rows : (k + 1) * rows, :].reshape(count * rows, 128)
            for k in range(width // 128)
        ],
        axis=1,
    )


def rows_tile(values):
    row = lax.broadcasted_iota(jnp.int32, (EXTRA, 128), 0)
    tile = jnp.zeros((EXTRA, 128), f32)
    for i, v in enumerate(values):
        tile = jnp.where(row == i, v, tile)
    return tile.astype(bf16)


LEVELS = 32760.0


def encode(value):
    most = jnp.max(jnp.abs(value), axis=0, keepdims=True)
    t = jnp.ceil(f32(8.0) * jnp.log2(jnp.maximum(most, f32(1e-30))) + f32(0.01))
    scaled = value * (f32(LEVELS) * jnp.exp2(t * f32(-0.125)))
    return jnp.round(scaled).astype(jnp.int32), t.astype(jnp.int32)


def start_kernel(img_hbm, txt_hbm, partner_hbm, keep_ref, send_ref, img, txt, partner, sems):
    copies = [
        pltpu.make_async_copy(src, dst, sems.at[i])
        for i, (src, dst) in enumerate(((img_hbm, img), (txt_hbm, txt), (partner_hbm, partner)))
    ]
    for c in copies:
        c.start()
    for c in copies:
        c.wait()
    image_core = lax.axis_index("c") == 0
    half, size = img.shape
    a, b = img[...].astype(f32), txt[...].astype(f32)
    keep_ref[:half] = jnp.where(image_core, a, b).astype(bf16)
    send_ref[:half] = jnp.where(image_core, b, a).astype(bf16)
    p = jnp.concatenate([partner[...]] * (128 // half), axis=1)
    hi = p // 128
    tile = rows_tile([hi.astype(f32), (p - hi * 128).astype(f32)])
    for dst in (keep_ref, send_ref):
        dst[half:] = jnp.zeros((EXTRA, size), bf16)
        dst[half:, :128] = tile


def prep_kernel(images, first, second, out):
    half = first.shape[0] - EXTRA
    unit = [normalize(src[:half, :])[0] for src in (first, second)]
    unit = jnp.concatenate(unit, axis=0).astype(bf16)
    size = unit.size // 128
    tile = jnp.zeros((EXTRA, 128), bf16)
    if images:
        lane = lax.broadcasted_iota(jnp.int32, (EXTRA, 128), 1)
        a, b = (src[half:, :128].astype(f32) for src in (first, second))
        tile = jnp.where(lane // half % 2 == 0, a, b).astype(bf16)
    for b in range(out.shape[0]):
        pack(out, b, unit)
        out[b, size:, :] = tile


def vectors(rows, image_ref, texts):
    per, half = 128 // rows, rows // 2
    packed = image_ref.shape[1]
    lane = lax.broadcasted_iota(jnp.int32, (1, 128), 1)
    chip = lax.axis_index("y") * lax.axis_size("x") + lax.axis_index("x")
    tail = image_ref[:, packed - EXTRA :, :].astype(f32)
    partner = tail[:, 0, :] * 128.0 + tail[:, 1, :]

    def partners(t):
        p = partner[per * t : per * t + 1]
        for q in range(1, per):
            p = jnp.where(lane >= q * rows, partner[per * t + q : per * t + q + 1], p)
        return p

    def ids(t):
        i = (lane % rows) // half * (texts * half) + (per * t + lane // rows) * half
        return (chip * (texts * rows) + i + lane % half).astype(f32)

    return partners, ids


def weigh(tiles, own, targets):
    own = jnp.broadcast_to(own, (128, 128)).T
    lanes = jnp.zeros((128, 128), f32)
    found = jnp.zeros((128, 128), f32)
    out = []
    for s, target in zip(tiles, targets):
        e = jnp.exp2(s * f32(sharpness * math.log2(math.e)))
        matched = jnp.where(own == target, e, f32(0.0))
        lanes += e
        found += matched
        out.append((e - f32(2.0) * matched).astype(bf16))
    sums = jnp.sum(lanes.T, axis=0, keepdims=True)
    return out, sums, jnp.sum(found.T, axis=0, keepdims=True)


def first_kernel(rows, x_ref, y_ref, e_ref, sums_ref, match_ref):
    blocks, packed, _ = x_ref.shape
    width = (packed - EXTRA) // rows * 128
    n = blocks * rows // 128
    low = lax.axis_index("c") == 0
    x_partners, ids = vectors(rows, x_ref, blocks)
    y_partners, _ = vectors(rows, y_ref, blocks)
    xs = [jnp.where(low, x_partners(r), ids(r)) for r in range(n)]
    ys = [jnp.where(low, ids(t), y_partners(t)) for t in range(n)]
    x = unpack(x_ref, 0, blocks, rows, width)
    y = unpack(y_ref, 0, blocks, rows, width)
    scores = lax.dot_general(x, y, NT, preferred_element_type=f32)
    sums_ref[...] = jnp.zeros(sums_ref.shape, f32)
    match_ref[...] = jnp.zeros(match_ref.shape, f32)
    for r in range(n):
        tiles = [scores[r * 128 : (r + 1) * 128, t * 128 : (t + 1) * 128] for t in range(n)]
        out, total, matched = weigh(tiles, xs[r], ys)
        for t in range(n):
            e_ref[r * n + t] = out[t]
        sums_ref[r : r + 1] = total
        match_ref[r : r + 1] = matched


def second_kernel(images, rows, free_ref, other_ref, sums_ref, matches_ref, *refs):
    *own, e_ref, pay_ref, match_ref, xs_ref, ys_ref, s_ref = refs
    blocks, packed, _ = free_ref.shape
    width = (packed - EXTRA) // rows * 128
    n = blocks * rows // 128
    if images:
        x_ref, y_ref = free_ref, other_ref
        xs, ys = vectors(rows, x_ref, blocks)
    else:
        (x_ref,), y_ref = own, other_ref
        ys, xs = vectors(rows, y_ref, blocks)
    for r in range(n):
        xs_ref[r : r + 1] = xs(r)
        ys_ref[r : r + 1] = ys(r)
    x = unpack(x_ref, 0, blocks, rows, width)
    y = unpack(y_ref, 0, blocks, rows, width)
    scores = lax.dot_general(x, y, NT, preferred_element_type=f32)
    for r in range(n):
        for t in range(n):
            s_ref[r * n + t] = scores[r * 128 : (r + 1) * 128, t * 128 : (t + 1) * 128]
    pay_ref[0] = sums_ref[...]
    match_ref[...] = matches_ref[...]

    def turn(i, carry):
        for r in range(n):
            tiles = [s_ref[r * n + t] for t in range(n)]
            targets = [ys_ref[t : t + 1] for t in range(n)]
            out, total, matched = weigh(tiles, xs_ref[r : r + 1], targets)
            for t in range(n):
                tile = r * n + t
                e_ref[tile // 2, tile % 2 * 128 : tile % 2 * 128 + 128] = out[t]
            if images:
                pay_ref[0, n + r : n + r + 1] = total
                match_ref[n + r : n + r + 1] = matched
            else:
                pay_ref[0, r : r + 1] = sums_ref[r : r + 1] + total
                match_ref[r : r + 1] = matches_ref[r : r + 1] + matched
        return carry

    lax.fori_loop(0, jnp.minimum(lax.axis_index("c") + 1, 1), turn, 0)
    if not images:
        m = match_ref[:n]
        logs = jnp.where(m > 0.0, jnp.log(jnp.where(m > 0.0, m, f32(1.0))), f32(0.0))
        logs = jnp.sum(jnp.sum(logs, axis=0, keepdims=True), axis=1, keepdims=True)
        pay_ref[0, n:] = jnp.broadcast_to(logs, (8 - n, 128))
    for b in range(1, pay_ref.shape[0]):
        pay_ref[b] = pay_ref[0]


def grads_kernel(images, rows, first_ref, second_ref, match_ref, mine_ref, other_ref, *refs):
    *y_refs, out_ref, first_vmem, sem = refs
    copy = pltpu.make_async_copy(first_ref, first_vmem, sem)
    copy.start()
    blocks, packed, _ = out_ref.shape
    width = (packed - EXTRA) // rows * 128
    per = 128 // rows
    nx = blocks // per
    n = y_refs[0].shape[0] * rows // 128
    ny = n * len(y_refs)
    col_total = other_ref[:ny]
    col_inv = f32(1.0) / col_total
    share = jnp.sum(jnp.log(col_total), axis=0, keepdims=True)
    share = jnp.broadcast_to(jnp.sum(share, axis=1, keepdims=True), (1, 128))
    if images:
        share -= 2.0 * other_ref[ny : ny + 1]
    whole = jnp.floor(share + f32(0.5))
    share = [whole.astype(jnp.int32), ((share - whole) * f32(32768.0)).astype(jnp.int32)]
    rest = [jnp.zeros((EXTRA - 2 - width // 128, 128), jnp.int32)]
    row_inv = f32(1.0) / mine_ref[:nx]
    y = [unpack(ref, 0, ref.shape[0], rows, width) for ref in y_refs]
    y = y[0] if images else jnp.concatenate(y, axis=0)
    gs = [None, None]
    for h in (1, 0) if images else (0, 1):
        if h == 0:
            copy.wait()
        ds = []
        for r in range(h * nx // 2, (h + 1) * nx // 2):
            ri = jnp.broadcast_to(row_inv[r : r + 1], (128, 128)).T
            matched = jnp.broadcast_to(match_ref[r : r + 1], (128, 128)).T
            d = []
            for t in range(ny):
                tile = r % n * n + t % n
                if r < n and t < n:
                    e = first_vmem[tile].astype(f32)
                else:
                    e = second_ref[tile // 2, tile % 2 * 128 : tile % 2 * 128 + 128].astype(f32)
                weight = ri + col_inv[t : t + 1]
                v = jnp.where(e < 0.0, matched * weight - f32(2.0), e * weight)
                d.append(v.astype(bf16))
            ds.append(jnp.concatenate(d, axis=1))
        gs[h] = jnp.dot(jnp.concatenate(ds, axis=0), y, preferred_element_type=f32)
    for b in range(blocks):
        steps = []
        for k in range(width // 128):
            q, t = encode(
                gs[b * 2 // blocks][
                    b % (blocks // 2) * rows : (b % (blocks // 2) + 1) * rows,
                    k * 128 : (k + 1) * 128,
                ]
            )
            out_ref[b, k * rows : (k + 1) * rows, :] = q.astype(jnp.int16)
            steps.append(t)
        tile = jnp.concatenate(steps + share + rest, axis=0)
        out_ref[b, packed - EXTRA :, :] = tile.astype(jnp.int16)


def finish_kernel(scale, keep_first, first, second, parts, keep_ref, send_ref, share_ref):
    half, size = keep_ref.shape
    rows = 2 * half
    body = rows * (size // 128)
    chunks = size // 128
    tail = parts[:, body:, :].astype(jnp.int32).astype(f32)
    step = jnp.exp2(tail[:, :chunks] * f32(0.125)) * f32(scale / LEVELS)
    total = []
    for k in range(chunks):
        piece = None
        for b in range(parts.shape[0]):
            q = parts[b, k * rows : (k + 1) * rows, :].astype(jnp.int32).astype(f32)
            q = q * step[b, k : k + 1]
            piece = q if piece is None else piece + q
        total.append(piece)
    total = jnp.concatenate(total, axis=1)
    grads = []
    for i, src in enumerate((first, second)):
        unit, factor = normalize(src[:half, :])
        g = total[i * half : (i + 1) * half]
        grads.append(factor * (g - unit * jnp.sum(unit * g, axis=1, keepdims=True)))
    keep, send = grads if keep_first else grads[::-1]
    keep_ref[...] = keep
    send_ref[:half] = send
    share = jnp.sum(tail[:, chunks : chunks + 1], axis=0)
    share += jnp.sum(tail[:, chunks + 1 : chunks + 2], axis=0) * f32(1.0 / 32768.0)
    share_ref[...] = jnp.broadcast_to(share, share_ref.shape)
    send_ref[half:] = jnp.broadcast_to(share[:, :1], (send_ref.shape[0] - half, size))


def output_kernel(batch, keep_ref, share_ref, recv_ref, img_ref, txt_ref, loss_ref):
    image_core = lax.axis_index("c") == 0
    half = keep_ref.shape[0]
    keep, recv = keep_ref[...], recv_ref[:half]
    img_ref[...] = jnp.where(image_core, keep, recv)
    txt_ref[...] = jnp.where(image_core, recv, keep)
    loss_ref[...] = (share_ref[:1, :1] + recv_ref[half : half + 1, :1]) / (2.0 * batch)


def call(kernel, outs, **kw):
    return pl.pallas_call(
        kernel,
        out_shape=[o if isinstance(o, pl.MemoryRef) else jax.ShapeDtypeStruct(*o) for o in outs],
        compiler_params=pltpu.CompilerParams(vmem_limit_bytes=48 * 1024 * 1024),
        **kw,
    )


def exchange(x, axes):
    return lax.all_to_all(x, axes, 0, 0)


def swap(x):
    return lax.ppermute(x, "c", [(0, 1), (1, 0)])


def local(image_embed, text_embed, partner):
    half, size = image_embed.shape
    rows = 2 * half
    n_plane = lax.axis_size("y") * lax.axis_size("x")
    n_line = lax.axis_size("z")
    batch = rows * n_plane * n_line
    image_core = lax.axis_index("c") == 0
    packed = rows * (size // 128) + EXTRA
    tiles = n_plane * n_line * rows * rows // (128 * 128)

    args = [
        pltpu.with_memory_space_constraint(a, pltpu.HBM)
        for a in (image_embed, text_embed, partner.reshape(1, half))
    ]
    own, send = call(
        start_kernel,
        [((half + EXTRA, size), bf16)] * 2,
        in_specs=[pl.BlockSpec(memory_space=pl.ANY)] * 3,
        scratch_shapes=[
            pltpu.VMEM((half, size), bf16),
            pltpu.VMEM((half, size), bf16),
            pltpu.VMEM((1, half), jnp.int32),
            pltpu.SemaphoreType.DMA((3,)),
        ],
    )(*args)
    off = swap(send)

    def gather_images():
        kernel = functools.partial(prep_kernel, True)
        every = exchange(call(kernel, [((n_plane, packed, 128), bf16)])(own, off)[0], PLANE)
        return every[:n_line], every[n_line:]

    def gather_texts():
        kernel = functools.partial(prep_kernel, False)
        every = exchange(call(kernel, [((n_line, packed, 128), bf16)])(off, own)[0], LINE)
        return every, every

    x1, x2 = lax.cond(image_core, gather_images, gather_texts)
    y1, y2 = swap(x1), swap(x2)
    e1, sums1, match1 = call(
        functools.partial(first_kernel, rows),
        [((tiles // 2, 128, 128), bf16), ((8, 128), f32), ((8, 128), f32)],
        cost_estimate=pl.CostEstimate(
            flops=tiles * 128 * 128 * size, bytes_accessed=2 * x1.size, transcendentals=x1.size
        ),
    )(x1, y1)

    def sums(images, count, axes):
        arrays = (x2, y1, sums1, match1) if images else (x2, y2, sums1, match1, x1)
        e2, pay, match = call(
            functools.partial(second_kernel, images, rows),
            [((n_line, packed, 128), bf16), ((count, 8, 128), f32), ((8, 128), f32)],
            input_output_aliases={0: 0},
            scratch_shapes=[pltpu.VMEM((8, 128), f32)] * 2
            + [pltpu.VMEM((tiles // 2, 128, 128), f32)],
        )(*arrays)
        return e2, match, jnp.sum(exchange(pay, axes), axis=0)

    e2, match, mine = lax.cond(
        image_core,
        functools.partial(sums, True, n_plane, PLANE),
        functools.partial(sums, False, n_line, LINE),
    )
    other = swap(mine)

    def grads(images, count, axes):
        y = [y1] if images else [y1, y2]
        pay = call(
            functools.partial(grads_kernel, images, rows),
            [((count, packed, 128), jnp.int16)],
            in_specs=[pl.BlockSpec(memory_space=pl.ANY)]
            + [pl.BlockSpec(memory_space=pltpu.VMEM)] * (4 + len(y)),
            scratch_shapes=[
                pltpu.VMEM((tiles // 2, 128, 128), bf16),
                pltpu.SemaphoreType.DMA,
            ],
        )(e1, e2, match, mine, other, *y)[0]
        return call(
            functools.partial(finish_kernel, sharpness / (2.0 * batch), images),
            [((half, size), f32), ((half + 8, size), f32), ((8, 128), f32)],
        )(*((own, off) if images else (off, own)), exchange(pay, axes))

    keep, send, share = lax.cond(
        image_core,
        functools.partial(grads, True, n_plane, PLANE),
        functools.partial(grads, False, n_line, LINE),
    )
    image_grad, text_grad, loss = call(
        functools.partial(output_kernel, batch),
        [((half, size), f32), ((half, size), f32), ((1, 1), f32)],
    )(keep, share, swap(send))
    return loss.reshape(()), image_grad, text_grad


def solution(mesh):
    shape = (mesh.shape["row"], 4, mesh.shape["col"] // 8, 2)
    fine = Mesh(mesh.devices.reshape(shape), ("z", "y", "x", "c"))
    by_image, by_text = P(("z", "y", "x", "c")), P(("y", "x", "c", "z"))
    return jax.shard_map(
        local,
        mesh=fine,
        in_specs=(by_image, by_text, by_image),
        out_specs=(P(), by_image, by_text),
        check_vma=False,
    )
```

```python
import functools
import math

import jax
import jax.numpy as jnp
from jax import lax
from jax.experimental import pallas as pl
from jax.experimental.pallas import tpu as pltpu
from jax.sharding import Mesh, PartitionSpec as P

sharpness = 1.0 / 0.07
f32 = jnp.float32
bf16 = jnp.bfloat16
NT = (((1,), (1,)), ((), ()))
PLANE, LINE = ("y", "x"), "z"
EXTRA = 16
FIRST = 2


def normalize(embed):
    flat = embed.astype(f32)
    factor = lax.rsqrt(jnp.sum(flat * flat, axis=1, keepdims=True) + 1e-06)
    return flat * factor, factor


def pack(dst, b, value):
    rows = value.shape[0]
    for k in range(value.shape[1] // 128):
        dst[b, k * rows : (k + 1) * rows, :] = value[:, k * 128 : (k + 1) * 128]


def unpack(ref, first, count, rows, width):
    return jnp.concatenate(
        [
            ref[first : first + count, k * rows : (k + 1) * rows, :].reshape(count * rows, 128)
            for k in range(width // 128)
        ],
        axis=1,
    )


def rows_tile(values):
    row = lax.broadcasted_iota(jnp.int32, (EXTRA, 128), 0)
    tile = jnp.zeros((EXTRA, 128), f32)
    for i, v in enumerate(values):
        tile = jnp.where(row == i, v, tile)
    return tile.astype(bf16)


LEVELS = 32760.0


def encode(value):
    most = jnp.max(jnp.abs(value), axis=0, keepdims=True)
    t = jnp.ceil(f32(8.0) * jnp.log2(jnp.maximum(most, f32(1e-30))) + f32(0.01))
    scaled = value * (f32(LEVELS) * jnp.exp2(t * f32(-0.125)))
    return jnp.round(scaled).astype(jnp.int32), t.astype(jnp.int32)


def start_kernel(img_hbm, txt_hbm, partner_hbm, keep_ref, send_ref, img, txt, partner, sems):
    copies = [
        pltpu.make_async_copy(src, dst, sems.at[i])
        for i, (src, dst) in enumerate(((img_hbm, img), (txt_hbm, txt), (partner_hbm, partner)))
    ]
    for c in copies:
        c.start()
    for c in copies:
        c.wait()
    image_core = lax.axis_index("c") == 0
    half, size = img.shape
    a, b = img[...].astype(f32), txt[...].astype(f32)
    keep_ref[:half] = jnp.where(image_core, a, b).astype(bf16)
    send_ref[:half] = jnp.where(image_core, b, a).astype(bf16)
    p = jnp.concatenate([partner[...]] * (128 // half), axis=1)
    hi = p // 128
    tile = rows_tile([hi.astype(f32), (p - hi * 128).astype(f32)])
    for dst in (keep_ref, send_ref):
        dst[half:] = jnp.zeros((EXTRA, size), bf16)
        dst[half:, :128] = tile


def prep_kernel(images, first, second, out):
    half = first.shape[0] - EXTRA
    unit = [normalize(src[:half, :])[0] for src in (first, second)]
    unit = jnp.concatenate(unit, axis=0).astype(bf16)
    size = unit.size // 128
    tile = jnp.zeros((EXTRA, 128), bf16)
    if images:
        lane = lax.broadcasted_iota(jnp.int32, (EXTRA, 128), 1)
        a, b = (src[half:, :128].astype(f32) for src in (first, second))
        tile = jnp.where(lane // half % 2 == 0, a, b).astype(bf16)
    for b in range(out.shape[0]):
        pack(out, b, unit)
        out[b, size:, :] = tile


def vectors(rows, image_ref, texts):
    per, half = 128 // rows, rows // 2
    packed = image_ref.shape[1]
    lane = lax.broadcasted_iota(jnp.int32, (1, 128), 1)
    chip = lax.axis_index("y") * lax.axis_size("x") + lax.axis_index("x")
    tail = image_ref[:, packed - EXTRA :, :].astype(f32)
    partner = tail[:, 0, :] * 128.0 + tail[:, 1, :]

    def partners(t):
        p = partner[per * t : per * t + 1]
        for q in range(1, per):
            p = jnp.where(lane >= q * rows, partner[per * t + q : per * t + q + 1], p)
        return p

    def ids(t):
        i = (lane % rows) // half * (texts * half) + (per * t + lane // rows) * half
        return (chip * (texts * rows) + i + lane % half).astype(f32)

    return partners, ids


def weigh(tiles, own, targets):
    own = jnp.broadcast_to(own, (128, 128)).T
    lanes = jnp.zeros((128, 128), f32)
    found = jnp.zeros((128, 128), f32)
    out = []
    for s, target in zip(tiles, targets):
        e = jnp.exp2(s * f32(sharpness * math.log2(math.e)))
        matched = jnp.where(own == target, e, f32(0.0))
        lanes += e
        found += matched
        out.append((e - f32(2.0) * matched).astype(bf16))
    sums = jnp.sum(lanes.T, axis=0, keepdims=True)
    return out, sums, jnp.sum(found.T, axis=0, keepdims=True)


def first_kernel(rows, x_ref, y_ref, e_ref, sums_ref, match_ref):
    blocks, packed, _ = x_ref.shape
    width = (packed - EXTRA) // rows * 128
    n = blocks * rows // 128
    low = lax.axis_index("c") == 0
    x_partners, ids = vectors(rows, x_ref, blocks)
    y_partners, _ = vectors(rows, y_ref, blocks)
    xs = [jnp.where(low, x_partners(r), ids(r)) for r in range(n)]
    ys = [jnp.where(low, ids(t), y_partners(t)) for t in range(FIRST)]
    x = unpack(x_ref, 0, blocks, rows, width)
    y = unpack(y_ref, 0, FIRST * 128 // rows, rows, width)
    scores = lax.dot_general(x, y, NT, preferred_element_type=f32)
    sums_ref[...] = jnp.zeros(sums_ref.shape, f32)
    match_ref[...] = jnp.zeros(match_ref.shape, f32)
    for r in range(n):
        tiles = [scores[r * 128 : (r + 1) * 128, t * 128 : (t + 1) * 128] for t in range(FIRST)]
        out, total, matched = weigh(tiles, xs[r], ys)
        for t in range(FIRST):
            e_ref[r * FIRST + t] = out[t]
        sums_ref[r : r + 1] = total
        match_ref[r : r + 1] = matched


def second_kernel(images, rows, free_ref, x1_ref, y1_ref, sums_ref, matches_ref, *refs):
    *far, e_ref, pay_ref, match_ref, xs_ref, ys_ref, s_ref = refs
    blocks, packed, _ = free_ref.shape
    width = (packed - EXTRA) // rows * 128
    n = blocks * rows // 128
    rest = n - FIRST
    x_ref, y_ref = (free_ref, y1_ref) if images else (x1_ref, far[0])
    partners, ids = vectors(rows, x1_ref if images else y1_ref, blocks)
    far_partners, _ = vectors(rows, x_ref if images else y_ref, blocks)
    near = (partners, ids) if images else (ids, partners)
    xs, ys = (far_partners, ids) if images else (ids, far_partners)
    for r in range(n):
        xs_ref[r : r + 1] = near[0](r)
        xs_ref[n + r : n + r + 1] = xs(r)
        ys_ref[r : r + 1] = near[1](r)
        ys_ref[n + r : n + r + 1] = ys(r)
    x = unpack(x1_ref, 0, blocks, rows, width)
    y = unpack(y1_ref, FIRST * 128 // rows, rest * 128 // rows, rows, width)
    scores = lax.dot_general(x, y, NT, preferred_element_type=f32)
    for r in range(n):
        for t in range(rest):
            s_ref[n * n + r * rest + t] = scores[r * 128 : (r + 1) * 128, t * 128 : (t + 1) * 128]
    x = unpack(x_ref, 0, blocks, rows, width)
    y = unpack(y_ref, 0, blocks, rows, width)
    scores = lax.dot_general(x, y, NT, preferred_element_type=f32)
    for r in range(n):
        for t in range(n):
            s_ref[r * n + t] = scores[r * 128 : (r + 1) * 128, t * 128 : (t + 1) * 128]
    pay_ref[0] = sums_ref[...]
    match_ref[...] = matches_ref[...]

    def turn(i, carry):
        for r in range(n):
            tiles = [s_ref[n * n + r * rest + t] for t in range(rest)]
            targets = [ys_ref[FIRST + t : FIRST + t + 1] for t in range(rest)]
            out, total, matched = weigh(tiles, xs_ref[r : r + 1], targets)
            for t in range(rest):
                e_ref[r * rest + t, 256:384] = out[t]
            pay_ref[0, r : r + 1] = sums_ref[r : r + 1] + total
            match_ref[r : r + 1] = matches_ref[r : r + 1] + matched
        for r in range(n):
            tiles = [s_ref[r * n + t] for t in range(n)]
            targets = [ys_ref[n + t : n + t + 1] for t in range(n)]
            out, total, matched = weigh(tiles, xs_ref[n + r : n + r + 1], targets)
            for t in range(n):
                tile = r * n + t
                e_ref[tile // 2, tile % 2 * 128 : tile % 2 * 128 + 128] = out[t]
            if images:
                pay_ref[0, n + r : n + r + 1] = total
                match_ref[n + r : n + r + 1] = matched
            else:
                pay_ref[0, r : r + 1] = pay_ref[0, r : r + 1] + total
                match_ref[r : r + 1] = match_ref[r : r + 1] + matched
        return carry

    lax.fori_loop(0, jnp.minimum(lax.axis_index("c") + 1, 1), turn, 0)
    if not images:
        m = match_ref[:n]
        logs = jnp.where(m > 0.0, jnp.log(jnp.where(m > 0.0, m, f32(1.0))), f32(0.0))
        logs = jnp.sum(jnp.sum(logs, axis=0, keepdims=True), axis=1, keepdims=True)
        pay_ref[0, n:] = jnp.broadcast_to(logs, (8 - n, 128))
    for b in range(1, pay_ref.shape[0]):
        pay_ref[b] = pay_ref[0]


def grads_kernel(images, rows, first_ref, second_ref, match_ref, mine_ref, other_ref, *refs):
    *y_refs, out_ref = refs
    blocks, packed, _ = out_ref.shape
    width = (packed - EXTRA) // rows * 128
    per = 128 // rows
    nx = blocks // per
    n = y_refs[0].shape[0] * rows // 128
    ny = n * len(y_refs)
    col_total = other_ref[:ny]
    col_inv = f32(1.0) / col_total
    share = jnp.sum(jnp.log(col_total), axis=0, keepdims=True)
    share = jnp.broadcast_to(jnp.sum(share, axis=1, keepdims=True), (1, 128))
    if images:
        share -= 2.0 * other_ref[ny : ny + 1]
    whole = jnp.floor(share + f32(0.5))
    share = [whole.astype(jnp.int32), ((share - whole) * f32(32768.0)).astype(jnp.int32)]
    rest = [jnp.zeros((EXTRA - 2 - width // 128, 128), jnp.int32)]
    row_inv = f32(1.0) / mine_ref[:nx]
    y = [unpack(ref, 0, ref.shape[0], rows, width) for ref in y_refs]
    y = y[0] if images else jnp.concatenate(y, axis=0)
    gs = []
    ds = []
    for r in range(nx):
        ri = jnp.broadcast_to(row_inv[r : r + 1], (128, 128)).T
        matched = jnp.broadcast_to(match_ref[r : r + 1], (128, 128)).T
        d = []
        for t in range(ny):
            tile = r % n * n + t % n
            if r < n and t < FIRST:
                e = first_ref[r * FIRST + t].astype(f32)
            elif r < n and t < n:
                e = second_ref[r * (n - FIRST) + t - FIRST, 256:384].astype(f32)
            else:
                e = second_ref[tile // 2, tile % 2 * 128 : tile % 2 * 128 + 128].astype(f32)
            weight = ri + col_inv[t : t + 1]
            v = jnp.where(e < 0.0, matched * weight - f32(2.0), e * weight)
            d.append(v.astype(bf16))
        ds.append(jnp.concatenate(d, axis=1))
        if (r + 1) % (nx // 2) == 0:
            gs.append(jnp.dot(jnp.concatenate(ds, axis=0), y, preferred_element_type=f32))
            ds = []
    for b in range(blocks):
        steps = []
        for k in range(width // 128):
            q, t = encode(
                gs[b * 2 // blocks][
                    b % (blocks // 2) * rows : (b % (blocks // 2) + 1) * rows,
                    k * 128 : (k + 1) * 128,
                ]
            )
            out_ref[b, k * rows : (k + 1) * rows, :] = q.astype(jnp.int16)
            steps.append(t)
        tile = jnp.concatenate(steps + share + rest, axis=0)
        out_ref[b, packed - EXTRA :, :] = tile.astype(jnp.int16)


def finish_kernel(scale, keep_first, first, second, parts, keep_ref, send_ref, share_ref):
    half, size = keep_ref.shape
    rows = 2 * half
    body = rows * (size // 128)
    chunks = size // 128
    tail = parts[:, body:, :].astype(jnp.int32).astype(f32)
    step = jnp.exp2(tail[:, :chunks] * f32(0.125)) * f32(scale / LEVELS)
    total = []
    for k in range(chunks):
        piece = None
        for b in range(parts.shape[0]):
            q = parts[b, k * rows : (k + 1) * rows, :].astype(jnp.int32).astype(f32)
            q = q * step[b, k : k + 1]
            piece = q if piece is None else piece + q
        total.append(piece)
    total = jnp.concatenate(total, axis=1)
    grads = []
    for i, src in enumerate((first, second)):
        unit, factor = normalize(src[:half, :])
        g = total[i * half : (i + 1) * half]
        grads.append(factor * (g - unit * jnp.sum(unit * g, axis=1, keepdims=True)))
    keep, send = grads if keep_first else grads[::-1]
    keep_ref[...] = keep
    send_ref[:half] = send
    share = jnp.sum(tail[:, chunks : chunks + 1], axis=0)
    share += jnp.sum(tail[:, chunks + 1 : chunks + 2], axis=0) * f32(1.0 / 32768.0)
    share_ref[...] = jnp.broadcast_to(share, share_ref.shape)
    send_ref[half:] = jnp.broadcast_to(share[:, :1], (send_ref.shape[0] - half, size))


def output_kernel(batch, keep_ref, share_ref, recv_ref, img_ref, txt_ref, loss_ref):
    image_core = lax.axis_index("c") == 0
    half = keep_ref.shape[0]
    keep, recv = keep_ref[...], recv_ref[:half]
    img_ref[...] = jnp.where(image_core, keep, recv)
    txt_ref[...] = jnp.where(image_core, recv, keep)
    loss_ref[...] = (share_ref[:1, :1] + recv_ref[half : half + 1, :1]) / (2.0 * batch)


def call(kernel, outs, **kw):
    return pl.pallas_call(
        kernel,
        out_shape=[o if isinstance(o, pl.MemoryRef) else jax.ShapeDtypeStruct(*o) for o in outs],
        compiler_params=pltpu.CompilerParams(vmem_limit_bytes=48 * 1024 * 1024),
        **kw,
    )


def exchange(x, axes):
    return lax.all_to_all(x, axes, 0, 0)


def swap(x):
    return lax.ppermute(x, "c", [(0, 1), (1, 0)])


def local(image_embed, text_embed, partner):
    half, size = image_embed.shape
    rows = 2 * half
    n_plane = lax.axis_size("y") * lax.axis_size("x")
    n_line = lax.axis_size("z")
    batch = rows * n_plane * n_line
    image_core = lax.axis_index("c") == 0
    packed = rows * (size // 128) + EXTRA
    tiles = n_plane * n_line * rows * rows // (128 * 128)

    args = [
        pltpu.with_memory_space_constraint(a, pltpu.HBM)
        for a in (image_embed, text_embed, partner.reshape(1, half))
    ]
    own, send = call(
        start_kernel,
        [((half + EXTRA, size), bf16)] * 2,
        in_specs=[pl.BlockSpec(memory_space=pl.ANY)] * 3,
        scratch_shapes=[
            pltpu.VMEM((half, size), bf16),
            pltpu.VMEM((half, size), bf16),
            pltpu.VMEM((1, half), jnp.int32),
            pltpu.SemaphoreType.DMA((3,)),
        ],
    )(*args)
    off = swap(send)

    def gather_images():
        kernel = functools.partial(prep_kernel, True)
        every = exchange(call(kernel, [((n_plane, packed, 128), bf16)])(own, off)[0], PLANE)
        return every[:n_line], every[n_line:]

    def gather_texts():
        kernel = functools.partial(prep_kernel, False)
        every = exchange(call(kernel, [((n_line, packed, 128), bf16)])(off, own)[0], LINE)
        return every, every

    x1, x2 = lax.cond(image_core, gather_images, gather_texts)
    y1, y2 = swap(x1), swap(x2)
    e1, sums1, match1 = call(
        functools.partial(first_kernel, rows),
        [pltpu.VMEM((tiles // 8 * FIRST, 128, 128), bf16), ((8, 128), f32), ((8, 128), f32)],
        cost_estimate=pl.CostEstimate(
            flops=tiles * 128 * 128 * size, bytes_accessed=2 * x1.size, transcendentals=x1.size
        ),
    )(x1, y1)

    def sums(images, count, axes):
        arrays = (x2, x1, y1, sums1, match1) if images else (x2, x1, y1, sums1, match1, y2)
        e2, pay, match = call(
            functools.partial(second_kernel, images, rows),
            [((n_line, packed, 128), bf16), ((count, 8, 128), f32), ((8, 128), f32)],
            input_output_aliases={0: 0},
            scratch_shapes=[pltpu.VMEM((8, 128), f32)] * 2 + [pltpu.VMEM((tiles, 128, 128), f32)],
        )(*arrays)
        return e2, match, jnp.sum(exchange(pay, axes), axis=0)

    e2, match, mine = lax.cond(
        image_core,
        functools.partial(sums, True, n_plane, PLANE),
        functools.partial(sums, False, n_line, LINE),
    )
    other = swap(mine)

    def grads(images, count, axes):
        pay = call(
            functools.partial(grads_kernel, images, rows),
            [((count, packed, 128), jnp.int16)],
        )(e1, e2, match, mine, other, *([y1] if images else [y1, y2]))[0]
        return call(
            functools.partial(finish_kernel, sharpness / (2.0 * batch), images),
            [((half, size), f32), ((half + 8, size), f32), ((8, 128), f32)],
        )(*((own, off) if images else (off, own)), exchange(pay, axes))

    keep, send, share = lax.cond(
        image_core,
        functools.partial(grads, True, n_plane, PLANE),
        functools.partial(grads, False, n_line, LINE),
    )
    image_grad, text_grad, loss = call(
        functools.partial(output_kernel, batch),
        [((half, size), f32), ((half, size), f32), ((1, 1), f32)],
    )(keep, share, swap(send))
    return loss.reshape(()), image_grad, text_grad


def solution(mesh):
    shape = (mesh.shape["row"], 4, mesh.shape["col"] // 8, 2)
    fine = Mesh(mesh.devices.reshape(shape), ("z", "y", "x", "c"))
    by_image, by_text = P(("z", "y", "x", "c")), P(("y", "x", "c", "z"))
    return jax.shard_map(
        local,
        mesh=fine,
        in_specs=(by_image, by_text, by_image),
        out_specs=(P(), by_image, by_text),
        check_vma=False,
    )
```

```python
import functools
import math

import jax
import jax.numpy as jnp
from jax import lax
from jax.experimental import pallas as pl
from jax.experimental.pallas import tpu as pltpu
from jax.sharding import Mesh, PartitionSpec as P

sharpness = 1.0 / 0.07
f32 = jnp.float32
bf16 = jnp.bfloat16
NT = (((1,), (1,)), ((), ()))
PLANE, LINE = ("y", "x"), "z"
EXTRA = 16


def normalize(embed):
    flat = embed.astype(f32)
    factor = lax.rsqrt(jnp.sum(flat * flat, axis=1, keepdims=True) + 1e-06)
    return flat * factor, factor


def pack(dst, b, value):
    rows = value.shape[0]
    for k in range(value.shape[1] // 128):
        dst[b, k * rows : (k + 1) * rows, :] = value[:, k * 128 : (k + 1) * 128]


def unpack(ref, first, count, rows, width):
    return jnp.concatenate(
        [
            ref[first : first + count, k * rows : (k + 1) * rows, :].reshape(count * rows, 128)
            for k in range(width // 128)
        ],
        axis=1,
    )


def rows_tile(values):
    row = lax.broadcasted_iota(jnp.int32, (EXTRA, 128), 0)
    tile = jnp.zeros((EXTRA, 128), f32)
    for i, v in enumerate(values):
        tile = jnp.where(row == i, v, tile)
    return tile.astype(bf16)


LEVELS = 32760.0


def encode(value):
    most = jnp.max(jnp.abs(value), axis=0, keepdims=True)
    t = jnp.ceil(f32(8.0) * jnp.log2(jnp.maximum(most, f32(1e-30))) + f32(0.01))
    scaled = value * (f32(LEVELS) * jnp.exp2(t * f32(-0.125)))
    return jnp.round(scaled).astype(jnp.int32), t.astype(jnp.int32)


def start_kernel(img_hbm, txt_hbm, partner_hbm, keep_ref, send_ref, img, txt, partner, sems):
    copies = [
        pltpu.make_async_copy(src, dst, sems.at[i])
        for i, (src, dst) in enumerate(((img_hbm, img), (txt_hbm, txt), (partner_hbm, partner)))
    ]
    for c in copies:
        c.start()
    for c in copies:
        c.wait()
    image_core = lax.axis_index("c") == 0
    half, size = img.shape
    a, b = img[...].astype(f32), txt[...].astype(f32)
    keep_ref[:half] = jnp.where(image_core, a, b).astype(bf16)
    send_ref[:half] = jnp.where(image_core, b, a).astype(bf16)
    p = jnp.concatenate([partner[...]] * (128 // half), axis=1)
    hi = p // 128
    tile = rows_tile([hi.astype(f32), (p - hi * 128).astype(f32)])
    for dst in (keep_ref, send_ref):
        dst[half:] = jnp.zeros((EXTRA, size), bf16)
        dst[half:, :128] = tile


def prep_kernel(images, first, second, out):
    half = first.shape[0] - EXTRA
    unit = [normalize(src[:half, :])[0] for src in (first, second)]
    unit = jnp.concatenate(unit, axis=0).astype(bf16)
    size = unit.size // 128
    tile = jnp.zeros((EXTRA, 128), bf16)
    if images:
        lane = lax.broadcasted_iota(jnp.int32, (EXTRA, 128), 1)
        a, b = (src[half:, :128].astype(f32) for src in (first, second))
        tile = jnp.where(lane // half % 2 == 0, a, b).astype(bf16)
    for b in range(out.shape[0]):
        pack(out, b, unit)
        out[b, size:, :] = tile


def vectors(rows, image_ref, texts):
    per, half = 128 // rows, rows // 2
    packed = image_ref.shape[1]
    lane = lax.broadcasted_iota(jnp.int32, (1, 128), 1)
    chip = lax.axis_index("y") * lax.axis_size("x") + lax.axis_index("x")
    tail = image_ref[:, packed - EXTRA :, :].astype(f32)
    partner = tail[:, 0, :] * 128.0 + tail[:, 1, :]

    def partners(t):
        p = partner[per * t : per * t + 1]
        for q in range(1, per):
            p = jnp.where(lane >= q * rows, partner[per * t + q : per * t + q + 1], p)
        return p

    def ids(t):
        i = (lane % rows) // half * (texts * half) + (per * t + lane // rows) * half
        return (chip * (texts * rows) + i + lane % half).astype(f32)

    return partners, ids


def weigh(tiles, own, targets):
    own = jnp.broadcast_to(own, (128, 128)).T
    lanes = jnp.zeros((128, 128), f32)
    found = jnp.zeros((128, 128), f32)
    out = []
    for s, target in zip(tiles, targets):
        e = jnp.exp2(s * f32(sharpness * math.log2(math.e)))
        matched = jnp.where(own == target, e, f32(0.0))
        lanes += e
        found += matched
        out.append((e - f32(2.0) * matched).astype(bf16))
    sums = jnp.sum(lanes.T, axis=0, keepdims=True)
    return out, sums, jnp.sum(found.T, axis=0, keepdims=True)


def first_kernel(rows, x_ref, y_ref, e_ref, sums_ref, match_ref):
    blocks, packed, _ = x_ref.shape
    width = (packed - EXTRA) // rows * 128
    n = blocks * rows // 128
    low = lax.axis_index("c") == 0
    x_partners, ids = vectors(rows, x_ref, blocks)
    y_partners, _ = vectors(rows, y_ref, blocks)
    xs = [jnp.where(low, x_partners(r), ids(r)) for r in range(n)]
    ys = [jnp.where(low, ids(t), y_partners(t)) for t in range(n)]
    x = unpack(x_ref, 0, blocks, rows, width)
    y = unpack(y_ref, 0, blocks, rows, width)
    scores = lax.dot_general(x, y, NT, preferred_element_type=f32)
    sums_ref[...] = jnp.zeros(sums_ref.shape, f32)
    match_ref[...] = jnp.zeros(match_ref.shape, f32)
    for r in range(n):
        tiles = [scores[r * 128 : (r + 1) * 128, t * 128 : (t + 1) * 128] for t in range(n)]
        out, total, matched = weigh(tiles, xs[r], ys)
        for t in range(n):
            e_ref[r * n + t] = out[t]
        sums_ref[r : r + 1] = total
        match_ref[r : r + 1] = matched


def second_kernel(images, rows, free_ref, other_ref, sums_ref, matches_ref, *refs):
    *own, e_ref, pay_ref, match_ref, xs_ref, ys_ref, s_ref = refs
    blocks, packed, _ = free_ref.shape
    width = (packed - EXTRA) // rows * 128
    n = blocks * rows // 128
    if images:
        x_ref, y_ref = free_ref, other_ref
        xs, ys = vectors(rows, x_ref, blocks)
    else:
        (x_ref,), y_ref = own, other_ref
        ys, xs = vectors(rows, y_ref, blocks)
    for r in range(n):
        xs_ref[r : r + 1] = xs(r)
        ys_ref[r : r + 1] = ys(r)
    x = unpack(x_ref, 0, blocks, rows, width)
    y = unpack(y_ref, 0, blocks, rows, width)
    scores = lax.dot_general(x, y, NT, preferred_element_type=f32)
    for r in range(n):
        for t in range(n):
            s_ref[r * n + t] = scores[r * 128 : (r + 1) * 128, t * 128 : (t + 1) * 128]
    pay_ref[0] = sums_ref[...]
    match_ref[...] = matches_ref[...]

    def turn(i, carry):
        for r in range(n):
            tiles = [s_ref[r * n + t] for t in range(n)]
            targets = [ys_ref[t : t + 1] for t in range(n)]
            out, total, matched = weigh(tiles, xs_ref[r : r + 1], targets)
            for t in range(n):
                tile = r * n + t
                e_ref[tile // 2, tile % 2 * 128 : tile % 2 * 128 + 128] = out[t]
            if images:
                pay_ref[0, n + r : n + r + 1] = total
                match_ref[n + r : n + r + 1] = matched
            else:
                pay_ref[0, r : r + 1] = sums_ref[r : r + 1] + total
                match_ref[r : r + 1] = matches_ref[r : r + 1] + matched
        return carry

    lax.fori_loop(0, jnp.minimum(lax.axis_index("c") + 1, 1), turn, 0)
    if not images:
        m = match_ref[:n]
        logs = jnp.where(m > 0.0, jnp.log(jnp.where(m > 0.0, m, f32(1.0))), f32(0.0))
        logs = jnp.sum(jnp.sum(logs, axis=0, keepdims=True), axis=1, keepdims=True)
        pay_ref[0, n:] = jnp.broadcast_to(logs, (8 - n, 128))
    for b in range(1, pay_ref.shape[0]):
        pay_ref[b] = pay_ref[0]


def text_kernel(rows, free_ref, far_hbm, sums_ref, matches_ref, x_ref, e_ref, pay_ref, match_ref, far, sems):
    del free_ref
    blocks, packed, _ = x_ref.shape
    width = (packed - EXTRA) // rows * 128
    n = blocks * rows // 128
    part = blocks // 2
    copies = [
        pltpu.make_async_copy(
            far_hbm.at[pl.ds(h * part, part)], far.at[pl.ds(h * part, part)], sems.at[h]
        )
        for h in range(2)
    ]
    for c in copies:
        c.start()
    x = unpack(x_ref, 0, blocks, rows, width)
    sums = [sums_ref[r : r + 1] for r in range(n)]
    found = [matches_ref[r : r + 1] for r in range(n)]
    for h in range(2):
        copies[h].wait()
        view = far.at[pl.ds(h * part, part)]
        partners, ids = vectors(rows, view, blocks)
        targets = [partners(t) for t in range(n // 2)]
        y = unpack(view, 0, part, rows, width)
        scores = lax.dot_general(x, y, NT, preferred_element_type=f32)
        for r in range(n):
            tiles = [
                scores[r * 128 : (r + 1) * 128, t * 128 : (t + 1) * 128] for t in range(n // 2)
            ]
            out, total, matched = weigh(tiles, ids(r), targets)
            for t in range(n // 2):
                tile = r * n + h * n // 2 + t
                e_ref[tile // 2, tile % 2 * 128 : tile % 2 * 128 + 128] = out[t]
            sums[r] += total
            found[r] += matched
    m = jnp.concatenate(found, axis=0)
    match_ref[:n] = m
    match_ref[n:] = jnp.zeros((8 - n, 128), f32)
    logs = jnp.where(m > 0.0, jnp.log(jnp.where(m > 0.0, m, f32(1.0))), f32(0.0))
    logs = jnp.sum(jnp.sum(logs, axis=0, keepdims=True), axis=1, keepdims=True)
    pay = jnp.concatenate(sums + [jnp.broadcast_to(logs, (8 - n, 128))], axis=0)
    for b in range(pay_ref.shape[0]):
        pay_ref[b] = pay


def grads_kernel(images, rows, first_ref, second_ref, match_ref, mine_ref, other_ref, *refs):
    *y_refs, out_ref = refs
    blocks, packed, _ = out_ref.shape
    width = (packed - EXTRA) // rows * 128
    per = 128 // rows
    nx = blocks // per
    n = y_refs[0].shape[0] * rows // 128
    ny = n * len(y_refs)
    col_total = other_ref[:ny]
    col_inv = f32(1.0) / col_total
    share = jnp.sum(jnp.log(col_total), axis=0, keepdims=True)
    share = jnp.broadcast_to(jnp.sum(share, axis=1, keepdims=True), (1, 128))
    if images:
        share -= 2.0 * other_ref[ny : ny + 1]
    whole = jnp.floor(share + f32(0.5))
    share = [whole.astype(jnp.int32), ((share - whole) * f32(32768.0)).astype(jnp.int32)]
    rest = [jnp.zeros((EXTRA - 2 - width // 128, 128), jnp.int32)]
    row_inv = f32(1.0) / mine_ref[:nx]
    y = [unpack(ref, 0, ref.shape[0], rows, width) for ref in y_refs]
    y = y[0] if images else jnp.concatenate(y, axis=0)
    gs = []
    ds = []
    for r in range(nx):
        ri = jnp.broadcast_to(row_inv[r : r + 1], (128, 128)).T
        matched = jnp.broadcast_to(match_ref[r : r + 1], (128, 128)).T
        d = []
        for t in range(ny):
            tile = r % n * n + t % n
            if r < n and t < n:
                e = first_ref[tile].astype(f32)
            else:
                e = second_ref[tile // 2, tile % 2 * 128 : tile % 2 * 128 + 128].astype(f32)
            weight = ri + col_inv[t : t + 1]
            v = jnp.where(e < 0.0, matched * weight - f32(2.0), e * weight)
            d.append(v.astype(bf16))
        ds.append(jnp.concatenate(d, axis=1))
        if (r + 1) % (nx // 2) == 0:
            gs.append(jnp.dot(jnp.concatenate(ds, axis=0), y, preferred_element_type=f32))
            ds = []
    for b in range(blocks):
        steps = []
        for k in range(width // 128):
            q, t = encode(
                gs[b * 2 // blocks][
                    b % (blocks // 2) * rows : (b % (blocks // 2) + 1) * rows,
                    k * 128 : (k + 1) * 128,
                ]
            )
            out_ref[b, k * rows : (k + 1) * rows, :] = q.astype(jnp.int16)
            steps.append(t)
        tile = jnp.concatenate(steps + share + rest, axis=0)
        out_ref[b, packed - EXTRA :, :] = tile.astype(jnp.int16)


def finish_kernel(scale, keep_first, first, second, parts, keep_ref, send_ref, share_ref):
    half, size = keep_ref.shape
    rows = 2 * half
    body = rows * (size // 128)
    chunks = size // 128
    tail = parts[:, body:, :].astype(jnp.int32).astype(f32)
    step = jnp.exp2(tail[:, :chunks] * f32(0.125)) * f32(scale / LEVELS)
    total = []
    for k in range(chunks):
        piece = None
        for b in range(parts.shape[0]):
            q = parts[b, k * rows : (k + 1) * rows, :].astype(jnp.int32).astype(f32)
            q = q * step[b, k : k + 1]
            piece = q if piece is None else piece + q
        total.append(piece)
    total = jnp.concatenate(total, axis=1)
    grads = []
    for i, src in enumerate((first, second)):
        unit, factor = normalize(src[:half, :])
        g = total[i * half : (i + 1) * half]
        grads.append(factor * (g - unit * jnp.sum(unit * g, axis=1, keepdims=True)))
    keep, send = grads if keep_first else grads[::-1]
    keep_ref[...] = keep
    send_ref[:half] = send
    share = jnp.sum(tail[:, chunks : chunks + 1], axis=0)
    share += jnp.sum(tail[:, chunks + 1 : chunks + 2], axis=0) * f32(1.0 / 32768.0)
    share_ref[...] = jnp.broadcast_to(share, share_ref.shape)
    send_ref[half:] = jnp.broadcast_to(share[:, :1], (send_ref.shape[0] - half, size))


def output_kernel(batch, keep_ref, share_ref, recv_ref, img_ref, txt_ref, loss_ref):
    image_core = lax.axis_index("c") == 0
    half = keep_ref.shape[0]
    keep, recv = keep_ref[...], recv_ref[:half]
    img_ref[...] = jnp.where(image_core, keep, recv)
    txt_ref[...] = jnp.where(image_core, recv, keep)
    loss_ref[...] = (share_ref[:1, :1] + recv_ref[half : half + 1, :1]) / (2.0 * batch)


def call(kernel, outs, **kw):
    return pl.pallas_call(
        kernel,
        out_shape=[o if isinstance(o, pl.MemoryRef) else jax.ShapeDtypeStruct(*o) for o in outs],
        compiler_params=pltpu.CompilerParams(vmem_limit_bytes=48 * 1024 * 1024),
        **kw,
    )


def exchange(x, axes):
    return lax.all_to_all(x, axes, 0, 0)


def swap(x):
    return lax.ppermute(x, "c", [(0, 1), (1, 0)])


def local(image_embed, text_embed, partner):
    half, size = image_embed.shape
    rows = 2 * half
    n_plane = lax.axis_size("y") * lax.axis_size("x")
    n_line = lax.axis_size("z")
    batch = rows * n_plane * n_line
    image_core = lax.axis_index("c") == 0
    packed = rows * (size // 128) + EXTRA
    tiles = n_plane * n_line * rows * rows // (128 * 128)

    args = [
        pltpu.with_memory_space_constraint(a, pltpu.HBM)
        for a in (image_embed, text_embed, partner.reshape(1, half))
    ]
    own, send = call(
        start_kernel,
        [((half + EXTRA, size), bf16)] * 2,
        in_specs=[pl.BlockSpec(memory_space=pl.ANY)] * 3,
        scratch_shapes=[
            pltpu.VMEM((half, size), bf16),
            pltpu.VMEM((half, size), bf16),
            pltpu.VMEM((1, half), jnp.int32),
            pltpu.SemaphoreType.DMA((3,)),
        ],
    )(*args)
    off = swap(send)

    def gather_images():
        kernel = functools.partial(prep_kernel, True)
        every = exchange(call(kernel, [((n_plane, packed, 128), bf16)])(own, off)[0], PLANE)
        return every[:n_line], every[n_line:]

    def gather_texts():
        kernel = functools.partial(prep_kernel, False)
        every = exchange(call(kernel, [((n_line, packed, 128), bf16)])(off, own)[0], LINE)
        return every, every

    x1, x2 = lax.cond(image_core, gather_images, gather_texts)
    y1, y2 = swap(x1), swap(x2)
    e1, sums1, match1 = call(
        functools.partial(first_kernel, rows),
        [pltpu.VMEM((tiles // 2, 128, 128), bf16), ((8, 128), f32), ((8, 128), f32)],
        cost_estimate=pl.CostEstimate(
            flops=tiles * 128 * 128 * size, bytes_accessed=2 * x1.size, transcendentals=x1.size
        ),
    )(x1, y1)

    def sums(images, count, axes):
        arrays = (x2, y1, sums1, match1) if images else (x2, y2, sums1, match1, x1)
        if images:
            kernel = functools.partial(second_kernel, True, rows)
            scratch = [pltpu.VMEM((8, 128), f32)] * 2
            scratch += [pltpu.VMEM((tiles // 2, 128, 128), f32)]
        else:
            kernel = functools.partial(text_kernel, rows)
            scratch = [pltpu.VMEM(y2.shape, bf16), pltpu.SemaphoreType.DMA((2,))]
        specs = [pl.BlockSpec(memory_space=pltpu.VMEM)] * len(arrays)
        if not images:
            specs[1] = pl.BlockSpec(memory_space=pl.ANY)
        e2, pay, match = call(
            kernel,
            [((n_line, packed, 128), bf16), ((count, 8, 128), f32), ((8, 128), f32)],
            input_output_aliases={0: 0},
            in_specs=specs,
            scratch_shapes=scratch,
        )(*arrays)
        return e2, match, jnp.sum(exchange(pay, axes), axis=0)

    e2, match, mine = lax.cond(
        image_core,
        functools.partial(sums, True, n_plane, PLANE),
        functools.partial(sums, False, n_line, LINE),
    )
    other = swap(mine)

    def grads(images, count, axes):
        pay = call(
            functools.partial(grads_kernel, images, rows),
            [((count, packed, 128), jnp.int16)],
        )(e1, e2, match, mine, other, *([y1] if images else [y1, y2]))[0]
        return call(
            functools.partial(finish_kernel, sharpness / (2.0 * batch), images),
            [((half, size), f32), ((half + 8, size), f32), ((8, 128), f32)],
        )(*((own, off) if images else (off, own)), exchange(pay, axes))

    keep, send, share = lax.cond(
        image_core,
        functools.partial(grads, True, n_plane, PLANE),
        functools.partial(grads, False, n_line, LINE),
    )
    image_grad, text_grad, loss = call(
        functools.partial(output_kernel, batch),
        [((half, size), f32), ((half, size), f32), ((1, 1), f32)],
    )(keep, share, swap(send))
    return loss.reshape(()), image_grad, text_grad


def solution(mesh):
    shape = (mesh.shape["row"], 4, mesh.shape["col"] // 8, 2)
    fine = Mesh(mesh.devices.reshape(shape), ("z", "y", "x", "c"))
    by_image, by_text = P(("z", "y", "x", "c")), P(("y", "x", "c", "z"))
    return jax.shard_map(
        local,
        mesh=fine,
        in_specs=(by_image, by_text, by_image),
        out_specs=(P(), by_image, by_text),
        check_vma=False,
    )
```

```python
import functools
import math

import jax
import jax.numpy as jnp
from jax import lax
from jax.experimental import pallas as pl
from jax.experimental.pallas import tpu as pltpu
from jax.sharding import Mesh, PartitionSpec as P

sharpness = 1.0 / 0.07
f32 = jnp.float32
bf16 = jnp.bfloat16
NT = (((1,), (1,)), ((), ()))
PLANE, LINE = ("x", "y"), "z"
EXTRA = 16


def normalize(embed):
    flat = embed.astype(f32)
    factor = lax.rsqrt(jnp.sum(flat * flat, axis=1, keepdims=True) + 1e-06)
    return flat * factor, factor


def pack(dst, b, value):
    rows = value.shape[0]
    for k in range(value.shape[1] // 128):
        dst[b, k * rows : (k + 1) * rows, :] = value[:, k * 128 : (k + 1) * 128]


def unpack(ref, first, count, rows, width):
    return jnp.concatenate(
        [
            ref[first : first + count, k * rows : (k + 1) * rows, :].reshape(count * rows, 128)
            for k in range(width // 128)
        ],
        axis=1,
    )


def rows_tile(values):
    row = lax.broadcasted_iota(jnp.int32, (EXTRA, 128), 0)
    tile = jnp.zeros((EXTRA, 128), f32)
    for i, v in enumerate(values):
        tile = jnp.where(row == i, v, tile)
    return tile.astype(bf16)


LEVELS = 32760.0


def encode(value):
    most = jnp.max(jnp.abs(value), axis=0, keepdims=True)
    t = jnp.ceil(f32(8.0) * jnp.log2(jnp.maximum(most, f32(1e-30))) + f32(0.01))
    scaled = value * (f32(LEVELS) * jnp.exp2(t * f32(-0.125)))
    return jnp.round(scaled).astype(jnp.int32), t.astype(jnp.int32)


def start_kernel(img_hbm, txt_hbm, partner_hbm, keep_ref, send_ref, img, txt, partner, sems):
    copies = [
        pltpu.make_async_copy(src, dst, sems.at[i])
        for i, (src, dst) in enumerate(((img_hbm, img), (txt_hbm, txt), (partner_hbm, partner)))
    ]
    for c in copies:
        c.start()
    for c in copies:
        c.wait()
    image_core = lax.axis_index("c") == 0
    half, size = img.shape
    a, b = img[...].astype(f32), txt[...].astype(f32)
    keep_ref[:half] = jnp.where(image_core, a, b).astype(bf16)
    send_ref[:half] = jnp.where(image_core, b, a).astype(bf16)
    p = jnp.concatenate([partner[...]] * (128 // half), axis=1)
    hi = p // 128
    tile = rows_tile([hi.astype(f32), (p - hi * 128).astype(f32)])
    for dst in (keep_ref, send_ref):
        dst[half:] = jnp.zeros((EXTRA, size), bf16)
        dst[half:, :128] = tile


def prep_kernel(images, first, second, out):
    half = first.shape[0] - EXTRA
    unit = [normalize(src[:half, :])[0] for src in (first, second)]
    unit = jnp.concatenate(unit, axis=0).astype(bf16)
    size = unit.size // 128
    tile = jnp.zeros((EXTRA, 128), bf16)
    if images:
        lane = lax.broadcasted_iota(jnp.int32, (EXTRA, 128), 1)
        a, b = (src[half:, :128].astype(f32) for src in (first, second))
        tile = jnp.where(lane // half % 2 == 0, a, b).astype(bf16)
    for b in range(out.shape[0]):
        pack(out, b, unit)
        out[b, size:, :] = tile


def place(images, tiles, r, t, ny):
    per_half = tiles // 2
    half, tile = divmod(r * ny + t, per_half)
    if not images:
        half = 1 - half
    return half * (per_half // 2) + tile // 2, slice(tile % 2 * 128, tile % 2 * 128 + 128)


def scores_kernel(images, rows, x_ref, y_ref, e_ref, pay_ref, match_ref, *scratch):
    packed = x_ref.shape[1]
    width = (packed - EXTRA) // rows * 128
    per, half = 128 // rows, rows // 2
    texts = x_ref.shape[0] // 2
    nx, ny = x_ref.shape[0] // per, y_ref.shape[0] // per
    if images:
        ny = texts // per
    else:
        nx = texts // per
    lane = lax.broadcasted_iota(jnp.int32, (1, 128), 1)
    chip = lax.axis_index("y") * lax.axis_size("x") + lax.axis_index("x")
    tail = (x_ref if images else y_ref)[:, packed - EXTRA :, :].astype(f32)
    partner = tail[:, 0, :] * 128.0 + tail[:, 1, :]

    def partners(t):
        p = partner[per * t : per * t + 1]
        for q in range(1, per):
            p = jnp.where(lane >= q * rows, partner[per * t + q : per * t + q + 1], p)
        return p

    def ids(t):
        i = (lane % rows) // half * (texts * half) + (per * t + lane // rows) * half
        return (chip * (texts * rows) + i + lane % half).astype(f32)

    xs, ys = (partners, ids) if images else (ids, partners)
    xs_ref, ys_ref, *s_refs = scratch
    for r in range(nx):
        xs_ref[r : r + 1] = xs(r)
    for t in range(ny):
        ys_ref[t : t + 1] = ys(t)
    part = nx // 2

    def product(h):
        x = unpack(x_ref, h * part * per, part * per, rows, width)
        y = unpack(y_ref, 0, ny * per, rows, width)
        s = lax.dot_general(x, y, NT, preferred_element_type=f32)
        for r in range(part):
            for t in range(ny):
                s_refs[h][r * ny + t] = s[r * 128 : (r + 1) * 128, t * 128 : (t + 1) * 128]

    def weigh(h):
        for r in range(h * part, (h + 1) * part):
            own = jnp.broadcast_to(xs_ref[r : r + 1], (128, 128)).T
            lanes = jnp.zeros((128, 128), f32)
            found = jnp.zeros((128, 128), f32)
            for t in range(ny):
                e = jnp.exp2(s_refs[h][(r - h * part) * ny + t] * f32(sharpness * math.log2(math.e)))
                matched = jnp.where(own == ys_ref[t : t + 1], e, f32(0.0))
                lanes += e
                found += matched
                block, at = place(images, nx * ny, r, t, ny)
                e_ref[block, at] = (e - f32(2.0) * matched).astype(bf16)
            pay_ref[0, r : r + 1] = jnp.sum(lanes.T, axis=0, keepdims=True)
            match_ref[r : r + 1] = jnp.sum(found.T, axis=0, keepdims=True)

    once = jnp.minimum(lax.axis_index("c") + 1, 1)
    product(0)

    def first(i, carry):
        product(1)
        weigh(0)
        return carry

    def second(i, carry):
        weigh(1)
        return carry

    lax.fori_loop(0, once, first, 0)
    lax.fori_loop(0, once, second, 0)
    if not images:
        m = match_ref[:nx]
        logs = jnp.where(m > 0.0, jnp.log(jnp.where(m > 0.0, m, f32(1.0))), f32(0.0))
        logs = jnp.sum(jnp.sum(logs, axis=0, keepdims=True), axis=1, keepdims=True)
        pay_ref[0, nx:] = jnp.broadcast_to(logs, (8 - nx, 128))
        match_ref[nx:] = jnp.zeros((8 - nx, 128), f32)
    for b in range(1, pay_ref.shape[0]):
        pay_ref[b] = pay_ref[0]


def grads_kernel(images, rows, y_ref, e_ref, match_ref, mine_ref, other_ref, out_ref):
    blocks, packed, _ = out_ref.shape
    width = (packed - EXTRA) // rows * 128
    per = 128 // rows
    nx = blocks // per
    ny = e_ref.shape[0] * 2 // nx
    col_total = other_ref[:ny]
    col_inv = f32(1.0) / col_total
    share = jnp.sum(jnp.log(col_total), axis=0, keepdims=True)
    share = jnp.broadcast_to(jnp.sum(share, axis=1, keepdims=True), (1, 128))
    if images:
        share -= 2.0 * other_ref[ny : ny + 1]
    whole = jnp.floor(share + f32(0.5))
    share = [whole.astype(jnp.int32), ((share - whole) * f32(32768.0)).astype(jnp.int32)]
    rest = [jnp.zeros((EXTRA - 2 - width // 128, 128), jnp.int32)]
    row_inv = f32(1.0) / mine_ref[:nx]
    y = unpack(y_ref, 0, ny * per, rows, width)
    gs = []
    ds = []
    for r in range(nx):
        ri = jnp.broadcast_to(row_inv[r : r + 1], (128, 128)).T
        matched = jnp.broadcast_to(match_ref[r : r + 1], (128, 128)).T
        d = []
        for t in range(ny):
            block, at = place(images, nx * ny, r, t, ny)
            e = e_ref[block, at].astype(f32)
            weight = ri + col_inv[t : t + 1]
            v = jnp.where(e < 0.0, matched * weight - f32(2.0), e * weight)
            d.append(v.astype(bf16))
        ds.append(jnp.concatenate(d, axis=1))
        if (r + 1) % (nx // 2) == 0:
            gs.append(jnp.dot(jnp.concatenate(ds, axis=0), y, preferred_element_type=f32))
            ds = []
    for b in range(blocks):
        steps = []
        for k in range(width // 128):
            q, t = encode(
                gs[b * 2 // blocks][
                    b % (blocks // 2) * rows : (b % (blocks // 2) + 1) * rows,
                    k * 128 : (k + 1) * 128,
                ]
            )
            out_ref[b, k * rows : (k + 1) * rows, :] = q.astype(jnp.int16)
            steps.append(t)
        tile = jnp.concatenate(steps + share + rest, axis=0)
        out_ref[b, packed - EXTRA :, :] = tile.astype(jnp.int16)


def finish_kernel(scale, keep_first, first, second, parts, keep_ref, send_ref, share_ref):
    half, size = keep_ref.shape
    rows = 2 * half
    body = rows * (size // 128)
    chunks = size // 128
    tail = parts[:, body:, :].astype(jnp.int32).astype(f32)
    step = jnp.exp2(tail[:, :chunks] * f32(0.125)) * f32(scale / LEVELS)
    total = []
    for k in range(chunks):
        piece = None
        for b in range(parts.shape[0]):
            q = parts[b, k * rows : (k + 1) * rows, :].astype(jnp.int32).astype(f32)
            q = q * step[b, k : k + 1]
            piece = q if piece is None else piece + q
        total.append(piece)
    total = jnp.concatenate(total, axis=1)
    grads = []
    for i, src in enumerate((first, second)):
        unit, factor = normalize(src[:half, :])
        g = total[i * half : (i + 1) * half]
        grads.append(factor * (g - unit * jnp.sum(unit * g, axis=1, keepdims=True)))
    keep, send = grads if keep_first else grads[::-1]
    keep_ref[...] = keep
    send_ref[:half] = send
    share = jnp.sum(tail[:, chunks : chunks + 1], axis=0)
    share += jnp.sum(tail[:, chunks + 1 : chunks + 2], axis=0) * f32(1.0 / 32768.0)
    share_ref[...] = jnp.broadcast_to(share, share_ref.shape)
    send_ref[half:] = jnp.broadcast_to(share[:, :1], (send_ref.shape[0] - half, size))


def output_kernel(batch, keep_ref, share_ref, recv_ref, img_ref, txt_ref, loss_ref):
    image_core = lax.axis_index("c") == 0
    half = keep_ref.shape[0]
    keep, recv = keep_ref[...], recv_ref[:half]
    img_ref[...] = jnp.where(image_core, keep, recv)
    txt_ref[...] = jnp.where(image_core, recv, keep)
    loss_ref[...] = (share_ref[:1, :1] + recv_ref[half : half + 1, :1]) / (2.0 * batch)


def call(kernel, outs, **kw):
    return pl.pallas_call(
        kernel,
        out_shape=[jax.ShapeDtypeStruct(*o) for o in outs],
        compiler_params=pltpu.CompilerParams(vmem_limit_bytes=48 * 1024 * 1024),
        **kw,
    )


def exchange(x, axes):
    return lax.all_to_all(x, axes, 0, 0)


def swap(x):
    return lax.ppermute(x, "c", [(0, 1), (1, 0)])


def local(image_embed, text_embed, partner):
    half, size = image_embed.shape
    rows = 2 * half
    n_plane = lax.axis_size("y") * lax.axis_size("x")
    n_line = lax.axis_size("z")
    batch = rows * n_plane * n_line
    image_core = lax.axis_index("c") == 0
    packed = rows * (size // 128) + EXTRA
    tiles = n_plane * n_line * rows * rows // (128 * 128)

    args = [
        pltpu.with_memory_space_constraint(a, pltpu.HBM)
        for a in (image_embed, text_embed, partner.reshape(1, half))
    ]
    own, send = call(
        start_kernel,
        [((half + EXTRA, size), bf16)] * 2,
        in_specs=[pl.BlockSpec(memory_space=pl.ANY)] * 3,
        scratch_shapes=[
            pltpu.VMEM((half, size), bf16),
            pltpu.VMEM((half, size), bf16),
            pltpu.VMEM((1, half), jnp.int32),
            pltpu.SemaphoreType.DMA((3,)),
        ],
    )(*args)
    off = swap(send)

    def gather_images():
        kernel = functools.partial(prep_kernel, True)
        return exchange(call(kernel, [((n_plane, packed, 128), bf16)])(own, off)[0], PLANE)

    def gather_texts():
        kernel = functools.partial(prep_kernel, False)
        every = exchange(call(kernel, [((n_line, packed, 128), bf16)])(off, own)[0], LINE)
        return jnp.pad(every, ((0, n_plane - n_line), (0, 0), (0, 0)))

    x = lax.cond(image_core, gather_images, gather_texts)
    y = swap(x)

    def sums(images, count, axes):
        e, pay, match = call(
            functools.partial(scores_kernel, images, rows),
            [((n_plane, packed, 128), bf16), ((count, 8, 128), f32), ((8, 128), f32)],
            input_output_aliases={0: 0},
            scratch_shapes=[pltpu.VMEM((8, 128), f32)] * 2
            + [pltpu.VMEM((tiles // 2, 128, 128), f32)] * 2,
        )(x, y)
        return e, match, jnp.sum(exchange(pay, axes), axis=0)

    e, match, mine = lax.cond(
        image_core,
        functools.partial(sums, True, n_plane, PLANE),
        functools.partial(sums, False, n_line, LINE),
    )
    other = swap(mine)

    def grads(images, count, axes):
        pay = call(
            functools.partial(grads_kernel, images, rows),
            [((count, packed, 128), jnp.int16)],
        )(y, e, match, mine, other)[0]
        return call(
            functools.partial(finish_kernel, sharpness / (2.0 * batch), images),
            [((half, size), f32), ((half + 8, size), f32), ((8, 128), f32)],
        )(*((own, off) if images else (off, own)), exchange(pay, axes))

    keep, send, share = lax.cond(
        image_core,
        functools.partial(grads, True, n_plane, PLANE),
        functools.partial(grads, False, n_line, LINE),
    )
    image_grad, text_grad, loss = call(
        functools.partial(output_kernel, batch),
        [((half, size), f32), ((half, size), f32), ((1, 1), f32)],
    )(keep, share, swap(send))
    return loss.reshape(()), image_grad, text_grad


def solution(mesh):
    shape = (mesh.shape["row"], 4, mesh.shape["col"] // 8, 2)
    fine = Mesh(mesh.devices.reshape(shape), ("z", "y", "x", "c"))
    by_image, by_text = P(("z", "y", "x", "c")), P(("y", "x", "c", "z"))
    return jax.shard_map(
        local,
        mesh=fine,
        in_specs=(by_image, by_text, by_image),
        out_specs=(P(), by_image, by_text),
        check_vma=False,
    )
```

```python
import functools
import math

import jax
import jax.numpy as jnp
from jax import lax
from jax.experimental import pallas as pl
from jax.experimental.pallas import tpu as pltpu
from jax.sharding import Mesh, PartitionSpec as P

sharpness = 1.0 / 0.07
f32 = jnp.float32
bf16 = jnp.bfloat16
NT = (((1,), (1,)), ((), ()))
PLANE, LINE = ("y", "x"), "z"
EXTRA = 16


def normalize(embed):
    flat = embed.astype(f32)
    factor = lax.rsqrt(jnp.sum(flat * flat, axis=1, keepdims=True) + 1e-06)
    return flat * factor, factor


def pack(dst, b, value):
    rows = value.shape[0]
    for k in range(value.shape[1] // 128):
        dst[b, k * rows : (k + 1) * rows, :] = value[:, k * 128 : (k + 1) * 128]


def unpack(ref, first, count, rows, width):
    return jnp.concatenate(
        [
            ref[first : first + count, k * rows : (k + 1) * rows, :].reshape(count * rows, 128)
            for k in range(width // 128)
        ],
        axis=1,
    )


def rows_tile(values):
    row = lax.broadcasted_iota(jnp.int32, (EXTRA, 128), 0)
    tile = jnp.zeros((EXTRA, 128), f32)
    for i, v in enumerate(values):
        tile = jnp.where(row == i, v, tile)
    return tile.astype(bf16)


LEVELS = 32760.0


def encode(value):
    most = jnp.max(jnp.abs(value), axis=0, keepdims=True)
    t = jnp.ceil(f32(8.0) * jnp.log2(jnp.maximum(most, f32(1e-30))) + f32(0.01))
    scaled = value * (f32(LEVELS) * jnp.exp2(t * f32(-0.125)))
    return jnp.round(scaled).astype(jnp.int32), t.astype(jnp.int32)


def start_kernel(img_hbm, txt_hbm, partner_hbm, keep_ref, send_ref, img, txt, partner, sems):
    copies = [
        pltpu.make_async_copy(src, dst, sems.at[i])
        for i, (src, dst) in enumerate(((img_hbm, img), (txt_hbm, txt), (partner_hbm, partner)))
    ]
    for c in copies:
        c.start()
    for c in copies:
        c.wait()
    image_core = lax.axis_index("c") == 0
    half, size = img.shape
    a, b = img[...].astype(f32), txt[...].astype(f32)
    keep_ref[:half] = jnp.where(image_core, a, b).astype(bf16)
    send_ref[:half] = jnp.where(image_core, b, a).astype(bf16)
    p = jnp.concatenate([partner[...]] * (128 // half), axis=1)
    hi = p // 128
    tile = rows_tile([hi.astype(f32), (p - hi * 128).astype(f32)])
    for dst in (keep_ref, send_ref):
        dst[half:] = jnp.zeros((EXTRA, size), bf16)
        dst[half:, :128] = tile


def prep_kernel(images, first, second, out):
    half = first.shape[0] - EXTRA
    unit = [normalize(src[:half, :])[0] for src in (first, second)]
    unit = jnp.concatenate(unit, axis=0).astype(bf16)
    size = unit.size // 128
    tile = jnp.zeros((EXTRA, 128), bf16)
    if images:
        lane = lax.broadcasted_iota(jnp.int32, (EXTRA, 128), 1)
        a, b = (src[half:, :128].astype(f32) for src in (first, second))
        tile = jnp.where(lane // half % 2 == 0, a, b).astype(bf16)
    for b in range(out.shape[0]):
        pack(out, b, unit)
        out[b, size:, :] = tile


def place(images, tiles, r, t, ny):
    per_half = tiles // 2
    half, tile = divmod(r * ny + t, per_half)
    if not images:
        half = 1 - half
    return half * (per_half // 2) + tile // 2, slice(tile % 2 * 128, tile % 2 * 128 + 128)


def scores_kernel(images, rows, x_ref, y_ref, e_ref, pay_ref, match_ref, *scratch):
    packed = x_ref.shape[1]
    width = (packed - EXTRA) // rows * 128
    per, half = 128 // rows, rows // 2
    texts = x_ref.shape[0] // 2
    nx, ny = x_ref.shape[0] // per, y_ref.shape[0] // per
    if images:
        ny = texts // per
    else:
        nx = texts // per
    lane = lax.broadcasted_iota(jnp.int32, (1, 128), 1)
    chip = lax.axis_index("y") * lax.axis_size("x") + lax.axis_index("x")
    tail = (x_ref if images else y_ref)[:, packed - EXTRA :, :].astype(f32)
    partner = tail[:, 0, :] * 128.0 + tail[:, 1, :]

    def partners(t):
        p = partner[per * t : per * t + 1]
        for q in range(1, per):
            p = jnp.where(lane >= q * rows, partner[per * t + q : per * t + q + 1], p)
        return p

    def ids(t):
        i = (lane % rows) // half * (texts * half) + (per * t + lane // rows) * half
        return (chip * (texts * rows) + i + lane % half).astype(f32)

    xs, ys = (partners, ids) if images else (ids, partners)
    xs_ref, ys_ref, *s_refs = scratch
    for r in range(nx):
        xs_ref[r : r + 1] = xs(r)
    for t in range(ny):
        ys_ref[t : t + 1] = ys(t)
    part = nx // 2

    def product(h):
        x = unpack(x_ref, h * part * per, part * per, rows, width)
        y = unpack(y_ref, 0, ny * per, rows, width)
        s = lax.dot_general(x, y, NT, preferred_element_type=f32)
        for r in range(part):
            for t in range(ny):
                s_refs[h][r * ny + t] = s[r * 128 : (r + 1) * 128, t * 128 : (t + 1) * 128]

    def weigh(h):
        for r in range(h * part, (h + 1) * part):
            own = jnp.broadcast_to(xs_ref[r : r + 1], (128, 128)).T
            lanes = jnp.zeros((128, 128), f32)
            found = jnp.zeros((128, 128), f32)
            for t in range(ny):
                e = jnp.exp2(s_refs[h][(r - h * part) * ny + t] * f32(sharpness * math.log2(math.e)))
                matched = jnp.where(own == ys_ref[t : t + 1], e, f32(0.0))
                lanes += e
                found += matched
                block, at = place(images, nx * ny, r, t, ny)
                e_ref[block, at] = (e - f32(2.0) * matched).astype(bf16)
            pay_ref[0, r : r + 1] = jnp.sum(lanes.T, axis=0, keepdims=True)
            match_ref[r : r + 1] = jnp.sum(found.T, axis=0, keepdims=True)

    once = jnp.minimum(lax.axis_index("c") + 1, 1)
    product(0)

    def first(i, carry):
        product(1)
        weigh(0)
        return carry

    def second(i, carry):
        weigh(1)
        return carry

    lax.fori_loop(0, once, first, 0)
    lax.fori_loop(0, once, second, 0)
    if not images:
        m = match_ref[:nx]
        logs = jnp.where(m > 0.0, jnp.log(jnp.where(m > 0.0, m, f32(1.0))), f32(0.0))
        logs = jnp.sum(jnp.sum(logs, axis=0, keepdims=True), axis=1, keepdims=True)
        pay_ref[0, nx:] = jnp.broadcast_to(logs, (8 - nx, 128))
        match_ref[nx:] = jnp.zeros((8 - nx, 128), f32)
    for b in range(1, pay_ref.shape[0]):
        pay_ref[b] = pay_ref[0]


def grads_kernel(images, rows, y_ref, e_ref, match_ref, mine_ref, other_ref, out_ref):
    blocks, packed, _ = out_ref.shape
    width = (packed - EXTRA) // rows * 128
    per = 128 // rows
    nx = blocks // per
    ny = e_ref.shape[0] * 2 // nx
    col_total = other_ref[:ny]
    col_inv = f32(1.0) / col_total
    share = jnp.sum(jnp.log(col_total), axis=0, keepdims=True)
    share = jnp.broadcast_to(jnp.sum(share, axis=1, keepdims=True), (1, 128))
    if images:
        share -= 2.0 * other_ref[ny : ny + 1]
    whole = jnp.floor(share + f32(0.5))
    share = [whole.astype(jnp.int32), ((share - whole) * f32(32768.0)).astype(jnp.int32)]
    rest = [jnp.zeros((EXTRA - 2 - width // 128, 128), jnp.int32)]
    row_inv = f32(1.0) / mine_ref[:nx]
    y = unpack(y_ref, 0, ny * per, rows, width)
    def store(b):
        steps = []
        for k in range(width // 128):
            q, t = encode(
                gs[b * 2 // blocks][
                    b % (blocks // 2) * rows : (b % (blocks // 2) + 1) * rows,
                    k * 128 : (k + 1) * 128,
                ]
            )
            out_ref[b, k * rows : (k + 1) * rows, :] = q.astype(jnp.int16)
            steps.append(t)
        tile = jnp.concatenate(steps + share + rest, axis=0)
        out_ref[b, packed - EXTRA :, :] = tile.astype(jnp.int16)

    gs = []
    ds = []
    for r in range(nx):
        ri = jnp.broadcast_to(row_inv[r : r + 1], (128, 128)).T
        matched = jnp.broadcast_to(match_ref[r : r + 1], (128, 128)).T
        d = []
        for t in range(ny):
            block, at = place(images, nx * ny, r, t, ny)
            e = e_ref[block, at].astype(f32)
            weight = ri + col_inv[t : t + 1]
            v = jnp.where(e < 0.0, matched * weight - f32(2.0), e * weight)
            d.append(v.astype(bf16))
        ds.append(jnp.concatenate(d, axis=1))
        if (r + 1) % (nx // 2) == 0:
            gs.append(jnp.dot(jnp.concatenate(ds, axis=0), y, preferred_element_type=f32))
            ds = []
            for b in range((len(gs) - 1) * blocks // 2, len(gs) * blocks // 2):
                store(b)


def finish_kernel(scale, keep_first, first, second, parts, keep_ref, send_ref, share_ref):
    half, size = keep_ref.shape
    rows = 2 * half
    body = rows * (size // 128)
    chunks = size // 128
    tail = parts[:, body:, :].astype(jnp.int32).astype(f32)
    step = jnp.exp2(tail[:, :chunks] * f32(0.125)) * f32(scale / LEVELS)
    total = []
    for k in range(chunks):
        piece = None
        for b in range(parts.shape[0]):
            q = parts[b, k * rows : (k + 1) * rows, :].astype(jnp.int32).astype(f32)
            q = q * step[b, k : k + 1]
            piece = q if piece is None else piece + q
        total.append(piece)
    total = jnp.concatenate(total, axis=1)
    grads = []
    for i, src in enumerate((first, second)):
        unit, factor = normalize(src[:half, :])
        g = total[i * half : (i + 1) * half]
        grads.append(factor * (g - unit * jnp.sum(unit * g, axis=1, keepdims=True)))
    keep, send = grads if keep_first else grads[::-1]
    keep_ref[...] = keep
    send_ref[:half] = send
    share = jnp.sum(tail[:, chunks : chunks + 1], axis=0)
    share += jnp.sum(tail[:, chunks + 1 : chunks + 2], axis=0) * f32(1.0 / 32768.0)
    share_ref[...] = jnp.broadcast_to(share, share_ref.shape)
    send_ref[half:] = jnp.broadcast_to(share[:, :1], (send_ref.shape[0] - half, size))


def output_kernel(batch, keep_ref, share_ref, recv_ref, img_ref, txt_ref, loss_ref):
    image_core = lax.axis_index("c") == 0
    half = keep_ref.shape[0]
    keep, recv = keep_ref[...], recv_ref[:half]
    img_ref[...] = jnp.where(image_core, keep, recv)
    txt_ref[...] = jnp.where(image_core, recv, keep)
    loss_ref[...] = (share_ref[:1, :1] + recv_ref[half : half + 1, :1]) / (2.0 * batch)


def call(kernel, outs, **kw):
    return pl.pallas_call(
        kernel,
        out_shape=[jax.ShapeDtypeStruct(*o) for o in outs],
        compiler_params=pltpu.CompilerParams(vmem_limit_bytes=48 * 1024 * 1024),
        **kw,
    )


def exchange(x, axes):
    return lax.all_to_all(x, axes, 0, 0)


def swap(x):
    return lax.ppermute(x, "c", [(0, 1), (1, 0)])


def local(image_embed, text_embed, partner):
    half, size = image_embed.shape
    rows = 2 * half
    n_plane = lax.axis_size("y") * lax.axis_size("x")
    n_line = lax.axis_size("z")
    batch = rows * n_plane * n_line
    image_core = lax.axis_index("c") == 0
    packed = rows * (size // 128) + EXTRA
    tiles = n_plane * n_line * rows * rows // (128 * 128)

    args = [
        pltpu.with_memory_space_constraint(a, pltpu.HBM)
        for a in (image_embed, text_embed, partner.reshape(1, half))
    ]
    own, send = call(
        start_kernel,
        [((half + EXTRA, size), bf16)] * 2,
        in_specs=[pl.BlockSpec(memory_space=pl.ANY)] * 3,
        scratch_shapes=[
            pltpu.VMEM((half, size), bf16),
            pltpu.VMEM((half, size), bf16),
            pltpu.VMEM((1, half), jnp.int32),
            pltpu.SemaphoreType.DMA((3,)),
        ],
    )(*args)
    off = swap(send)

    def gather_images():
        kernel = functools.partial(prep_kernel, True)
        return exchange(call(kernel, [((n_plane, packed, 128), bf16)])(own, off)[0], PLANE)

    def gather_texts():
        kernel = functools.partial(prep_kernel, False)
        every = exchange(call(kernel, [((n_line, packed, 128), bf16)])(off, own)[0], LINE)
        return jnp.pad(every, ((0, n_plane - n_line), (0, 0), (0, 0)))

    x = lax.cond(image_core, gather_images, gather_texts)
    y = swap(x)

    def sums(images, count, axes):
        e, pay, match = call(
            functools.partial(scores_kernel, images, rows),
            [((n_plane, packed, 128), bf16), ((count, 8, 128), f32), ((8, 128), f32)],
            input_output_aliases={0: 0},
            scratch_shapes=[pltpu.VMEM((8, 128), f32)] * 2
            + [pltpu.VMEM((tiles // 2, 128, 128), f32)] * 2,
        )(x, y)
        return e, match, jnp.sum(exchange(pay, axes), axis=0)

    e, match, mine = lax.cond(
        image_core,
        functools.partial(sums, True, n_plane, PLANE),
        functools.partial(sums, False, n_line, LINE),
    )
    other = swap(mine)

    def grads(images, count, axes):
        pay = call(
            functools.partial(grads_kernel, images, rows),
            [((count, packed, 128), jnp.int16)],
        )(y, e, match, mine, other)[0]
        return call(
            functools.partial(finish_kernel, sharpness / (2.0 * batch), images),
            [((half, size), f32), ((half + 8, size), f32), ((8, 128), f32)],
        )(*((own, off) if images else (off, own)), exchange(pay, axes))

    keep, send, share = lax.cond(
        image_core,
        functools.partial(grads, True, n_plane, PLANE),
        functools.partial(grads, False, n_line, LINE),
    )
    image_grad, text_grad, loss = call(
        functools.partial(output_kernel, batch),
        [((half, size), f32), ((half, size), f32), ((1, 1), f32)],
    )(keep, share, swap(send))
    return loss.reshape(()), image_grad, text_grad


def solution(mesh):
    shape = (mesh.shape["row"], 4, mesh.shape["col"] // 8, 2)
    fine = Mesh(mesh.devices.reshape(shape), ("z", "y", "x", "c"))
    by_image, by_text = P(("z", "y", "x", "c")), P(("y", "x", "c", "z"))
    return jax.shard_map(
        local,
        mesh=fine,
        in_specs=(by_image, by_text, by_image),
        out_specs=(P(), by_image, by_text),
        check_vma=False,
    )
```
